256 devices in a mesh: ep: 64 (over z, x, core), grp: 4 (over y).
Axes of the slice: x: 4, y: 4, z: 8, core: 2. Of those that a mesh axis runs over, the one named last changes fastest.
Arguments:
- hidden: bfloat16 [4096, 3584], P(('ep', 'grp')), may hold values from -6 to 6
- expert_ids: int32 [4096, 8], P(('ep', 'grp')), may hold values from 0 to 63, all different within a row; in each aligned block of 16 rows (0 to 15, 16 to 31, ...) at most 4 rows name the same one
- gate_weights: float32 [4096, 8], P(('ep', 'grp')), may hold values from 0.05 to 0.5
- w_up: bfloat16 [64, 3584, 1024], P('ep', None, 'grp'), may hold values from -0.09375 to 0.09375
- w_down: bfloat16 [64, 3584, 1024], P('ep', None, 'grp'), may hold values from -0.1875 to 0.1875
- query_first: bfloat16 [4096, 64, 576], P(('ep', 'grp')), may hold values from -17 to 17
- kv_first: bfloat16 [4096, 576], P(('ep', 'grp')), may hold values from -6 to 6
- query_second: bfloat16 [4096, 64, 576], P(('ep', 'grp')), may hold values from -17 to 17
- kv_second: bfloat16 [4096, 576], P(('ep', 'grp')), may hold values from -6 to 6
- cache_pool: bfloat16 [8192, 64, 576], P(('ep', 'grp')), may hold values from -6 to 6
- cache_len: int32 [256, 16], P(('ep', 'grp')), may hold values from 1 to 512, 1024 in all within a row
- page_perm: int32 [256, 32], P(('ep', 'grp')), may hold values from 0 to 31, each once within a row
- mig_slot: int32 [64, 4], P('ep', 'grp'), may hold values from 0 to 15
- mig_dest: int32 [64, 4], P('ep', 'grp'), may hold values from 0 to 3, each once within a row
Outputs:
- attn_first: bfloat16 [4096, 64, 512], P(('ep', 'grp'))
- attn_second: bfloat16 [4096, 64, 512], P(('ep', 'grp'))
- moe_out: bfloat16 [4096, 3584], P(('ep', 'grp'))
The draws below stay inside these ranges and needn't reach their ends.
Inputs may be any that keep to these rules, and one draw needn't show every extreme that they name: `expert_ids`: the entries of the rows of one device name each expert at most 4 times. `cache_len`: each row's lengths sum to 1024. `page_perm`: each row is a permutation of the 32 page numbers. `mig_dest`: each row is a permutation of the 4 grp indices.
All inputs are finite; a program needn't handle non-finite values.
Results may differ from the reference program's by a relative error of at most 0.0058.
Values may be sent and summed in bfloat16 or wider, within the bound.
No kernel may reach another device: no remote copies, remote signals or barrier semaphores. Data moves between devices by JAX's collectives and lax.ppermute only.
A program may use at most 128 MiB of HBM per device.

```python
import math
import jax
import jax.numpy as jnp
import numpy as np
from jax import lax

D = 3584
FFE = 1024
HEADS = 64
LAT = 512
KW = 576
PAGE = 64
MAXP = 8
TOPK = 8
SAMPLES = 16
EXPERTS = 64
CAP = 4
POOL = 32
TOKENS = 4096
N_EP = 64
N_GRP = 4


def draw_cache_pool(key, part):
    key = jax.random.fold_in(key, 3)
    base_draw = jnp.clip(jax.random.normal(key, (N_EP * N_GRP * POOL, PAGE, KW), jnp.float32), -6.0, 6.0)
    return base_draw.astype(jnp.bfloat16)


def draw_kv_first(key, part):
    key = jax.random.fold_in(key, 5)
    base_draw = jnp.clip(jax.random.normal(key, (TOKENS, KW), jnp.float32), -6.0, 6.0)
    return base_draw.astype(jnp.bfloat16)


def draw_kv_second(key, part):
    key = jax.random.fold_in(key, 7)
    base_draw = jnp.clip(jax.random.normal(key, (TOKENS, KW), jnp.float32), -6.0, 6.0)
    return base_draw.astype(jnp.bfloat16)


def draw_query_first(key, part):
    key = jax.random.fold_in(key, 11)
    key_noise = jax.random.fold_in(key, 0)
    base_draw = jnp.clip(jax.random.normal(key_noise, (TOKENS, HEADS, KW), jnp.float32), -6.0, 6.0)
    return base_draw.astype(jnp.bfloat16)


def draw_query_second(key, part):
    key = jax.random.fold_in(key, 13)
    key_noise = jax.random.fold_in(key, 0)
    base_draw = jnp.clip(jax.random.normal(key_noise, (TOKENS, HEADS, KW), jnp.float32), -6.0, 6.0)
    return base_draw.astype(jnp.bfloat16)


def touch_ends(result, stream_key, low, largest):
    longest = result.shape.index(max(result.shape))
    spots = []
    for shift in (0, 1):
        where = [jax.random.randint(jax.random.fold_in(stream_key, axis), (), 0, length) for axis, length in enumerate(result.shape)]
        where[longest] = (where[longest] + shift) % result.shape[longest]
        spots.append(tuple(where))
    return result.at[spots[0]].set(low).at[spots[1]].set(largest)


def levels(rng, shape, shards, smallest, high):
    factor_of = 1.0
    for axis_at, blocks in shards:
        draws = jax.random.uniform(jax.random.fold_in(jax.random.fold_in(rng, 6), axis_at), (blocks,), jnp.float32, smallest / len(shards), high / len(shards))
        factor_of = factor_of * jnp.repeat(jnp.exp(draws), shape[axis_at] // blocks).reshape((-1,) + (1,) * (len(shape) - 1 - axis_at))
    return factor_of


def split_up(amount, total, bound, lean):
    weights = [(1 << 20) // math.isqrt(standing ** lean) + 1 for standing in range(2, amount + 1)]
    rest, holding = total - bound - (amount - 1), [1] * (amount - 1)
    while rest > 0:
        free = [i for i in range(amount - 1) if holding[i] < bound]
        whole, budget = sum([weights[i] for i in free]), rest
        for i in free:
            extra = min(bound - holding[i], max(1, budget * weights[i] // whole), rest)
            holding[i] = holding[i] + extra
            rest = rest - extra
    return np.array([bound] + holding)


def ragged(rng, count, total, most, skew):
    if count == 2:
        one = jax.random.randint(rng, (), max(1, total - most), min(most, total - 1) + 1)
        return jnp.stack([one, total - one])
    lengths = jnp.asarray(split_up(count, total, most, skew), jnp.int32)
    pairs = (count - 1) // 2
    donor, sink = lengths[1:1 + 2 * pairs:2], lengths[2:2 + 2 * pairs:2]
    slack = jnp.minimum(donor - 1, most - sink)
    shifted = jax.random.randint(jax.random.fold_in(rng, 1), (pairs,), 0, 1 << 20) % (slack + 1)
    lengths = lengths.at[1:1 + 2 * pairs:2].set(donor - shifted).at[2:2 + 2 * pairs:2].set(sink + shifted)
    return lengths[jax.random.permutation(jax.random.fold_in(rng, 2), count)]


def shared_out(rng, own, number, rows, count, top, bound, slope):
    sequence = jax.random.permutation(rng, count)
    heavy_load, common = portions_of(count, rows * top, bound, slope, True), portions_of(count, rows * top, bound, slope, False)
    places = jnp.arange(count)

    def named(sizes, turn):
        used = int((sizes > 0).sum())
        fixed = max(1, used // 4)
        moved = fixed + (places - fixed + turn * (used - fixed)) % max(1, count - fixed)
        return jnp.zeros((count,), jnp.int32).at[sequence[jnp.where(places < fixed, places, moved)]].set(jnp.asarray(sizes, jnp.int32))

    sizes = jnp.where(number % 4 == 0, named(heavy_load, number // 4), named(common, number - number // 4 - 1))
    mixed = jax.random.permutation(jax.random.fold_in(own, 3), count)
    donor, receiver = mixed[0:count // 2 * 2:2], mixed[1:count // 2 * 2:2]
    room = jnp.minimum(sizes[donor] - 1, bound - sizes[receiver]) // 2
    room = jnp.where((donor == sequence[0]) | (receiver == sequence[0]) | (sizes[receiver] == 0), 0, jnp.maximum(room, 0))
    moved = jax.random.randint(jax.random.fold_in(own, 4), (count // 2,), 0, 1 << 20) % (room + 1)
    sizes = sizes.at[donor].add(-moved).at[receiver].add(moved)
    items = jnp.searchsorted(jnp.cumsum(sizes), jnp.arange(rows * top), side="right").astype(jnp.int32)
    table = items.reshape(top, rows).T
    table = table[jax.random.permutation(jax.random.fold_in(own, 1), rows)]
    turn = jax.random.randint(jax.random.fold_in(own, 2), (rows, 1), 0, top)
    return jnp.take_along_axis(table, (jnp.arange(top)[None, :] + turn) % top, axis=1)


def portions_of(count, total, most, skew, full):
    loads = [(1 << 20) // math.isqrt(standing ** skew) + 1 for standing in range(1, count + 1)]
    largest = most if full else min(most, max(-(-total // count), total * loads[0] // sum(loads)))
    least = 1 if total - largest >= count - 1 else 0
    counts, surplus = [largest] + [least] * (count - 1), total - largest - least * (count - 1)
    while surplus > 0:
        movable = [i for i in range(1, count) if counts[i] < largest] or [i for i in range(1, count) if counts[i] < most]
        whole, left = sum([loads[i] for i in movable]), surplus
        for i in movable:
            more = min(most - counts[i], max(1, left * loads[i] // whole), surplus)
            counts[i] = counts[i] + more
            surplus = surplus - more
    return np.array(counts)


def bell_draw(stream_key, shape, spread, bound, pieces=(), held_as=jnp.bfloat16):
    factor_of = levels(stream_key, shape, pieces, -0.22, 0.18) if pieces else 1.0
    values = jax.random.normal(stream_key, shape, jnp.float32) * spread * factor_of
    return jnp.minimum(jnp.maximum(values, -bound), bound).astype(held_as)


def setup_inputs(seed: int = 0) -> dict:
    key_list = jax.random.split(jax.random.key(seed), 15)
    hidden = bell_draw(key_list[0], (TOKENS, D), 1.0, 6.0, ((0, 256),))
    expert_ids_keys = jax.random.split(jax.random.fold_in(key_list[1], 1), TOKENS // SAMPLES)
    expert_ids_turns = jax.random.permutation(jax.random.fold_in(key_list[1], 3), TOKENS // SAMPLES)
    expert_ids = jax.vmap(lambda own, number: shared_out(jax.random.fold_in(key_list[1], 2), own, number, SAMPLES, EXPERTS, TOPK, CAP, 2))(expert_ids_keys, expert_ids_turns).reshape((TOKENS, TOPK))
    gate_weights = jnp.clip(jnp.exp(math.log(0.5) - 2.3025851 * jax.random.uniform(key_list[2], (TOKENS, TOPK), jnp.float32) ** levels(key_list[2], (TOKENS, TOPK), ((0, 256),), -0.2, 0.2)), 0.05, 0.5)
    w_up = bell_draw(key_list[3], (EXPERTS, D, FFE), D ** -0.5, 0.09375, ((0, 64), (2, 4)))
    w_down = bell_draw(key_list[4], (EXPERTS, D, FFE), FFE ** -0.5, 0.1875, ((0, 64), (2, 4)))
    query_first = draw_query_first(jax.random.fold_in(key_list[14], 71), 0)
    kv_first = draw_kv_first(jax.random.fold_in(key_list[14], 71), 0)
    query_second = draw_query_second(jax.random.fold_in(key_list[14], 71), 0)
    kv_second = draw_kv_second(jax.random.fold_in(key_list[14], 71), 0)
    cache_pool = draw_cache_pool(jax.random.fold_in(key_list[14], 71), 0)
    cache_len = jax.vmap(lambda own: ragged(own, SAMPLES, (POOL - SAMPLES) * PAGE, MAXP * PAGE, 2))(jax.random.split(key_list[10], (N_EP * N_GRP))).reshape((N_EP * N_GRP, SAMPLES)).astype(jnp.int32)
    page_perm = jax.vmap(lambda own: jax.random.permutation(own, POOL))(jax.random.split(key_list[11], (N_EP * N_GRP))).reshape((N_EP * N_GRP, POOL)).astype(jnp.int32)
    mig_slot = touch_ends(jax.random.randint(key_list[12], (N_EP, N_GRP), 0, SAMPLES), jax.random.fold_in(key_list[12], 1), 0, SAMPLES - 1).astype(jnp.int32)
    mig_dest = jax.vmap(lambda own: jax.random.permutation(own, N_GRP))(jax.random.split(key_list[13], N_EP)).reshape((N_EP, N_GRP)).astype(jnp.int32)
    return {"hidden": hidden, "expert_ids": expert_ids, "gate_weights": gate_weights, "w_up": w_up, "w_down": w_down, "query_first": query_first, "kv_first": kv_first, "query_second": query_second, "kv_second": kv_second, "cache_pool": cache_pool, "cache_len": cache_len, "page_perm": page_perm, "mig_slot": mig_slot, "mig_dest": mig_dest}


def build_table(cache_len, page_perm):
    pages_used = (cache_len + PAGE - 1) // PAGE
    page_offset = jnp.cumsum(pages_used, axis=1) - pages_used
    page_slots = page_offset[:, :, None] + jnp.arange(MAXP, dtype=jnp.int32)[None, None, :]
    page_slots = jnp.minimum(page_slots, POOL - 1).astype(jnp.int32)
    row_count = page_slots.shape[0]
    chosen = jnp.take_along_axis(page_perm, page_slots.reshape(row_count, SAMPLES * MAXP), axis=1)
    chosen = chosen.reshape(row_count, SAMPLES, MAXP)
    return chosen + (jnp.arange(row_count, dtype=jnp.int32) * POOL)[:, None, None]

def attend(query_rows, key_rows, key_valid):
    score_scale = 1.0 / math.sqrt(KW / 3.0)
    scores = jnp.einsum('bhk,blk->bhl', query_rows.astype(jnp.float32), key_rows.astype(jnp.float32)) * score_scale
    scores = jnp.where(key_valid[:, None, :], scores, -jnp.inf)
    row_max = lax.optimization_barrier(jnp.max(scores, axis=2, keepdims=True))
    weights = jnp.exp(scores - row_max)
    probability = (weights / lax.optimization_barrier(jnp.sum(weights, axis=2, keepdims=True))).astype(jnp.bfloat16)
    value_rows = key_rows[:, :, :LAT]
    return jnp.einsum('bhl,blk->bhk', probability.astype(jnp.float32), value_rows.astype(jnp.float32)).astype(jnp.bfloat16)

def reference(hidden, expert_ids, gate_weights, w_up, w_down, query_first, kv_first, query_second, kv_second, cache_pool, cache_len, page_perm, mig_slot, mig_dest):
    devices = N_EP * N_GRP
    page_table = build_table(cache_len, page_perm)
    positions = jnp.arange(MAXP * PAGE, dtype=jnp.int32)

    def first_step(device):
        page_index = page_table[device].reshape(-1)
        key_rows = cache_pool[page_index].reshape(SAMPLES, MAXP * PAGE, KW)
        key_valid = positions[None, :] < cache_len[device][:, None]
        start_row = (device * SAMPLES).astype(jnp.int32)
        fresh_key = lax.dynamic_slice_in_dim(kv_first, start_row, SAMPLES, 0)
        query_rows = lax.dynamic_slice_in_dim(query_first, start_row, SAMPLES, 0)
        key_rows = jnp.concatenate([key_rows, fresh_key[:, None, :]], axis=1)
        key_valid = jnp.concatenate([key_valid, jnp.ones((SAMPLES, 1), dtype=bool)], axis=1)
        return attend(query_rows, key_rows, key_valid)

    def second_step(device):
        group_index = device // N_GRP
        member_index = device % N_GRP
        dest_row = mig_dest[group_index]
        source_index = jnp.sum(jnp.where(dest_row == member_index, jnp.arange(N_GRP, dtype=jnp.int32), 0)).astype(jnp.int32)
        source_device = (group_index * N_GRP + source_index).astype(jnp.int32)
        here_slot = mig_slot[group_index, member_index]
        source_slot = mig_slot[group_index, source_index]
        slot_range = jnp.arange(SAMPLES, dtype=jnp.int32)
        moved_mask = slot_range == here_slot
        old_device = jnp.where(moved_mask, source_device, device).astype(jnp.int32)
        old_slot = jnp.where(moved_mask, source_slot, slot_range).astype(jnp.int32)
        page_index = page_table[old_device, old_slot].reshape(-1)
        key_rows = cache_pool[page_index].reshape(SAMPLES, MAXP * PAGE, KW)
        key_valid = positions[None, :] < cache_len[old_device, old_slot][:, None]
        first_key = kv_first[old_device * SAMPLES + old_slot]
        start_row = (device * SAMPLES).astype(jnp.int32)
        second_key = lax.dynamic_slice_in_dim(kv_second, start_row, SAMPLES, 0)
        query_rows = lax.dynamic_slice_in_dim(query_second, start_row, SAMPLES, 0)
        key_rows = jnp.concatenate([key_rows, first_key[:, None, :], second_key[:, None, :]], axis=1)
        key_valid = jnp.concatenate([key_valid, jnp.ones((SAMPLES, 2), dtype=bool)], axis=1)
        return attend(query_rows, key_rows, key_valid)
    device_range = jnp.arange(devices, dtype=jnp.int32)
    attn_first = lax.map(first_step, device_range).reshape(TOKENS, HEADS, LAT)
    attn_second = lax.map(second_step, device_range).reshape(TOKENS, HEADS, LAT)
    flat_ids = expert_ids.reshape(-1)
    entry_gate = gate_weights.reshape(-1)
    rows_max = CAP * devices

    def one_expert(expert_num, running):
        expert_hit = flat_ids == expert_num
        picks = jnp.nonzero(expert_hit, size=rows_max, fill_value=0)[0].astype(jnp.int32)
        live_rows = jnp.arange(rows_max, dtype=jnp.int32) < jnp.sum(expert_hit.astype(jnp.int32))
        token_index = (picks // TOPK).astype(jnp.int32)
        routed_rows = hidden[token_index]
        hidden_units = jax.nn.silu(jnp.dot(routed_rows, w_up[expert_num], preferred_element_type=jnp.float32)).astype(jnp.bfloat16)
        expert_out = jnp.dot(hidden_units, w_down[expert_num].T, preferred_element_type=jnp.float32).astype(jnp.bfloat16)
        row_gate = jnp.where(live_rows, entry_gate[picks], jnp.zeros((), entry_gate.dtype))
        return running.at[token_index].add(row_gate[:, None] * expert_out.astype(jnp.float32))
    running = lax.fori_loop(0, EXPERTS, one_expert, jnp.zeros((TOKENS, D), jnp.float32))
    return (attn_first, attn_second, running.astype(jnp.bfloat16))
```

```python
import functools
import math

import jax
import jax.numpy as jnp
from jax import lax
from jax.experimental import pallas as pl
from jax.experimental.pallas import tpu as pltpu
from jax.sharding import PartitionSpec as P

LAT = 512
MAXP = 8
CHUNKS = 4
NEG = -1e30


def hop(value, axis, step):
    size = lax.axis_size(axis)
    return lax.ppermute(value, axis, [(i, (i + step) % size) for i in range(size)])


def attention_kernel(
    lens, pages, moved, q_one, q_two, q_in, kv_one, kv_two, kv_in, pool, out_one, out_two, out_moved, acc
):
    slot = pl.program_id(0)
    heads = q_one.shape[1]
    rows = 2 * heads
    key_width = q_one.shape[2]
    page_rows = pool.shape[1]
    block = 2 * page_rows
    scale = 1.0 / math.sqrt(key_width / 3.0)
    is_moved = slot == moved[0]
    second = jnp.where(is_moved, q_in[...], q_two[0])
    queries = jnp.concatenate([q_one[0], second], axis=0)
    fresh_one = kv_one[0]
    fresh_two = jnp.where(is_moved, kv_in[...], kv_two[0])
    fresh = jnp.concatenate(
        [fresh_one, fresh_two, jnp.zeros((14, key_width), jnp.bfloat16)], axis=0
    )
    contract = (((1,), (1,)), ((), ()))
    scores = lax.dot_general(queries, fresh, contract, preferred_element_type=jnp.float32) * scale
    row = lax.broadcasted_iota(jnp.int32, scores.shape, 0)
    col = lax.broadcasted_iota(jnp.int32, scores.shape, 1)
    scores = jnp.where((col == 0) | ((col == 1) & (row >= heads)), scores, NEG)
    top = jnp.max(scores, axis=1, keepdims=True)
    weights = jnp.exp(scores - top)
    total = jnp.sum(weights, axis=1, keepdims=True)
    acc[...] = jnp.dot(
        weights.astype(jnp.bfloat16), fresh[:, :LAT], preferred_element_type=jnp.float32
    )
    live = lens[slot]

    def step(b, carry):
        top, total = carry
        keys = jnp.concatenate(
            [pool[pages[slot * MAXP + 2 * b]], pool[pages[slot * MAXP + 2 * b + 1]]], axis=0
        )
        scores = (
            lax.dot_general(queries, keys, contract, preferred_element_type=jnp.float32) * scale
        )
        col = lax.broadcasted_iota(jnp.int32, scores.shape, 1) + b * block
        scores = jnp.where(col < live, scores, NEG)
        new_top = jnp.maximum(top, jnp.max(scores, axis=1, keepdims=True))
        shrink = jnp.exp(top - new_top)
        weights = jnp.exp(scores - new_top)
        total = total * shrink + jnp.sum(weights, axis=1, keepdims=True)
        acc[...] = acc[...] * shrink + jnp.dot(
            weights.astype(jnp.bfloat16), keys[:, :LAT], preferred_element_type=jnp.float32
        )
        return new_top, total

    top, total = lax.fori_loop(0, (live + block - 1) // block, step, (top, total))
    result = (acc[...] / total).astype(jnp.bfloat16)
    out_one[0] = result[:heads]
    out_two[0] = result[heads:]

    @pl.when(is_moved)
    def _():
        out_moved[...] = result[heads:]


def attention(lens, pages, moved, q_one, q_two, q_in, kv_one, kv_two, kv_in, pool):
    samples, heads, key_width = q_one.shape
    one = lambda *shape: pl.BlockSpec((1,) + shape, lambda i, *_: (i,) + (0,) * len(shape))
    whole = lambda *shape: pl.BlockSpec(shape, lambda i, *_: (0,) * len(shape))
    return pl.pallas_call(
        attention_kernel,
        grid_spec=pltpu.PrefetchScalarGridSpec(
            num_scalar_prefetch=3,
            grid=(samples,),
            in_specs=[
                one(heads, key_width),
                one(heads, key_width),
                whole(heads, key_width),
                one(1, key_width),
                one(1, key_width),
                whole(1, key_width),
                whole(*pool.shape),
            ],
            out_specs=[one(heads, LAT), one(heads, LAT), whole(heads, LAT)],
            scratch_shapes=[pltpu.VMEM((2 * heads, LAT), jnp.float32)],
        ),
        out_shape=[
            jax.ShapeDtypeStruct((samples, heads, LAT), jnp.bfloat16),
            jax.ShapeDtypeStruct((samples, heads, LAT), jnp.bfloat16),
            jax.ShapeDtypeStruct((heads, LAT), jnp.bfloat16),
        ],
        compiler_params=pltpu.CompilerParams(vmem_limit_bytes=24 * 1024 * 1024),
        cost_estimate=pl.CostEstimate(
            flops=12_000_000_000, bytes_accessed=8_000_000, transcendentals=1_000_000
        ),
        name="attention",
    )(lens, pages, moved, q_one, q_two, q_in, kv_one, kv_two, kv_in, pool)


def page_table(cache_len, page_perm, page_rows, pool_pages):
    used = (cache_len + page_rows - 1) // page_rows
    slots = used.shape[0]
    before = jnp.arange(slots)[None, :] < jnp.arange(slots)[:, None]
    offset = jnp.sum(jnp.where(before, used[None, :], 0), axis=1)
    place = jnp.minimum(
        offset[:, None] + jnp.arange(MAXP, dtype=jnp.int32)[None, :], pool_pages - 1
    ).reshape(-1)
    hit = place[:, None] == jnp.arange(pool_pages, dtype=jnp.int32)[None, :]
    return jnp.sum(jnp.where(hit, page_perm[None, :], 0), axis=1)


def shards(
    hidden,
    expert_ids,
    gate_weights,
    w_up,
    w_down,
    query_first,
    kv_first,
    query_second,
    kv_second,
    cache_pool,
    cache_len,
    page_perm,
    mig_slot,
    mig_dest,
):
    samples, picks = expert_ids.shape
    width = hidden.shape[1]
    ep_size = lax.axis_size("ep")
    grp_size = lax.axis_size("grp")
    capacity = min(samples, max(2, 2 * samples * picks // ep_size))
    slots_all = ep_size * capacity
    me = lax.axis_index("grp")

    up, down = w_up[0], w_down[0]
    half = width // 2
    piece = width // CHUNKS
    up_parts = [up[:half], up[half:]]
    up_prev = [hop(p, "grp", 1) for p in up_parts]
    up_next = [hop(p, "grp", -1) for p in reversed(up_parts)][::-1]
    up_far = [hop(up_prev[0], "grp", 1), hop(up_next[1], "grp", -1)]
    down_all = []
    for c in range(CHUNKS):
        mid = piece // 2
        own = down[c * piece : (c + 1) * piece]
        parts = [own[:mid], own[mid:]]
        prev = [hop(p, "grp", 1) for p in parts]
        nxt = [hop(p, "grp", -1) for p in reversed(parts)][::-1]
        far = [hop(prev[0], "grp", 1), hop(nxt[1], "grp", -1)]
        down_all.append((parts, prev, nxt, far))

    moved_slot = mig_slot[0, 0]
    moved_target = mig_dest[0, 0]
    q_here = lax.dynamic_index_in_dim(query_second, moved_slot, 0, keepdims=False)
    kv_here = lax.dynamic_index_in_dim(kv_second, moved_slot, 0, keepdims=True)
    packet = jnp.concatenate(
        [q_here, kv_here, jnp.zeros((15, q_here.shape[1]), jnp.bfloat16)], axis=0
    )
    offset = (moved_target - me) % grp_size
    got = packet
    for step in range(1, grp_size):
        got = jnp.where(offset == step, hop(packet, "grp", -step), got)
    heads = q_here.shape[0]
    q_in, kv_in = got[:heads], got[heads : heads + 1]

    lens = cache_len[0]
    pages = page_table(lens, page_perm[0], cache_pool.shape[1], cache_pool.shape[0])
    attn_first, attn_second, out_moved = attention(
        lens,
        pages,
        moved_slot[None],
        query_first,
        query_second,
        q_in,
        kv_first[:, None, :],
        kv_second[:, None, :],
        kv_in,
        cache_pool,
    )
    zero = jnp.zeros((), jnp.bfloat16)
    arrived_out = jnp.where(offset == 0, out_moved, zero)
    for step in range(1, grp_size):
        arrived_out = arrived_out + hop(jnp.where(offset == step, out_moved, zero), "grp", step)
    attn_second = lax.dynamic_update_index_in_dim(attn_second, arrived_out, moved_slot, 0)

    flat_ids = expert_ids.reshape(-1)
    entries = flat_ids.shape[0]
    hits = flat_ids[:, None] == jnp.arange(ep_size, dtype=jnp.int32)[None, :]
    order = jnp.arange(entries, dtype=jnp.int32)
    lower = (order[None, :] < order[:, None]).astype(jnp.bfloat16)
    ahead = jnp.dot(lower, hits.astype(jnp.bfloat16), preferred_element_type=jnp.float32)
    earlier = jnp.sum(jnp.where(hits, ahead, 0.0), axis=1).astype(jnp.int32)
    slot_index = (flat_ids * capacity + earlier).reshape(samples, picks)
    slot_range = jnp.arange(slots_all, dtype=jnp.int32)
    match = slot_index[:, :, None] == slot_range[None, None, :]
    placing = jnp.sum(match.astype(jnp.float32), axis=1).astype(jnp.bfloat16)
    mixing = jnp.sum(jnp.where(match, gate_weights[:, :, None], 0.0), axis=1)
    outgoing = lax.dot_general(
        placing, hidden, (((0,), (0,)), ((), ())), preferred_element_type=jnp.float32
    ).astype(jnp.bfloat16)
    arrived = lax.all_to_all(
        outgoing.reshape(ep_size, capacity, width), "ep", split_axis=0, concat_axis=0, tiled=True
    ).reshape(slots_all, width)

    f32dot = functools.partial(jnp.dot, preferred_element_type=jnp.float32)

    def act(v):
        return jax.nn.silu(v).astype(jnp.bfloat16)

    def up_of(parts):
        return act(f32dot(arrived[:, :half], parts[0]) + f32dot(arrived[:, half:], parts[1]))

    h_all = [up_of(p) for p in (up_parts, up_prev, up_next, up_far)]
    contract = (((1,), (1,)), ((), ()))
    results = []
    for c in range(CHUNKS):
        cols = []
        for s in range(2):
            total = 0.0
            for h, parts in zip(h_all, down_all[c]):
                total = total + lax.dot_general(
                    h, parts[s], contract, preferred_element_type=jnp.float32
                )
            cols.append(total.astype(jnp.bfloat16))
        produced = jnp.concatenate(cols, axis=1)
        returned = lax.all_to_all(
            produced.reshape(ep_size, capacity, piece), "ep", split_axis=0, concat_axis=0, tiled=True
        ).reshape(slots_all, piece)
        results.append(
            jnp.dot(
                mixing,
                returned.astype(jnp.float32),
                preferred_element_type=jnp.float32,
                precision=lax.Precision.HIGHEST,
            ).astype(jnp.bfloat16)
        )
    moe_out = jnp.concatenate(results, axis=1)
    return (attn_first, attn_second, moe_out)


def solution(mesh):
    return jax.shard_map(
        shards,
        mesh=mesh,
        in_specs=(
            P(("ep", "grp"), None),
            P(("ep", "grp"), None),
            P(("ep", "grp"), None),
            P("ep", None, "grp"),
            P("ep", None, "grp"),
            P(("ep", "grp"), None, None),
            P(("ep", "grp"), None),
            P(("ep", "grp"), None, None),
            P(("ep", "grp"), None),
            P(("ep", "grp"), None, None),
            P(("ep", "grp"), None),
            P(("ep", "grp"), None),
            P("ep", "grp"),
            P("ep", "grp"),
        ),
        out_specs=(
            P(("ep", "grp"), None, None),
            P(("ep", "grp"), None, None),
            P(("ep", "grp"), None),
        ),
        check_vma=False,
    )
```

```python
import functools
import math

import jax
import jax.numpy as jnp
from jax import lax
from jax.experimental import pallas as pl
from jax.experimental.pallas import tpu as pltpu
from jax.sharding import PartitionSpec as P

LAT = 512
MAXP = 8
CHUNKS = 2
NEG = -1e30


def hop(value, axis, step):
    size = lax.axis_size(axis)
    return lax.ppermute(value, axis, [(i, (i + step) % size) for i in range(size)])


def after(first, *values):
    return lax.optimization_barrier((first,) + values)[1:]


def attention_kernel(
    lens, pages, moved, q_one, q_two, q_in, kv_one, kv_two, kv_in, pool, out_one, out_two, out_moved, acc
):
    slot = pl.program_id(0)
    heads = q_one.shape[1]
    rows = 2 * heads
    key_width = q_one.shape[2]
    page_rows = pool.shape[1]
    block = 2 * page_rows
    scale = 1.0 / math.sqrt(key_width / 3.0)
    is_moved = slot == moved[0]
    second = jnp.where(is_moved, q_in[...], q_two[0])
    queries = jnp.concatenate([q_one[0], second], axis=0)
    fresh_one = kv_one[0]
    fresh_two = jnp.where(is_moved, kv_in[...], kv_two[0])
    fresh = jnp.concatenate(
        [fresh_one, fresh_two, jnp.zeros((14, key_width), jnp.bfloat16)], axis=0
    )
    contract = (((1,), (1,)), ((), ()))
    scores = lax.dot_general(queries, fresh, contract, preferred_element_type=jnp.float32) * scale
    row = lax.broadcasted_iota(jnp.int32, scores.shape, 0)
    col = lax.broadcasted_iota(jnp.int32, scores.shape, 1)
    scores = jnp.where((col == 0) | ((col == 1) & (row >= heads)), scores, NEG)
    top = jnp.max(scores, axis=1, keepdims=True)
    weights = jnp.exp(scores - top)
    total = jnp.sum(weights, axis=1, keepdims=True)
    acc[...] = jnp.dot(
        weights.astype(jnp.bfloat16), fresh[:, :LAT], preferred_element_type=jnp.float32
    )
    live = lens[slot]

    def step(b, carry):
        top, total = carry
        keys = jnp.concatenate(
            [pool[pages[slot * MAXP + 2 * b]], pool[pages[slot * MAXP + 2 * b + 1]]], axis=0
        )
        scores = (
            lax.dot_general(queries, keys, contract, preferred_element_type=jnp.float32) * scale
        )
        col = lax.broadcasted_iota(jnp.int32, scores.shape, 1) + b * block
        scores = jnp.where(col < live, scores, NEG)
        new_top = jnp.maximum(top, jnp.max(scores, axis=1, keepdims=True))
        shrink = jnp.exp(top - new_top)
        weights = jnp.exp(scores - new_top)
        total = total * shrink + jnp.sum(weights, axis=1, keepdims=True)
        acc[...] = acc[...] * shrink + jnp.dot(
            weights.astype(jnp.bfloat16), keys[:, :LAT], preferred_element_type=jnp.float32
        )
        return new_top, total

    top, total = lax.fori_loop(0, (live + block - 1) // block, step, (top, total))
    result = (acc[...] / total).astype(jnp.bfloat16)
    out_one[0] = result[:heads]
    out_two[0] = result[heads:]

    @pl.when(is_moved)
    def _():
        out_moved[...] = result[heads:]


def attention(lens, pages, moved, q_one, q_two, q_in, kv_one, kv_two, kv_in, pool):
    samples, heads, key_width = q_one.shape
    one = lambda *shape: pl.BlockSpec((1,) + shape, lambda i, *_: (i,) + (0,) * len(shape))
    whole = lambda *shape: pl.BlockSpec(shape, lambda i, *_: (0,) * len(shape))
    return pl.pallas_call(
        attention_kernel,
        grid_spec=pltpu.PrefetchScalarGridSpec(
            num_scalar_prefetch=3,
            grid=(samples,),
            in_specs=[
                one(heads, key_width),
                one(heads, key_width),
                whole(heads, key_width),
                one(1, key_width),
                one(1, key_width),
                whole(1, key_width),
                whole(*pool.shape),
            ],
            out_specs=[one(heads, LAT), one(heads, LAT), whole(heads, LAT)],
            scratch_shapes=[pltpu.VMEM((2 * heads, LAT), jnp.float32)],
        ),
        out_shape=[
            jax.ShapeDtypeStruct((samples, heads, LAT), jnp.bfloat16),
            jax.ShapeDtypeStruct((samples, heads, LAT), jnp.bfloat16),
            jax.ShapeDtypeStruct((heads, LAT), jnp.bfloat16),
        ],
        compiler_params=pltpu.CompilerParams(vmem_limit_bytes=24 * 1024 * 1024),
        cost_estimate=pl.CostEstimate(
            flops=12_000_000_000, bytes_accessed=8_000_000, transcendentals=1_000_000
        ),
        name="attention",
    )(lens, pages, moved, q_one, q_two, q_in, kv_one, kv_two, kv_in, pool)


def page_table(cache_len, page_perm, page_rows, pool_pages):
    used = (cache_len + page_rows - 1) // page_rows
    slots = used.shape[0]
    before = jnp.arange(slots)[None, :] < jnp.arange(slots)[:, None]
    offset = jnp.sum(jnp.where(before, used[None, :], 0), axis=1)
    place = jnp.minimum(
        offset[:, None] + jnp.arange(MAXP, dtype=jnp.int32)[None, :], pool_pages - 1
    ).reshape(-1)
    hit = place[:, None] == jnp.arange(pool_pages, dtype=jnp.int32)[None, :]
    return jnp.sum(jnp.where(hit, page_perm[None, :], 0), axis=1)


def shards(
    hidden,
    expert_ids,
    gate_weights,
    w_up,
    w_down,
    query_first,
    kv_first,
    query_second,
    kv_second,
    cache_pool,
    cache_len,
    page_perm,
    mig_slot,
    mig_dest,
):
    samples, picks = expert_ids.shape
    width = hidden.shape[1]
    ep_size = lax.axis_size("ep")
    grp_size = lax.axis_size("grp")
    capacity = min(samples, max(2, 2 * samples * picks // ep_size))
    slots_all = ep_size * capacity

    up, down = w_up[0], w_down[0]
    half = width // 2
    piece = width // CHUNKS
    mid = piece // 2
    own = [down[c * piece : (c + 1) * piece] for c in range(CHUNKS)]
    up_prev, up_next = hop(up, "grp", 1), hop(up, "grp", -1)
    prev, nxt, far = [], [], []
    ahead_of = (up_prev, up_next)
    far_from = (up_prev[:half], up_next[half:])
    far_all = []
    for c in range(CHUNKS):
        out, top, low = after(ahead_of, own[c], far_from[0], far_from[1])
        far_all.append((hop(top, "grp", 1), hop(low, "grp", -1)))
        prev.append(hop(out, "grp", 1))
        nxt.append(hop(out, "grp", -1))
        ahead_of = (prev[c], nxt[c])
        far_from = (prev[c][:mid], nxt[c][mid:])
    far_all.append((hop(far_from[0], "grp", 1), hop(far_from[1], "grp", -1)))
    up_far, down_far = far_all[0], far_all[1:]

    moved_slot = mig_slot[0, 0]
    moved_target = mig_dest[0, 0]
    q_here = lax.dynamic_index_in_dim(query_second, moved_slot, 0, keepdims=False)
    kv_here = lax.dynamic_index_in_dim(kv_second, moved_slot, 0, keepdims=True)
    packet = jnp.concatenate(
        [q_here, kv_here, jnp.zeros((15, q_here.shape[1]), jnp.bfloat16)], axis=0
    )
    offered = lax.all_to_all(
        jnp.broadcast_to(packet[None], (grp_size,) + packet.shape),
        "grp",
        split_axis=0,
        concat_axis=0,
        tiled=True,
    )
    got = lax.dynamic_index_in_dim(offered, moved_target, 0, keepdims=False)
    heads = q_here.shape[0]
    q_in, kv_in = got[:heads], got[heads : heads + 1]

    lens = cache_len[0]
    pages = page_table(lens, page_perm[0], cache_pool.shape[1], cache_pool.shape[0])
    attn_first, attn_second, out_moved = attention(
        lens,
        pages,
        moved_slot[None],
        query_first,
        query_second,
        q_in,
        kv_first[:, None, :],
        kv_second[:, None, :],
        kv_in,
        cache_pool,
    )
    to_target = jnp.arange(grp_size, dtype=jnp.int32) == moved_target
    sent_out = jnp.where(to_target[:, None, None], out_moved[None], jnp.zeros((), jnp.bfloat16))
    got_out = lax.all_to_all(sent_out, "grp", split_axis=0, concat_axis=0, tiled=True)
    arrived_out = got_out[0] + got_out[1] + got_out[2] + got_out[3]
    attn_second = lax.dynamic_update_index_in_dim(attn_second, arrived_out, moved_slot, 0)

    flat_ids = expert_ids.reshape(-1)
    entries = flat_ids.shape[0]
    hits = flat_ids[:, None] == jnp.arange(ep_size, dtype=jnp.int32)[None, :]
    order = jnp.arange(entries, dtype=jnp.int32)
    lower = (order[None, :] < order[:, None]).astype(jnp.bfloat16)
    ahead = jnp.dot(lower, hits.astype(jnp.bfloat16), preferred_element_type=jnp.float32)
    earlier = jnp.sum(jnp.where(hits, ahead, 0.0), axis=1).astype(jnp.int32)
    slot_index = (flat_ids * capacity + earlier).reshape(samples, picks)
    slot_range = jnp.arange(slots_all, dtype=jnp.int32)
    match = slot_index[:, :, None] == slot_range[None, None, :]
    placing = jnp.sum(match.astype(jnp.float32), axis=1).astype(jnp.bfloat16)
    mixing = jnp.sum(jnp.where(match, gate_weights[:, :, None], 0.0), axis=1)
    outgoing = lax.dot_general(
        placing, hidden, (((0,), (0,)), ((), ())), preferred_element_type=jnp.float32
    ).astype(jnp.bfloat16)
    arrived = lax.all_to_all(
        outgoing.reshape(ep_size, capacity, width), "ep", split_axis=0, concat_axis=0, tiled=True
    ).reshape(slots_all, width)

    f32dot = functools.partial(jnp.dot, preferred_element_type=jnp.float32)

    def act(v):
        return jax.nn.silu(v).astype(jnp.bfloat16)

    def up_of(weight):
        return act(f32dot(arrived, weight))

    far_up = act(f32dot(arrived[:, :half], up_far[0]) + f32dot(arrived[:, half:], up_far[1]))
    h_own, h_prev, h_next = up_of(up), up_of(up_prev), up_of(up_next)
    contract = (((1,), (1,)), ((), ()))

    def down_of(h, weight):
        return lax.dot_general(h, weight, contract, preferred_element_type=jnp.float32)

    results = []
    for c in range(CHUNKS):
        near = down_of(h_own, own[c]) + down_of(h_prev, prev[c]) + down_of(h_next, nxt[c])
        top, low = down_of(far_up, down_far[c][0]), down_of(far_up, down_far[c][1])
        cols = [
            (near[:, :mid] + top).astype(jnp.bfloat16),
            (near[:, mid:] + low).astype(jnp.bfloat16),
        ]
        produced = jnp.concatenate(cols, axis=1)
        returned = lax.all_to_all(
            produced.reshape(ep_size, capacity, piece), "ep", split_axis=0, concat_axis=0, tiled=True
        ).reshape(slots_all, piece)
        results.append(
            jnp.dot(
                mixing,
                returned.astype(jnp.float32),
                preferred_element_type=jnp.float32,
                precision=lax.Precision.HIGHEST,
            ).astype(jnp.bfloat16)
        )
    moe_out = jnp.concatenate(results, axis=1)
    return (attn_first, attn_second, moe_out)


def solution(mesh):
    return jax.shard_map(
        shards,
        mesh=mesh,
        in_specs=(
            P(("ep", "grp"), None),
            P(("ep", "grp"), None),
            P(("ep", "grp"), None),
            P("ep", None, "grp"),
            P("ep", None, "grp"),
            P(("ep", "grp"), None, None),
            P(("ep", "grp"), None),
            P(("ep", "grp"), None, None),
            P(("ep", "grp"), None),
            P(("ep", "grp"), None, None),
            P(("ep", "grp"), None),
            P(("ep", "grp"), None),
            P("ep", "grp"),
            P("ep", "grp"),
        ),
        out_specs=(
            P(("ep", "grp"), None, None),
            P(("ep", "grp"), None, None),
            P(("ep", "grp"), None),
        ),
        check_vma=False,
    )
```

```python
import functools
import math

import jax
import jax.numpy as jnp
from jax import lax
from jax.experimental import pallas as pl
from jax.experimental.pallas import tpu as pltpu
from jax.sharding import PartitionSpec as P

LAT = 512
MAXP = 8
NEG = -1e30


def hop(value, axis, step):
    size = lax.axis_size(axis)
    return lax.ppermute(value, axis, [(i, (i + step) % size) for i in range(size)])


def after(first, *values):
    return lax.optimization_barrier((first,) + values)[1:]


def attention_kernel(
    lens, pages, moved, q_one, q_two, q_in, kv_one, kv_two, kv_in, pool, out_one, out_two, out_moved, acc
):
    slot = pl.program_id(0)
    heads = q_one.shape[1]
    rows = 2 * heads
    key_width = q_one.shape[2]
    page_rows = pool.shape[1]
    block = 2 * page_rows
    scale = 1.0 / math.sqrt(key_width / 3.0)
    is_moved = slot == moved[0]
    second = jnp.where(is_moved, q_in[...], q_two[0])
    queries = jnp.concatenate([q_one[0], second], axis=0)
    fresh_one = kv_one[0]
    fresh_two = jnp.where(is_moved, kv_in[...], kv_two[0])
    fresh = jnp.concatenate(
        [fresh_one, fresh_two, jnp.zeros((14, key_width), jnp.bfloat16)], axis=0
    )
    contract = (((1,), (1,)), ((), ()))
    scores = lax.dot_general(queries, fresh, contract, preferred_element_type=jnp.float32) * scale
    row = lax.broadcasted_iota(jnp.int32, scores.shape, 0)
    col = lax.broadcasted_iota(jnp.int32, scores.shape, 1)
    scores = jnp.where((col == 0) | ((col == 1) & (row >= heads)), scores, NEG)
    top = jnp.max(scores, axis=1, keepdims=True)
    weights = jnp.exp(scores - top)
    total = jnp.sum(weights, axis=1, keepdims=True)
    acc[...] = jnp.dot(
        weights.astype(jnp.bfloat16), fresh[:, :LAT], preferred_element_type=jnp.float32
    )
    live = lens[slot]

    def step(b, carry):
        top, total = carry
        keys = jnp.concatenate(
            [pool[pages[slot * MAXP + 2 * b]], pool[pages[slot * MAXP + 2 * b + 1]]], axis=0
        )
        scores = (
            lax.dot_general(queries, keys, contract, preferred_element_type=jnp.float32) * scale
        )
        col = lax.broadcasted_iota(jnp.int32, scores.shape, 1) + b * block
        scores = jnp.where(col < live, scores, NEG)
        new_top = jnp.maximum(top, jnp.max(scores, axis=1, keepdims=True))
        shrink = jnp.exp(top - new_top)
        weights = jnp.exp(scores - new_top)
        total = total * shrink + jnp.sum(weights, axis=1, keepdims=True)
        acc[...] = acc[...] * shrink + jnp.dot(
            weights.astype(jnp.bfloat16), keys[:, :LAT], preferred_element_type=jnp.float32
        )
        return new_top, total

    top, total = lax.fori_loop(0, (live + block - 1) // block, step, (top, total))
    result = (acc[...] / total).astype(jnp.bfloat16)
    out_one[0] = result[:heads]
    out_two[0] = result[heads:]

    @pl.when(is_moved)
    def _():
        out_moved[...] = result[heads:]


def attention(lens, pages, moved, q_one, q_two, q_in, kv_one, kv_two, kv_in, pool):
    samples, heads, key_width = q_one.shape
    one = lambda *shape: pl.BlockSpec((1,) + shape, lambda i, *_: (i,) + (0,) * len(shape))
    whole = lambda *shape: pl.BlockSpec(shape, lambda i, *_: (0,) * len(shape))
    return pl.pallas_call(
        attention_kernel,
        grid_spec=pltpu.PrefetchScalarGridSpec(
            num_scalar_prefetch=3,
            grid=(samples,),
            in_specs=[
                one(heads, key_width),
                one(heads, key_width),
                whole(heads, key_width),
                one(1, key_width),
                one(1, key_width),
                whole(1, key_width),
                whole(*pool.shape),
            ],
            out_specs=[one(heads, LAT), one(heads, LAT), whole(heads, LAT)],
            scratch_shapes=[pltpu.VMEM((2 * heads, LAT), jnp.float32)],
        ),
        out_shape=[
            jax.ShapeDtypeStruct((samples, heads, LAT), jnp.bfloat16),
            jax.ShapeDtypeStruct((samples, heads, LAT), jnp.bfloat16),
            jax.ShapeDtypeStruct((heads, LAT), jnp.bfloat16),
        ],
        compiler_params=pltpu.CompilerParams(vmem_limit_bytes=24 * 1024 * 1024),
        cost_estimate=pl.CostEstimate(
            flops=12_000_000_000, bytes_accessed=8_000_000, transcendentals=1_000_000
        ),
        name="attention",
    )(lens, pages, moved, q_one, q_two, q_in, kv_one, kv_two, kv_in, pool)


def page_table(cache_len, page_perm, page_rows, pool_pages):
    used = (cache_len + page_rows - 1) // page_rows
    slots = used.shape[0]
    before = jnp.arange(slots)[None, :] < jnp.arange(slots)[:, None]
    offset = jnp.sum(jnp.where(before, used[None, :], 0), axis=1)
    place = jnp.minimum(
        offset[:, None] + jnp.arange(MAXP, dtype=jnp.int32)[None, :], pool_pages - 1
    ).reshape(-1)
    hit = place[:, None] == jnp.arange(pool_pages, dtype=jnp.int32)[None, :]
    return jnp.sum(jnp.where(hit, page_perm[None, :], 0), axis=1)


def shards(
    hidden,
    expert_ids,
    gate_weights,
    w_up,
    w_down,
    query_first,
    kv_first,
    query_second,
    kv_second,
    cache_pool,
    cache_len,
    page_perm,
    mig_slot,
    mig_dest,
):
    samples, picks = expert_ids.shape
    width = hidden.shape[1]
    ep_size = lax.axis_size("ep")
    grp_size = lax.axis_size("grp")
    capacity = min(samples, max(2, 2 * samples * picks // ep_size))
    slots_all = ep_size * capacity
    me = lax.axis_index("grp")
    steps = range(grp_size)

    flat_ids = expert_ids.reshape(-1)
    entries = flat_ids.shape[0]
    hits = flat_ids[:, None] == jnp.arange(ep_size, dtype=jnp.int32)[None, :]
    order = jnp.arange(entries, dtype=jnp.int32)
    lower = (order[None, :] < order[:, None]).astype(jnp.bfloat16)
    ahead = jnp.dot(lower, hits.astype(jnp.bfloat16), preferred_element_type=jnp.float32)
    earlier = jnp.sum(jnp.where(hits, ahead, 0.0), axis=1).astype(jnp.int32)
    slot_index = (flat_ids * capacity + earlier).reshape(samples, picks)
    match = slot_index[:, :, None] == jnp.arange(slots_all, dtype=jnp.int32)[None, None, :]
    placing = jnp.sum(match.astype(jnp.float32), axis=1).astype(jnp.bfloat16)
    outgoing = lax.dot_general(
        placing, hidden, (((0,), (0,)), ((), ())), preferred_element_type=jnp.float32
    ).astype(jnp.bfloat16)
    arrived = lax.all_to_all(
        outgoing.reshape(ep_size, capacity, width), "ep", split_axis=0, concat_axis=0, tiled=True
    ).reshape(slots_all, width)

    up_all = lax.all_gather(w_up[0], "grp", axis=0, tiled=False)
    quarter = width // grp_size
    blocks = w_down[0].reshape(grp_size, quarter, w_down.shape[2])
    down_own = lax.dynamic_index_in_dim(blocks, me, 0, keepdims=False)
    down_all = [down_own] + [
        hop(lax.dynamic_index_in_dim(blocks, (me + r) % grp_size, 0, keepdims=False), "grp", r)
        for r in steps[1:]
    ]

    note = jnp.concatenate([slot_index.astype(jnp.float32), gate_weights], axis=1)
    notes = jnp.concatenate([note] + [hop(note, "grp", r) for r in steps[1:]], axis=0)
    went = notes[:, :picks].astype(jnp.int32)
    plane = (me - jnp.arange(grp_size * samples, dtype=jnp.int32) // samples) % grp_size
    place = (went // capacity) * grp_size + plane[:, None]
    place = place * capacity + went % capacity
    lanes = jnp.arange(grp_size * slots_all, dtype=jnp.int32)
    mixing = jnp.sum(
        jnp.where(place[:, :, None] == lanes[None, None, :], notes[:, picks:][:, :, None], 0.0),
        axis=1,
    )
    high = lax.reduce_precision(mixing, 8, 7)
    mixing = jnp.concatenate([high, mixing - high], axis=0).astype(jnp.bfloat16)

    moved_slot = mig_slot[0, 0]
    moved_target = mig_dest[0, 0]
    query_second, kv_second = after(outgoing, query_second, kv_second)
    q_here = lax.dynamic_index_in_dim(query_second, moved_slot, 0, keepdims=False)
    kv_here = lax.dynamic_index_in_dim(kv_second, moved_slot, 0, keepdims=True)
    packet = jnp.concatenate(
        [q_here, kv_here, jnp.zeros((15, q_here.shape[1]), jnp.bfloat16)], axis=0
    )
    offset = (moved_target - me) % grp_size
    got = packet
    for r in steps[1:]:
        got = jnp.where(offset == r, hop(packet, "grp", -r), got)
    heads = q_here.shape[0]
    q_in, kv_in = got[:heads], got[heads : heads + 1]

    lens = cache_len[0]
    pages = page_table(lens, page_perm[0], cache_pool.shape[1], cache_pool.shape[0])
    attn_first, attn_second, out_moved = attention(
        lens,
        pages,
        moved_slot[None],
        query_first,
        query_second,
        q_in,
        kv_first[:, None, :],
        kv_second[:, None, :],
        kv_in,
        cache_pool,
    )
    zero = jnp.zeros((), jnp.bfloat16)
    arrived_out = jnp.where(offset == 0, out_moved, zero)
    for r in steps[1:]:
        arrived_out = arrived_out + hop(jnp.where(offset == r, out_moved, zero), "grp", r)
    attn_second = lax.dynamic_update_index_in_dim(attn_second, arrived_out, moved_slot, 0)

    f32dot = functools.partial(jnp.dot, preferred_element_type=jnp.float32)
    arrived, *down_all = lax.optimization_barrier((arrived, *down_all))
    held = jnp.concatenate(
        [jax.nn.silu(f32dot(arrived, up_all[q])).astype(jnp.bfloat16) for q in range(grp_size)],
        axis=1,
    )
    held_all = lax.all_gather(held, "grp", axis=0, tiled=False)
    units = w_down.shape[2]
    rows = (
        held_all.reshape(grp_size, ep_size, capacity, grp_size * units)
        .transpose(1, 0, 2, 3)
        .reshape(grp_size * slots_all, grp_size * units)
    )
    produced = 0.0
    for r in steps:
        source = (me - r) % grp_size
        part = lax.dynamic_slice_in_dim(rows, source * units, units, 1)
        produced = produced + lax.dot_general(
            part, down_all[r], (((1,), (1,)), ((), ())), preferred_element_type=jnp.float32
        )
    returned = lax.all_to_all(
        produced.astype(jnp.bfloat16).reshape(ep_size, grp_size * capacity, quarter),
        "ep",
        split_axis=0,
        concat_axis=0,
        tiled=True,
    ).reshape(grp_size * slots_all, quarter)
    mixed = f32dot(mixing, returned)
    tokens = grp_size * samples
    summed = (mixed[:tokens] + mixed[tokens:]).astype(jnp.bfloat16)
    summed = summed.reshape(grp_size, samples, quarter)
    own = jnp.stack([summed[0]] + [hop(summed[r], "grp", -r) for r in steps[1:]])
    moe_out = jnp.concatenate(
        [
            lax.dynamic_index_in_dim(own, (q - me) % grp_size, 0, keepdims=False)
            for q in steps
        ],
        axis=1,
    )
    return (attn_first, attn_second, moe_out)


def solution(mesh):
    return jax.shard_map(
        shards,
        mesh=mesh,
        in_specs=(
            P(("ep", "grp"), None),
            P(("ep", "grp"), None),
            P(("ep", "grp"), None),
            P("ep", None, "grp"),
            P("ep", None, "grp"),
            P(("ep", "grp"), None, None),
            P(("ep", "grp"), None),
            P(("ep", "grp"), None, None),
            P(("ep", "grp"), None),
            P(("ep", "grp"), None, None),
            P(("ep", "grp"), None),
            P(("ep", "grp"), None),
            P("ep", "grp"),
            P("ep", "grp"),
        ),
        out_specs=(
            P(("ep", "grp"), None, None),
            P(("ep", "grp"), None, None),
            P(("ep", "grp"), None),
        ),
        check_vma=False,
    )
```

```python
import functools
import math

import jax
import jax.numpy as jnp
from jax import lax
from jax.experimental import pallas as pl
from jax.experimental.pallas import tpu as pltpu
from jax.sharding import PartitionSpec as P

LAT = 512
MAXP = 8
NEG = -1e30


def hop(value, axis, step):
    size = lax.axis_size(axis)
    return lax.ppermute(value, axis, [(i, (i + step) % size) for i in range(size)])


def after(first, *values):
    return lax.optimization_barrier((first,) + values)[1:]


def attention_kernel(
    lens, pages, moved, q_one, q_two, q_in, kv_one, kv_two, kv_in, pool, out_one, out_two, out_moved, acc
):
    slot = pl.program_id(0)
    heads = q_one.shape[1]
    rows = 2 * heads
    key_width = q_one.shape[2]
    page_rows = pool.shape[1]
    block = 2 * page_rows
    scale = 1.0 / math.sqrt(key_width / 3.0)
    is_moved = slot == moved[0]
    second = jnp.where(is_moved, q_in[...], q_two[0])
    queries = jnp.concatenate([q_one[0], second], axis=0)
    fresh_one = kv_one[0]
    fresh_two = jnp.where(is_moved, kv_in[...], kv_two[0])
    fresh = jnp.concatenate(
        [fresh_one, fresh_two, jnp.zeros((14, key_width), jnp.bfloat16)], axis=0
    )
    contract = (((1,), (1,)), ((), ()))
    scores = lax.dot_general(queries, fresh, contract, preferred_element_type=jnp.float32) * scale
    row = lax.broadcasted_iota(jnp.int32, scores.shape, 0)
    col = lax.broadcasted_iota(jnp.int32, scores.shape, 1)
    scores = jnp.where((col == 0) | ((col == 1) & (row >= heads)), scores, NEG)
    top = jnp.max(scores, axis=1, keepdims=True)
    weights = jnp.exp(scores - top)
    total = jnp.sum(weights, axis=1, keepdims=True)
    acc[...] = jnp.dot(
        weights.astype(jnp.bfloat16), fresh[:, :LAT], preferred_element_type=jnp.float32
    )
    live = lens[slot]

    def step(b, carry):
        top, total = carry
        keys = jnp.concatenate(
            [pool[pages[slot * MAXP + 2 * b]], pool[pages[slot * MAXP + 2 * b + 1]]], axis=0
        )
        scores = (
            lax.dot_general(queries, keys, contract, preferred_element_type=jnp.float32) * scale
        )
        col = lax.broadcasted_iota(jnp.int32, scores.shape, 1) + b * block
        scores = jnp.where(col < live, scores, NEG)
        new_top = jnp.maximum(top, jnp.max(scores, axis=1, keepdims=True))
        shrink = jnp.exp(top - new_top)
        weights = jnp.exp(scores - new_top)
        total = total * shrink + jnp.sum(weights, axis=1, keepdims=True)
        acc[...] = acc[...] * shrink + jnp.dot(
            weights.astype(jnp.bfloat16), keys[:, :LAT], preferred_element_type=jnp.float32
        )
        return new_top, total

    top, total = lax.fori_loop(0, (live + block - 1) // block, step, (top, total))
    result = (acc[...] / total).astype(jnp.bfloat16)
    out_one[0] = result[:heads]
    out_two[0] = result[heads:]

    @pl.when(is_moved)
    def _():
        out_moved[...] = result[heads:]


def attention(lens, pages, moved, q_one, q_two, q_in, kv_one, kv_two, kv_in, pool):
    samples, heads, key_width = q_one.shape
    one = lambda *shape: pl.BlockSpec((1,) + shape, lambda i, *_: (i,) + (0,) * len(shape))
    whole = lambda *shape: pl.BlockSpec(shape, lambda i, *_: (0,) * len(shape))
    return pl.pallas_call(
        attention_kernel,
        grid_spec=pltpu.PrefetchScalarGridSpec(
            num_scalar_prefetch=3,
            grid=(samples,),
            in_specs=[
                one(heads, key_width),
                one(heads, key_width),
                whole(heads, key_width),
                one(1, key_width),
                one(1, key_width),
                whole(1, key_width),
                whole(*pool.shape),
            ],
            out_specs=[one(heads, LAT), one(heads, LAT), whole(heads, LAT)],
            scratch_shapes=[pltpu.VMEM((2 * heads, LAT), jnp.float32)],
        ),
        out_shape=[
            jax.ShapeDtypeStruct((samples, heads, LAT), jnp.bfloat16),
            jax.ShapeDtypeStruct((samples, heads, LAT), jnp.bfloat16),
            jax.ShapeDtypeStruct((heads, LAT), jnp.bfloat16),
        ],
        compiler_params=pltpu.CompilerParams(vmem_limit_bytes=24 * 1024 * 1024),
        cost_estimate=pl.CostEstimate(
            flops=12_000_000_000, bytes_accessed=8_000_000, transcendentals=1_000_000
        ),
        name="attention",
    )(lens, pages, moved, q_one, q_two, q_in, kv_one, kv_two, kv_in, pool)


def page_table(cache_len, page_perm, page_rows, pool_pages):
    used = (cache_len + page_rows - 1) // page_rows
    slots = used.shape[0]
    before = jnp.arange(slots)[None, :] < jnp.arange(slots)[:, None]
    offset = jnp.sum(jnp.where(before, used[None, :], 0), axis=1)
    place = jnp.minimum(
        offset[:, None] + jnp.arange(MAXP, dtype=jnp.int32)[None, :], pool_pages - 1
    ).reshape(-1)
    hit = place[:, None] == jnp.arange(pool_pages, dtype=jnp.int32)[None, :]
    return jnp.sum(jnp.where(hit, page_perm[None, :], 0), axis=1)


def shards(
    hidden,
    expert_ids,
    gate_weights,
    w_up,
    w_down,
    query_first,
    kv_first,
    query_second,
    kv_second,
    cache_pool,
    cache_len,
    page_perm,
    mig_slot,
    mig_dest,
):
    samples, picks = expert_ids.shape
    width = hidden.shape[1]
    ep_size = lax.axis_size("ep")
    grp_size = lax.axis_size("grp")
    capacity = min(samples, max(2, 2 * samples * picks // ep_size))
    me = lax.axis_index("grp")
    steps = range(grp_size)

    half = width // 2
    side = me // 2
    partner = [(1, 2), (2, 1), (3, 0), (0, 3)]
    relay = [(0, 1), (1, 0), (2, 3), (3, 2)]

    def in_order(own, other, axis):
        first = jnp.where(side == 0, own, other)
        second = jnp.where(side == 0, other, own)
        return jnp.concatenate([first, second], axis=axis)

    def part(value, which, axis):
        return lax.dynamic_slice_in_dim(value, which * half, half, axis)

    ids = in_order(expert_ids, lax.ppermute(expert_ids, "grp", partner), 0)
    rows = in_order(
        part(hidden, side, 1), lax.ppermute(part(hidden, 1 - side, 1), "grp", partner), 0
    )
    pair_gates = lax.ppermute(gate_weights, "grp", partner)

    def spread(weight):
        ahead = jnp.where((me == 0) | (me == 3), 0, 1)
        prev = hop(part(weight, ahead, 0), "grp", 1)
        nxt = hop(part(weight, 1 - ahead, 0), "grp", -1)
        return part(weight, side, 0), prev, nxt

    def pass_on(prev, nxt):
        return lax.ppermute(jnp.where(me % 2 == 0, prev, nxt), "grp", relay)

    up_own, up_prev, up_next = spread(w_up[0])
    up_prev, up_next, down = lax.optimization_barrier((up_prev, up_next, w_down[0]))
    up_far = pass_on(up_prev, up_next)
    down_own, down_prev, down_next = spread(down)
    down_far = pass_on(down_prev, down_next)
    up_all = [up_own, up_next, up_far, up_prev]
    down_all = [down_own, down_next, down_far, down_prev]

    rank = 2 * capacity
    lanes_all = ep_size * rank
    flat_ids = ids.reshape(-1)
    entries = flat_ids.shape[0]
    hits = flat_ids[:, None] == jnp.arange(ep_size, dtype=jnp.int32)[None, :]
    order = jnp.arange(entries, dtype=jnp.int32)
    per = samples * picks
    lower = (order[None, :] < order[:, None]) & (order[None, :] // per == order[:, None] // per)
    ahead = jnp.dot(
        lower.astype(jnp.bfloat16), hits.astype(jnp.bfloat16), preferred_element_type=jnp.float32
    )
    earlier = jnp.sum(jnp.where(hits, ahead, 0.0), axis=1).astype(jnp.int32)
    place = (flat_ids * rank + (order // per) * capacity + earlier).reshape(2 * samples, picks)
    match = place[:, :, None] == jnp.arange(lanes_all, dtype=jnp.int32)[None, None, :]
    placing = jnp.sum(match.astype(jnp.float32), axis=1).astype(jnp.bfloat16)
    outgoing = lax.dot_general(
        placing, rows, (((0,), (0,)), ((), ())), preferred_element_type=jnp.float32
    ).astype(jnp.bfloat16)
    arrived = lax.all_to_all(
        outgoing.reshape(ep_size, rank, half), "ep", split_axis=0, concat_axis=0, tiled=True
    ).reshape(lanes_all, half)

    moved_slot = mig_slot[0, 0]
    moved_target = mig_dest[0, 0]
    query_second, kv_second = after(outgoing, query_second, kv_second)
    q_here = lax.dynamic_index_in_dim(query_second, moved_slot, 0, keepdims=False)
    kv_here = lax.dynamic_index_in_dim(kv_second, moved_slot, 0, keepdims=True)
    packet = jnp.concatenate(
        [q_here, kv_here, jnp.zeros((15, q_here.shape[1]), jnp.bfloat16)], axis=0
    )
    offset = (moved_target - me) % grp_size
    got = packet
    for r in steps[1:]:
        got = jnp.where(offset == r, hop(packet, "grp", -r), got)
    heads = q_here.shape[0]
    q_in, kv_in = got[:heads], got[heads : heads + 1]

    lens = cache_len[0]
    pages = page_table(lens, page_perm[0], cache_pool.shape[1], cache_pool.shape[0])
    attn_first, attn_second, out_moved = attention(
        lens,
        pages,
        moved_slot[None],
        query_first,
        query_second,
        q_in,
        kv_first[:, None, :],
        kv_second[:, None, :],
        kv_in,
        cache_pool,
    )
    zero = jnp.zeros((), jnp.bfloat16)
    arrived_out = jnp.where(offset == 0, out_moved, zero)
    for r in steps[1:]:
        arrived_out = arrived_out + hop(jnp.where(offset == r, out_moved, zero), "grp", r)
    attn_second = lax.dynamic_update_index_in_dim(attn_second, arrived_out, moved_slot, 0)

    f32dot = functools.partial(jnp.dot, preferred_element_type=jnp.float32)
    mine = [f32dot(arrived, weight) for weight in up_all]
    theirs = lax.ppermute(jnp.stack([m.astype(jnp.bfloat16) for m in mine]), "grp", partner)
    odd = me % 2 == 1
    held = []
    for i in range(grp_size):
        other = jnp.where(odd, theirs[(i - 1) % grp_size], theirs[(i + 1) % grp_size])
        held.append(jax.nn.silu(mine[i] + other.astype(jnp.float32)).astype(jnp.bfloat16))
    produced = 0.0
    for h, weight in zip(held, down_all):
        produced = produced + lax.dot_general(
            h, weight, (((1,), (1,)), ((), ())), preferred_element_type=jnp.float32
        )
    returned = lax.all_to_all(
        produced.astype(jnp.bfloat16).reshape(ep_size, rank, half),
        "ep",
        split_axis=0,
        concat_axis=0,
        tiled=True,
    ).reshape(lanes_all, half)
    gates = in_order(gate_weights, pair_gates, 0)
    mixing = jnp.sum(jnp.where(match, gates[:, :, None], 0.0), axis=1)
    high = lax.reduce_precision(mixing, 8, 7)
    mixing = jnp.concatenate([high, mixing - high], axis=0).astype(jnp.bfloat16)
    mixed = f32dot(mixing, returned)
    summed = (mixed[: 2 * samples] + mixed[2 * samples :]).astype(jnp.bfloat16)
    first, second = summed[:samples], summed[samples:]
    own = jnp.where(side == 0, first, second)
    other = lax.ppermute(jnp.where(side == 0, second, first), "grp", partner)
    moe_out = in_order(own, other, 1)
    return (attn_first, attn_second, moe_out)


def solution(mesh):
    return jax.shard_map(
        shards,
        mesh=mesh,
        in_specs=(
            P(("ep", "grp"), None),
            P(("ep", "grp"), None),
            P(("ep", "grp"), None),
            P("ep", None, "grp"),
            P("ep", None, "grp"),
            P(("ep", "grp"), None, None),
            P(("ep", "grp"), None),
            P(("ep", "grp"), None, None),
            P(("ep", "grp"), None),
            P(("ep", "grp"), None, None),
            P(("ep", "grp"), None),
            P(("ep", "grp"), None),
            P("ep", "grp"),
            P("ep", "grp"),
        ),
        out_specs=(
            P(("ep", "grp"), None, None),
            P(("ep", "grp"), None, None),
            P(("ep", "grp"), None),
        ),
        check_vma=False,
    )
```

```python
import math

import jax
import jax.numpy as jnp
from jax import lax
from jax.experimental import pallas as pl
from jax.experimental.pallas import tpu as pltpu
from jax.sharding import PartitionSpec as P

LAT = 512
MAXP = 8
NEG = -1e30


def hop(value, axis, step):
    size = lax.axis_size(axis)
    return lax.ppermute(value, axis, [(i, (i + step) % size) for i in range(size)])


def after(first, *values):
    return lax.optimization_barrier((first,) + values)[1:]


def attention_kernel(
    lens, pages, moved, q_one, q_two, q_in, kv_one, kv_two, kv_in, pool, out_one, out_two, out_moved, acc
):
    slot = pl.program_id(0)
    heads = q_one.shape[1]
    rows = 2 * heads
    key_width = q_one.shape[2]
    page_rows = pool.shape[1]
    block = 2 * page_rows
    scale = 1.0 / math.sqrt(key_width / 3.0)
    is_moved = slot == moved[0]
    second = jnp.where(is_moved, q_in[...], q_two[0])
    queries = jnp.concatenate([q_one[0], second], axis=0)
    fresh_one = kv_one[0]
    fresh_two = jnp.where(is_moved, kv_in[...], kv_two[0])
    fresh = jnp.concatenate(
        [fresh_one, fresh_two, jnp.zeros((14, key_width), jnp.bfloat16)], axis=0
    )
    contract = (((1,), (1,)), ((), ()))
    scores = lax.dot_general(queries, fresh, contract, preferred_element_type=jnp.float32) * scale
    row = lax.broadcasted_iota(jnp.int32, scores.shape, 0)
    col = lax.broadcasted_iota(jnp.int32, scores.shape, 1)
    scores = jnp.where((col == 0) | ((col == 1) & (row >= heads)), scores, NEG)
    top = jnp.max(scores, axis=1, keepdims=True)
    weights = jnp.exp(scores - top)
    total = jnp.sum(weights, axis=1, keepdims=True)
    acc[...] = jnp.dot(
        weights.astype(jnp.bfloat16), fresh[:, :LAT], preferred_element_type=jnp.float32
    )
    live = lens[slot]

    def step(b, carry):
        top, total = carry
        keys = jnp.concatenate(
            [pool[pages[slot * MAXP + 2 * b]], pool[pages[slot * MAXP + 2 * b + 1]]], axis=0
        )
        scores = (
            lax.dot_general(queries, keys, contract, preferred_element_type=jnp.float32) * scale
        )
        col = lax.broadcasted_iota(jnp.int32, scores.shape, 1) + b * block
        scores = jnp.where(col < live, scores, NEG)
        new_top = jnp.maximum(top, jnp.max(scores, axis=1, keepdims=True))
        shrink = jnp.exp(top - new_top)
        weights = jnp.exp(scores - new_top)
        total = total * shrink + jnp.sum(weights, axis=1, keepdims=True)
        acc[...] = acc[...] * shrink + jnp.dot(
            weights.astype(jnp.bfloat16), keys[:, :LAT], preferred_element_type=jnp.float32
        )
        return new_top, total

    top, total = lax.fori_loop(0, (live + block - 1) // block, step, (top, total))
    result = (acc[...] / total).astype(jnp.bfloat16)
    out_one[0] = result[:heads]
    out_two[0] = result[heads:]

    @pl.when(is_moved)
    def _():
        out_moved[...] = result[heads:]


def attention(lens, pages, moved, q_one, q_two, q_in, kv_one, kv_two, kv_in, pool):
    samples, heads, key_width = q_one.shape
    one = lambda *shape: pl.BlockSpec((1,) + shape, lambda i, *_: (i,) + (0,) * len(shape))
    whole = lambda *shape: pl.BlockSpec(shape, lambda i, *_: (0,) * len(shape))
    return pl.pallas_call(
        attention_kernel,
        grid_spec=pltpu.PrefetchScalarGridSpec(
            num_scalar_prefetch=3,
            grid=(samples,),
            in_specs=[
                one(heads, key_width),
                one(heads, key_width),
                whole(heads, key_width),
                one(1, key_width),
                one(1, key_width),
                whole(1, key_width),
                whole(*pool.shape),
            ],
            out_specs=[one(heads, LAT), one(heads, LAT), whole(heads, LAT)],
            scratch_shapes=[pltpu.VMEM((2 * heads, LAT), jnp.float32)],
        ),
        out_shape=[
            jax.ShapeDtypeStruct((samples, heads, LAT), jnp.bfloat16),
            jax.ShapeDtypeStruct((samples, heads, LAT), jnp.bfloat16),
            jax.ShapeDtypeStruct((heads, LAT), jnp.bfloat16),
        ],
        compiler_params=pltpu.CompilerParams(vmem_limit_bytes=24 * 1024 * 1024),
        cost_estimate=pl.CostEstimate(
            flops=12_000_000_000, bytes_accessed=8_000_000, transcendentals=1_000_000
        ),
        name="attention",
    )(lens, pages, moved, q_one, q_two, q_in, kv_one, kv_two, kv_in, pool)


def up_kernel(rows, *refs):
    weights, (whole, sent) = refs[:4], refs[4:]
    step = pl.program_id(0)
    for i, weight in enumerate(weights):
        part = jnp.dot(rows[...], weight[...], preferred_element_type=jnp.float32)

        @pl.when(step == 0)
        def _():
            whole[i] = part

        @pl.when(step > 0)
        def _():
            whole[i] += part

    @pl.when(step == pl.num_programs(0) - 1)
    def _():
        sent[...] = whole[...].astype(jnp.bfloat16)


def up_project(rows, weights, steps):
    count, depth = rows.shape
    units = weights[0].shape[1]
    shape = (len(weights), count, units)
    out = pl.BlockSpec(shape, lambda k: (0, 0, 0))
    return pl.pallas_call(
        up_kernel,
        grid=(steps,),
        in_specs=[pl.BlockSpec((count, depth // steps), lambda k: (0, k))]
        + [pl.BlockSpec((depth // steps, units), lambda k: (k, 0))] * len(weights),
        out_specs=[out, out],
        out_shape=[
            jax.ShapeDtypeStruct(shape, jnp.float32),
            jax.ShapeDtypeStruct(shape, jnp.bfloat16),
        ],
        compiler_params=pltpu.CompilerParams(vmem_limit_bytes=32 * 1024 * 1024),
        cost_estimate=pl.CostEstimate(
            flops=2 * len(weights) * count * depth * units,
            bytes_accessed=9_000_000,
            transcendentals=0,
        ),
        name="up_project",
    )(rows, *weights)


def down_kernel(shift, mine, theirs, *refs):
    weights, out, held = refs[:4], refs[4], refs[5]

    @pl.when(pl.program_id(0) == 0)
    def _():
        for i in range(len(weights)):
            other = theirs[lax.rem(i + shift[0], len(weights))].astype(jnp.float32)
            value = mine[i] + other
            held[i] = (value / (1.0 + jnp.exp(-value))).astype(jnp.bfloat16)

    total = None
    for i, weight in enumerate(weights):
        part = lax.dot_general(
            held[i], weight[...], (((1,), (1,)), ((), ())), preferred_element_type=jnp.float32
        )
        total = part if total is None else total + part
    out[...] = total.astype(jnp.bfloat16)


def down_project(shift, mine, theirs, weights, steps):
    count, units = mine.shape[1:]
    depth = weights[0].shape[0]
    whole = pl.BlockSpec(mine.shape, lambda k, *_: (0, 0, 0))
    return pl.pallas_call(
        down_kernel,
        grid_spec=pltpu.PrefetchScalarGridSpec(
            num_scalar_prefetch=1,
            grid=(steps,),
            in_specs=[whole, whole]
            + [pl.BlockSpec((depth // steps, units), lambda k, *_: (k, 0))] * len(weights),
            out_specs=pl.BlockSpec((count, depth // steps), lambda k, *_: (0, k)),
            scratch_shapes=[pltpu.VMEM(mine.shape, jnp.bfloat16)],
        ),
        out_shape=jax.ShapeDtypeStruct((count, depth), jnp.bfloat16),
        compiler_params=pltpu.CompilerParams(vmem_limit_bytes=32 * 1024 * 1024),
        cost_estimate=pl.CostEstimate(
            flops=2 * len(weights) * count * depth * units,
            bytes_accessed=9_000_000,
            transcendentals=mine.size,
        ),
        name="down_project",
    )(shift, mine, theirs, *weights)


def page_table(cache_len, page_perm, page_rows, pool_pages):
    used = (cache_len + page_rows - 1) // page_rows
    slots = used.shape[0]
    before = jnp.arange(slots)[None, :] < jnp.arange(slots)[:, None]
    offset = jnp.sum(jnp.where(before, used[None, :], 0), axis=1)
    place = jnp.minimum(
        offset[:, None] + jnp.arange(MAXP, dtype=jnp.int32)[None, :], pool_pages - 1
    ).reshape(-1)
    hit = place[:, None] == jnp.arange(pool_pages, dtype=jnp.int32)[None, :]
    return jnp.sum(jnp.where(hit, page_perm[None, :], 0), axis=1)


def shards(
    hidden,
    expert_ids,
    gate_weights,
    w_up,
    w_down,
    query_first,
    kv_first,
    query_second,
    kv_second,
    cache_pool,
    cache_len,
    page_perm,
    mig_slot,
    mig_dest,
):
    samples, picks = expert_ids.shape
    width = hidden.shape[1]
    ep_size = lax.axis_size("ep")
    grp_size = lax.axis_size("grp")
    capacity = min(samples, max(2, 2 * samples * picks // ep_size))
    me = lax.axis_index("grp")
    steps = range(grp_size)

    half = width // 2
    side = me // 2
    partner = [(1, 2), (2, 1), (3, 0), (0, 3)]
    relay = [(0, 1), (1, 0), (2, 3), (3, 2)]

    def in_order(own, other, axis):
        first = jnp.where(side == 0, own, other)
        second = jnp.where(side == 0, other, own)
        return jnp.concatenate([first, second], axis=axis)

    def part(value, which, axis):
        return lax.dynamic_slice_in_dim(value, which * half, half, axis)

    rows = in_order(
        part(hidden, side, 1), lax.ppermute(part(hidden, 1 - side, 1), "grp", partner), 0
    )
    ids = in_order(expert_ids, lax.ppermute(expert_ids, "grp", partner), 0)

    def spread(weight):
        ahead = jnp.where((me == 0) | (me == 3), 0, 1)
        prev = hop(part(weight, ahead, 0), "grp", 1)
        nxt = hop(part(weight, 1 - ahead, 0), "grp", -1)
        return part(weight, side, 0), prev, nxt

    def pass_on(prev, nxt):
        return lax.ppermute(jnp.where(me % 2 == 0, prev, nxt), "grp", relay)

    up_own, up_prev, up_next = spread(w_up[0])
    up_prev, up_next, down = lax.optimization_barrier((up_prev, up_next, w_down[0]))
    up_far = pass_on(up_prev, up_next)
    down_own, down_prev, down_next = spread(down)
    down_far = pass_on(down_prev, down_next)
    up_all = [up_own, up_next, up_far, up_prev]
    down_all = [down_own, down_next, down_far, down_prev]

    rank = 2 * capacity
    lanes_all = ep_size * rank
    flat_ids = ids.reshape(-1)
    entries = flat_ids.shape[0]
    hits = flat_ids[:, None] == jnp.arange(ep_size, dtype=jnp.int32)[None, :]
    order = jnp.arange(entries, dtype=jnp.int32)
    per = samples * picks
    lower = (order[None, :] < order[:, None]) & (order[None, :] // per == order[:, None] // per)
    ahead = jnp.dot(
        lower.astype(jnp.bfloat16), hits.astype(jnp.bfloat16), preferred_element_type=jnp.float32
    )
    earlier = jnp.sum(jnp.where(hits, ahead, 0.0), axis=1).astype(jnp.int32)
    place = (flat_ids * rank + (order // per) * capacity + earlier).reshape(2 * samples, picks)
    match = place[:, :, None] == jnp.arange(lanes_all, dtype=jnp.int32)[None, None, :]
    placing = jnp.sum(match.astype(jnp.float32), axis=1).astype(jnp.bfloat16)
    outgoing = lax.dot_general(
        placing, rows, (((0,), (0,)), ((), ())), preferred_element_type=jnp.float32
    ).astype(jnp.bfloat16)
    arrived = lax.all_to_all(
        outgoing.reshape(ep_size, rank, half), "ep", split_axis=0, concat_axis=0, tiled=True
    ).reshape(lanes_all, half)

    moved_slot = mig_slot[0, 0]
    moved_target = mig_dest[0, 0]
    query_second, kv_second = after(outgoing, query_second, kv_second)
    q_here = lax.dynamic_index_in_dim(query_second, moved_slot, 0, keepdims=False)
    kv_here = lax.dynamic_index_in_dim(kv_second, moved_slot, 0, keepdims=True)
    packet = jnp.concatenate(
        [q_here, kv_here, jnp.zeros((15, q_here.shape[1]), jnp.bfloat16)], axis=0
    )
    offset = (moved_target - me) % grp_size
    got = packet
    for r in steps[1:]:
        got = jnp.where(offset == r, hop(packet, "grp", -r), got)
    heads = q_here.shape[0]
    q_in, kv_in = got[:heads], got[heads : heads + 1]

    lens = cache_len[0]
    pages = page_table(lens, page_perm[0], cache_pool.shape[1], cache_pool.shape[0])
    attn_first, attn_second, out_moved = attention(
        lens,
        pages,
        moved_slot[None],
        query_first,
        query_second,
        q_in,
        kv_first[:, None, :],
        kv_second[:, None, :],
        kv_in,
        cache_pool,
    )
    zero = jnp.zeros((), jnp.bfloat16)
    arrived_out = jnp.where(offset == 0, out_moved, zero)
    for r in steps[1:]:
        arrived_out = arrived_out + hop(jnp.where(offset == r, out_moved, zero), "grp", r)
    attn_second = lax.dynamic_update_index_in_dim(attn_second, arrived_out, moved_slot, 0)

    mine, rounded = up_project(arrived, up_all, 2)
    theirs = lax.ppermute(rounded, "grp", partner)
    shift = jnp.where(me % 2 == 1, grp_size - 1, 1).astype(jnp.int32)
    produced = down_project(shift[None], mine, theirs, down_all, 7)
    returned = lax.all_to_all(
        produced.reshape(ep_size, rank, half),
        "ep",
        split_axis=0,
        concat_axis=0,
        tiled=True,
    ).reshape(lanes_all, half)
    (late_gates,) = after(outgoing, gate_weights)
    gates = in_order(gate_weights, lax.ppermute(late_gates, "grp", partner), 0)
    mixing = jnp.sum(jnp.where(match, gates[:, :, None], 0.0), axis=1)
    high = lax.reduce_precision(mixing, 8, 7)
    mixing = jnp.concatenate([high, mixing - high], axis=0).astype(jnp.bfloat16)
    mixed = jnp.dot(mixing, returned, preferred_element_type=jnp.float32)
    summed = (mixed[: 2 * samples] + mixed[2 * samples :]).astype(jnp.bfloat16)
    first, second = summed[:samples], summed[samples:]
    own = jnp.where(side == 0, first, second)
    other = lax.ppermute(jnp.where(side == 0, second, first), "grp", partner)
    moe_out = in_order(own, other, 1)
    return (attn_first, attn_second, moe_out)


def solution(mesh):
    return jax.shard_map(
        shards,
        mesh=mesh,
        in_specs=(
            P(("ep", "grp"), None),
            P(("ep", "grp"), None),
            P(("ep", "grp"), None),
            P("ep", None, "grp"),
            P("ep", None, "grp"),
            P(("ep", "grp"), None, None),
            P(("ep", "grp"), None),
            P(("ep", "grp"), None, None),
            P(("ep", "grp"), None),
            P(("ep", "grp"), None, None),
            P(("ep", "grp"), None),
            P(("ep", "grp"), None),
            P("ep", "grp"),
            P("ep", "grp"),
        ),
        out_specs=(
            P(("ep", "grp"), None, None),
            P(("ep", "grp"), None, None),
            P(("ep", "grp"), None),
        ),
        check_vma=False,
    )
```

```python
import math

import jax
import jax.numpy as jnp
from jax import lax
from jax.experimental import pallas as pl
from jax.experimental.pallas import tpu as pltpu
from jax.sharding import PartitionSpec as P

LAT = 512
MAXP = 8
NEG = -1e30
PAIRS = ((1, 2), (2, 1), (3, 0), (0, 3))


def hop(value, axis, step):
    size = lax.axis_size(axis)
    return lax.ppermute(value, axis, [(i, (i + step) % size) for i in range(size)])


def after(first, *values):
    return lax.optimization_barrier((first,) + values)[1:]


def attention_kernel(
    lens, pages, moved, q_one, q_two, q_in, kv_one, kv_two, kv_in, pool, out_one, out_two, out_moved, acc
):
    slot = pl.program_id(0)
    heads = q_one.shape[1]
    rows = 2 * heads
    key_width = q_one.shape[2]
    page_rows = pool.shape[1]
    block = 2 * page_rows
    scale = 1.0 / math.sqrt(key_width / 3.0)
    is_moved = slot == moved[0]
    second = jnp.where(is_moved, q_in[...], q_two[0])
    queries = jnp.concatenate([q_one[0], second], axis=0)
    fresh_one = kv_one[0]
    fresh_two = jnp.where(is_moved, kv_in[...], kv_two[0])
    fresh = jnp.concatenate(
        [fresh_one, fresh_two, jnp.zeros((14, key_width), jnp.bfloat16)], axis=0
    )
    contract = (((1,), (1,)), ((), ()))
    scores = lax.dot_general(queries, fresh, contract, preferred_element_type=jnp.float32) * scale
    row = lax.broadcasted_iota(jnp.int32, scores.shape, 0)
    col = lax.broadcasted_iota(jnp.int32, scores.shape, 1)
    scores = jnp.where((col == 0) | ((col == 1) & (row >= heads)), scores, NEG)
    top = jnp.max(scores, axis=1, keepdims=True)
    weights = jnp.exp(scores - top)
    total = jnp.sum(weights, axis=1, keepdims=True)
    acc[...] = jnp.dot(
        weights.astype(jnp.bfloat16), fresh[:, :LAT], preferred_element_type=jnp.float32
    )
    live = lens[slot]

    def step(b, carry):
        top, total = carry
        keys = jnp.concatenate(
            [pool[pages[slot * MAXP + 2 * b]], pool[pages[slot * MAXP + 2 * b + 1]]], axis=0
        )
        scores = (
            lax.dot_general(queries, keys, contract, preferred_element_type=jnp.float32) * scale
        )
        col = lax.broadcasted_iota(jnp.int32, scores.shape, 1) + b * block
        scores = jnp.where(col < live, scores, NEG)
        new_top = jnp.maximum(top, jnp.max(scores, axis=1, keepdims=True))
        shrink = jnp.exp(top - new_top)
        weights = jnp.exp(scores - new_top)
        total = total * shrink + jnp.sum(weights, axis=1, keepdims=True)
        acc[...] = acc[...] * shrink + jnp.dot(
            weights.astype(jnp.bfloat16), keys[:, :LAT], preferred_element_type=jnp.float32
        )
        return new_top, total

    top, total = lax.fori_loop(0, (live + block - 1) // block, step, (top, total))
    result = (acc[...] / total).astype(jnp.bfloat16)
    out_one[0] = result[:heads]
    out_two[0] = result[heads:]

    @pl.when(is_moved)
    def _():
        out_moved[...] = result[heads:]


def attention(lens, pages, moved, q_one, q_two, q_in, kv_one, kv_two, kv_in, pool):
    samples, heads, key_width = q_one.shape
    one = lambda *shape: pl.BlockSpec((1,) + shape, lambda i, *_: (i,) + (0,) * len(shape))
    whole = lambda *shape: pl.BlockSpec(shape, lambda i, *_: (0,) * len(shape))
    return pl.pallas_call(
        attention_kernel,
        grid_spec=pltpu.PrefetchScalarGridSpec(
            num_scalar_prefetch=3,
            grid=(samples,),
            in_specs=[
                one(heads, key_width),
                one(heads, key_width),
                whole(heads, key_width),
                one(1, key_width),
                one(1, key_width),
                whole(1, key_width),
                whole(*pool.shape),
            ],
            out_specs=[one(heads, LAT), one(heads, LAT), whole(heads, LAT)],
            scratch_shapes=[pltpu.VMEM((2 * heads, LAT), jnp.float32)],
        ),
        out_shape=[
            jax.ShapeDtypeStruct((samples, heads, LAT), jnp.bfloat16),
            jax.ShapeDtypeStruct((samples, heads, LAT), jnp.bfloat16),
            jax.ShapeDtypeStruct((heads, LAT), jnp.bfloat16),
        ],
        compiler_params=pltpu.CompilerParams(vmem_limit_bytes=24 * 1024 * 1024),
        cost_estimate=pl.CostEstimate(
            flops=12_000_000_000, bytes_accessed=8_000_000, transcendentals=1_000_000
        ),
        name="attention",
    )(lens, pages, moved, q_one, q_two, q_in, kv_one, kv_two, kv_in, pool)


def up_kernel(rows, *refs):
    weights, (whole, sent) = refs[:4], refs[4:]
    for i, weight in enumerate(weights):
        part = jnp.dot(rows[...], weight[...], preferred_element_type=jnp.float32)
        whole[i] = part
        sent[i] = part.astype(jnp.bfloat16)


def up_project(rows, weights, steps):
    count, depth = rows.shape
    units = weights[0].shape[1]
    shape = (len(weights), count, units)
    out = pl.BlockSpec((len(weights), count // steps, units), lambda k: (0, k, 0))
    return pl.pallas_call(
        up_kernel,
        grid=(steps,),
        in_specs=[pl.BlockSpec((count // steps, depth), lambda k: (k, 0))]
        + [pl.BlockSpec((depth, units), lambda k: (0, 0))] * len(weights),
        out_specs=[out, out],
        out_shape=[
            jax.ShapeDtypeStruct(shape, jnp.float32),
            jax.ShapeDtypeStruct(shape, jnp.bfloat16),
        ],
        compiler_params=pltpu.CompilerParams(vmem_limit_bytes=58 * 1024 * 1024),
        cost_estimate=pl.CostEstimate(
            flops=2 * len(weights) * count * depth * units,
            bytes_accessed=9_000_000,
            transcendentals=0,
        ),
        name="up_project",
    )(rows, *weights)


def down_kernel(shift, mine, theirs, *refs):
    weights, out, held = refs[:4], refs[4], refs[5]

    @pl.when(pl.program_id(0) == 0)
    def _():
        for i in range(len(weights)):
            other = theirs[lax.rem(i + shift[0], len(weights))].astype(jnp.float32)
            value = mine[i] + other
            held[i] = (value / (1.0 + jnp.exp(-value))).astype(jnp.bfloat16)

    total = None
    for i, weight in enumerate(weights):
        part = lax.dot_general(
            held[i], weight[...], (((1,), (1,)), ((), ())), preferred_element_type=jnp.float32
        )
        total = part if total is None else total + part
    out[...] = total.astype(jnp.bfloat16)


def down_project(shift, mine, theirs, weights, steps):
    count, units = mine.shape[1:]
    depth = weights[0].shape[0]
    whole = pl.BlockSpec(mine.shape, lambda k, *_: (0, 0, 0))
    return pl.pallas_call(
        down_kernel,
        grid_spec=pltpu.PrefetchScalarGridSpec(
            num_scalar_prefetch=1,
            grid=(steps,),
            in_specs=[whole, whole]
            + [pl.BlockSpec((depth // steps, units), lambda k, *_: (k, 0))] * len(weights),
            out_specs=pl.BlockSpec((count, depth // steps), lambda k, *_: (0, k)),
            scratch_shapes=[pltpu.VMEM(mine.shape, jnp.bfloat16)],
        ),
        out_shape=jax.ShapeDtypeStruct((count, depth), jnp.bfloat16),
        compiler_params=pltpu.CompilerParams(vmem_limit_bytes=24 * 1024 * 1024),
        cost_estimate=pl.CostEstimate(
            flops=2 * len(weights) * count * depth * units,
            bytes_accessed=9_000_000,
            transcendentals=mine.size,
        ),
        name="down_project",
    )(shift, mine, theirs, *weights)


def page_table(cache_len, page_perm, page_rows, pool_pages):
    used = (cache_len + page_rows - 1) // page_rows
    slots = used.shape[0]
    before = jnp.arange(slots)[None, :] < jnp.arange(slots)[:, None]
    offset = jnp.sum(jnp.where(before, used[None, :], 0), axis=1)
    place = jnp.minimum(
        offset[:, None] + jnp.arange(MAXP, dtype=jnp.int32)[None, :], pool_pages - 1
    ).reshape(-1)
    hit = place[:, None] == jnp.arange(pool_pages, dtype=jnp.int32)[None, :]
    return jnp.sum(jnp.where(hit, page_perm[None, :], 0), axis=1)


def shards(
    hidden,
    expert_ids,
    gate_weights,
    w_up,
    w_down,
    query_first,
    kv_first,
    query_second,
    kv_second,
    cache_pool,
    cache_len,
    page_perm,
    mig_slot,
    mig_dest,
):
    samples, picks = expert_ids.shape
    width = hidden.shape[1]
    ep_size = lax.axis_size("ep")
    grp_size = lax.axis_size("grp")
    capacity = min(samples, max(2, 2 * samples * picks // ep_size))
    me = lax.axis_index("grp")
    steps = range(grp_size)

    half = width // 2
    core = lax.axis_index("ep") % 2
    turned = [(me - c) % grp_size for c in range(2)]
    side = [turned[c] // 2 for c in range(2)]
    here = jnp.where(core == 0, turned[0], turned[1])
    partner = [[((a + c) % grp_size, (b + c) % grp_size) for a, b in PAIRS] for c in range(2)]

    def by_core(pairs):
        return [
            (e * grp_size + (a + e % 2) % grp_size, e * grp_size + (b + e % 2) % grp_size)
            for e in range(ep_size)
            for a, b in pairs
        ]

    def part(value, which, axis):
        return lax.dynamic_slice_in_dim(value, which * half, half, axis)

    rows, id_list = [], [expert_ids]
    for c in range(2):
        id_list.append(lax.ppermute(expert_ids, "grp", partner[c]))
        rows.append(part(hidden, side[c], 1))
        rows.append(lax.ppermute(part(hidden, 1 - side[c], 1), "grp", partner[c]))
    rows = jnp.concatenate(rows, axis=0)

    def spread(weight):
        ahead = jnp.where((here == 0) | (here == 3), 0, 1)
        prev = hop(part(weight, ahead, 0), "grp", 1)
        nxt = hop(part(weight, 1 - ahead, 0), "grp", -1)
        return part(weight, here // 2, 0), prev, nxt

    def pass_on(prev, nxt):
        return lax.ppermute(
            jnp.where(here % 2 == 0, prev, nxt), ("ep", "grp"), by_core([(0, 1), (1, 0), (2, 3), (3, 2)])
        )

    up_own, up_prev, up_next = spread(w_up[0])
    up_prev, up_next, down = lax.optimization_barrier((up_prev, up_next, w_down[0]))
    up_far = pass_on(up_prev, up_next)
    down_own, down_prev, down_next = spread(down)
    down_far = pass_on(down_prev, down_next)
    up_all = [up_own, up_next, up_far, up_prev]
    down_all = [down_own, down_next, down_far, down_prev]

    rank = 2 * capacity
    lanes_all = ep_size * rank
    flat_ids = jnp.concatenate(id_list, axis=0).reshape(-1)
    entries = flat_ids.shape[0]
    hits = flat_ids[:, None] == jnp.arange(ep_size, dtype=jnp.int32)[None, :]
    order = jnp.arange(entries, dtype=jnp.int32)
    per = samples * picks
    lower = (order[None, :] < order[:, None]) & (order[None, :] // per == order[:, None] // per)
    ahead = jnp.dot(
        lower.astype(jnp.bfloat16), hits.astype(jnp.bfloat16), preferred_element_type=jnp.float32
    )
    earlier = jnp.sum(jnp.where(hits, ahead, 0.0), axis=1).astype(jnp.int32)
    place = (flat_ids * rank + earlier).reshape(3, samples, picks)
    own_at, first_at, second_at = place[0], place[1], place[2]
    even = (expert_ids % 2) == 0
    place = jnp.concatenate(
        [
            jnp.where(even, own_at + side[0] * capacity, -1),
            jnp.where((id_list[1] % 2) == 0, first_at + (1 - side[0]) * capacity, -1),
            jnp.where(even, -1, own_at + side[1] * capacity),
            jnp.where((id_list[2] % 2) == 0, -1, second_at + (1 - side[1]) * capacity),
        ],
        axis=0,
    )
    match = place[:, :, None] == jnp.arange(lanes_all, dtype=jnp.int32)[None, None, :]
    placing = jnp.sum(match.astype(jnp.float32), axis=1).astype(jnp.bfloat16)
    outgoing = lax.dot_general(
        placing, rows, (((0,), (0,)), ((), ())), preferred_element_type=jnp.float32
    ).astype(jnp.bfloat16)
    arrived = lax.all_to_all(
        outgoing.reshape(ep_size, rank, half), "ep", split_axis=0, concat_axis=0, tiled=True
    ).reshape(lanes_all, half)

    moved_slot = mig_slot[0, 0]
    moved_target = mig_dest[0, 0]
    query_second, kv_second = after(outgoing, query_second, kv_second)
    q_here = lax.dynamic_index_in_dim(query_second, moved_slot, 0, keepdims=False)
    kv_here = lax.dynamic_index_in_dim(kv_second, moved_slot, 0, keepdims=True)
    packet = jnp.concatenate(
        [q_here, kv_here, jnp.zeros((15, q_here.shape[1]), jnp.bfloat16)], axis=0
    )
    offset = (moved_target - me) % grp_size
    got = packet
    for r in steps[1:]:
        got = jnp.where(offset == r, hop(packet, "grp", -r), got)
    heads = q_here.shape[0]
    q_in, kv_in = got[:heads], got[heads : heads + 1]

    lens = cache_len[0]
    pages = page_table(lens, page_perm[0], cache_pool.shape[1], cache_pool.shape[0])
    attn_first, attn_second, out_moved = attention(
        lens,
        pages,
        moved_slot[None],
        query_first,
        query_second,
        q_in,
        kv_first[:, None, :],
        kv_second[:, None, :],
        kv_in,
        cache_pool,
    )
    zero = jnp.zeros((), jnp.bfloat16)
    arrived_out = jnp.where(offset == 0, out_moved, zero)
    for r in steps[1:]:
        arrived_out = arrived_out + hop(jnp.where(offset == r, out_moved, zero), "grp", r)
    attn_second = lax.dynamic_update_index_in_dim(attn_second, arrived_out, moved_slot, 0)

    mine, rounded = up_project(arrived, up_all, 2)
    theirs = lax.ppermute(rounded, ("ep", "grp"), by_core(PAIRS))
    shift = jnp.where(here % 2 == 1, grp_size - 1, 1).astype(jnp.int32)
    produced = down_project(shift[None], mine, theirs, down_all, 2)
    returned = lax.all_to_all(
        produced.reshape(ep_size, rank, half),
        "ep",
        split_axis=0,
        concat_axis=0,
        tiled=True,
    ).reshape(lanes_all, half)
    (late_gates,) = after(outgoing, gate_weights)
    gates = jnp.concatenate(
        [
            gate_weights,
            lax.ppermute(late_gates, "grp", partner[0]),
            gate_weights,
            lax.ppermute(late_gates, "grp", partner[1]),
        ],
        axis=0,
    )
    mixing = jnp.sum(jnp.where(match, gates[:, :, None], 0.0), axis=1)
    high = lax.reduce_precision(mixing, 8, 7)
    mixing = jnp.concatenate([high, mixing - high], axis=0).astype(jnp.bfloat16)
    mixed = jnp.dot(mixing, returned, preferred_element_type=jnp.float32)
    summed = (mixed[: 4 * samples] + mixed[4 * samples :]).reshape(4, samples, half)
    first, second = 0.0, 0.0
    for c in range(2):
        own = summed[2 * c]
        other = lax.ppermute(summed[2 * c + 1], "grp", partner[c])
        first = first + jnp.where(side[c] == 0, own, other)
        second = second + jnp.where(side[c] == 0, other, own)
    moe_out = jnp.concatenate([first, second], axis=1).astype(jnp.bfloat16)
    return (attn_first, attn_second, moe_out)


def solution(mesh):
    return jax.shard_map(
        shards,
        mesh=mesh,
        in_specs=(
            P(("ep", "grp"), None),
            P(("ep", "grp"), None),
            P(("ep", "grp"), None),
            P("ep", None, "grp"),
            P("ep", None, "grp"),
            P(("ep", "grp"), None, None),
            P(("ep", "grp"), None),
            P(("ep", "grp"), None, None),
            P(("ep", "grp"), None),
            P(("ep", "grp"), None, None),
            P(("ep", "grp"), None),
            P(("ep", "grp"), None),
            P("ep", "grp"),
            P("ep", "grp"),
        ),
        out_specs=(
            P(("ep", "grp"), None, None),
            P(("ep", "grp"), None, None),
            P(("ep", "grp"), None),
        ),
        check_vma=False,
    )
```

```python
import math

import jax
import jax.numpy as jnp
from jax import lax
from jax.experimental import pallas as pl
from jax.experimental.pallas import tpu as pltpu
from jax.sharding import PartitionSpec as P

LAT = 512
MAXP = 8
NEG = -1e30
PAIRS = ((1, 2), (2, 1), (3, 0), (0, 3))


def hop(value, axis, step):
    size = lax.axis_size(axis)
    return lax.ppermute(value, axis, [(i, (i + step) % size) for i in range(size)])


def after(first, *values):
    return lax.optimization_barrier((first,) + values)[1:]


def attention_kernel(
    lens, pages, moved, q_one, q_two, q_in, kv_one, kv_two, kv_in, pool, out_one, out_two, out_moved, acc
):
    slot = pl.program_id(0)
    heads = q_one.shape[1]
    rows = 2 * heads
    key_width = q_one.shape[2]
    page_rows = pool.shape[1]
    block = 2 * page_rows
    scale = 1.0 / math.sqrt(key_width / 3.0)
    is_moved = slot == moved[0]
    second = jnp.where(is_moved, q_in[...], q_two[0])
    queries = jnp.concatenate([q_one[0], second], axis=0)
    fresh_one = kv_one[0]
    fresh_two = jnp.where(is_moved, kv_in[...], kv_two[0])
    fresh = jnp.concatenate(
        [fresh_one, fresh_two, jnp.zeros((14, key_width), jnp.bfloat16)], axis=0
    )
    contract = (((1,), (1,)), ((), ()))
    scores = lax.dot_general(queries, fresh, contract, preferred_element_type=jnp.float32) * scale
    row = lax.broadcasted_iota(jnp.int32, scores.shape, 0)
    col = lax.broadcasted_iota(jnp.int32, scores.shape, 1)
    scores = jnp.where((col == 0) | ((col == 1) & (row >= heads)), scores, NEG)
    top = jnp.max(scores, axis=1, keepdims=True)
    weights = jnp.exp(scores - top)
    total = jnp.sum(weights, axis=1, keepdims=True)
    acc[...] = jnp.dot(
        weights.astype(jnp.bfloat16), fresh[:, :LAT], preferred_element_type=jnp.float32
    )
    live = lens[slot]

    def step(b, carry):
        top, total = carry
        keys = jnp.concatenate(
            [pool[pages[slot * MAXP + 2 * b]], pool[pages[slot * MAXP + 2 * b + 1]]], axis=0
        )
        scores = (
            lax.dot_general(queries, keys, contract, preferred_element_type=jnp.float32) * scale
        )
        col = lax.broadcasted_iota(jnp.int32, scores.shape, 1) + b * block
        scores = jnp.where(col < live, scores, NEG)
        new_top = jnp.maximum(top, jnp.max(scores, axis=1, keepdims=True))
        shrink = jnp.exp(top - new_top)
        weights = jnp.exp(scores - new_top)
        total = total * shrink + jnp.sum(weights, axis=1, keepdims=True)
        acc[...] = acc[...] * shrink + jnp.dot(
            weights.astype(jnp.bfloat16), keys[:, :LAT], preferred_element_type=jnp.float32
        )
        return new_top, total

    top, total = lax.fori_loop(0, (live + block - 1) // block, step, (top, total))
    result = (acc[...] / total).astype(jnp.bfloat16)
    out_one[0] = result[:heads]
    out_two[0] = result[heads:]

    @pl.when(is_moved)
    def _():
        out_moved[...] = result[heads:]


def attention(lens, pages, moved, q_one, q_two, q_in, kv_one, kv_two, kv_in, pool):
    samples, heads, key_width = q_one.shape
    one = lambda *shape: pl.BlockSpec((1,) + shape, lambda i, *_: (i,) + (0,) * len(shape))
    whole = lambda *shape: pl.BlockSpec(shape, lambda i, *_: (0,) * len(shape))
    return pl.pallas_call(
        attention_kernel,
        grid_spec=pltpu.PrefetchScalarGridSpec(
            num_scalar_prefetch=3,
            grid=(samples,),
            in_specs=[
                one(heads, key_width),
                one(heads, key_width),
                whole(heads, key_width),
                one(1, key_width),
                one(1, key_width),
                whole(1, key_width),
                whole(*pool.shape),
            ],
            out_specs=[one(heads, LAT), one(heads, LAT), whole(heads, LAT)],
            scratch_shapes=[pltpu.VMEM((2 * heads, LAT), jnp.float32)],
        ),
        out_shape=[
            jax.ShapeDtypeStruct((samples, heads, LAT), jnp.bfloat16),
            jax.ShapeDtypeStruct((samples, heads, LAT), jnp.bfloat16),
            jax.ShapeDtypeStruct((heads, LAT), jnp.bfloat16),
        ],
        compiler_params=pltpu.CompilerParams(vmem_limit_bytes=24 * 1024 * 1024),
        cost_estimate=pl.CostEstimate(
            flops=12_000_000_000, bytes_accessed=8_000_000, transcendentals=1_000_000
        ),
        name="attention",
    )(lens, pages, moved, q_one, q_two, q_in, kv_one, kv_two, kv_in, pool)


def choose_kernel(which, first, second, out, sem):
    @pl.when(which[0] == 0)
    def _():
        copy = pltpu.make_async_copy(first, out, sem)
        copy.start()
        copy.wait()

    @pl.when(which[0] != 0)
    def _():
        copy = pltpu.make_async_copy(second, out, sem)
        copy.start()
        copy.wait()


def choose(which, first, second, flops):
    return pl.pallas_call(
        choose_kernel,
        grid_spec=pltpu.PrefetchScalarGridSpec(
            num_scalar_prefetch=1,
            grid=(1,),
            in_specs=[pl.BlockSpec(memory_space=pl.ANY)] * 2,
            out_specs=pl.BlockSpec(memory_space=pl.ANY),
            scratch_shapes=[pltpu.SemaphoreType.DMA],
        ),
        out_shape=jax.ShapeDtypeStruct(first.shape, first.dtype),
        cost_estimate=pl.CostEstimate(
            flops=flops, bytes_accessed=2 * first.size * 2, transcendentals=0
        ),
        name="choose",
    )(which, first, second)


def up_kernel(rows, *refs):
    weights, (whole, sent) = refs[:4], refs[4:]
    for i, weight in enumerate(weights):
        part = jnp.dot(rows[...], weight[...], preferred_element_type=jnp.float32)
        whole[i] = part
        sent[i] = part.astype(jnp.bfloat16)


def up_project(rows, weights, steps):
    count, depth = rows.shape
    units = weights[0].shape[1]
    shape = (len(weights), count, units)
    out = pl.BlockSpec((len(weights), count // steps, units), lambda k: (0, k, 0))
    return pl.pallas_call(
        up_kernel,
        grid=(steps,),
        in_specs=[pl.BlockSpec((count // steps, depth), lambda k: (k, 0))]
        + [pl.BlockSpec((depth, units), lambda k: (0, 0))] * len(weights),
        out_specs=[out, out],
        out_shape=[
            jax.ShapeDtypeStruct(shape, jnp.float32),
            jax.ShapeDtypeStruct(shape, jnp.bfloat16),
        ],
        compiler_params=pltpu.CompilerParams(vmem_limit_bytes=58 * 1024 * 1024),
        cost_estimate=pl.CostEstimate(
            flops=2 * len(weights) * count * depth * units,
            bytes_accessed=9_000_000,
            transcendentals=0,
        ),
        name="up_project",
    )(rows, *weights)


def down_kernel(shift, mine, theirs, *refs):
    weights, out, held = refs[:4], refs[4], refs[5]

    @pl.when(pl.program_id(0) == 0)
    def _():
        for i in range(len(weights)):
            other = theirs[lax.rem(i + shift[0], len(weights))].astype(jnp.float32)
            value = mine[i] + other
            held[i] = (value / (1.0 + jnp.exp(-value))).astype(jnp.bfloat16)

    total = None
    for i, weight in enumerate(weights):
        part = lax.dot_general(
            held[i], weight[...], (((1,), (1,)), ((), ())), preferred_element_type=jnp.float32
        )
        total = part if total is None else total + part
    out[...] = total.astype(jnp.bfloat16)


def down_project(shift, mine, theirs, weights, steps):
    count, units = mine.shape[1:]
    depth = weights[0].shape[0]
    whole = pl.BlockSpec(mine.shape, lambda k, *_: (0, 0, 0))
    return pl.pallas_call(
        down_kernel,
        grid_spec=pltpu.PrefetchScalarGridSpec(
            num_scalar_prefetch=1,
            grid=(steps,),
            in_specs=[whole, whole]
            + [pl.BlockSpec((depth // steps, units), lambda k, *_: (k, 0))] * len(weights),
            out_specs=pl.BlockSpec((count, depth // steps), lambda k, *_: (0, k)),
            scratch_shapes=[pltpu.VMEM(mine.shape, jnp.bfloat16)],
        ),
        out_shape=jax.ShapeDtypeStruct((count, depth), jnp.bfloat16),
        compiler_params=pltpu.CompilerParams(vmem_limit_bytes=24 * 1024 * 1024),
        cost_estimate=pl.CostEstimate(
            flops=2 * len(weights) * count * depth * units,
            bytes_accessed=9_000_000,
            transcendentals=mine.size,
        ),
        name="down_project",
    )(shift, mine, theirs, *weights)


def page_table(cache_len, page_perm, page_rows, pool_pages):
    used = (cache_len + page_rows - 1) // page_rows
    slots = used.shape[0]
    before = jnp.arange(slots)[None, :] < jnp.arange(slots)[:, None]
    offset = jnp.sum(jnp.where(before, used[None, :], 0), axis=1)
    place = jnp.minimum(
        offset[:, None] + jnp.arange(MAXP, dtype=jnp.int32)[None, :], pool_pages - 1
    ).reshape(-1)
    hit = place[:, None] == jnp.arange(pool_pages, dtype=jnp.int32)[None, :]
    return jnp.sum(jnp.where(hit, page_perm[None, :], 0), axis=1)


def shards(
    hidden,
    expert_ids,
    gate_weights,
    w_up,
    w_down,
    query_first,
    kv_first,
    query_second,
    kv_second,
    cache_pool,
    cache_len,
    page_perm,
    mig_slot,
    mig_dest,
):
    samples, picks = expert_ids.shape
    width = hidden.shape[1]
    ep_size = lax.axis_size("ep")
    grp_size = lax.axis_size("grp")
    capacity = min(samples, max(2, 2 * samples * picks // ep_size))
    me = lax.axis_index("grp")
    steps = range(grp_size)

    half = width // 2
    core = lax.axis_index("ep") % 2
    turned = [(me - c) % grp_size for c in range(2)]
    side = [turned[c] // 2 for c in range(2)]
    here = jnp.where(core == 0, turned[0], turned[1])
    partner = [[((a + c) % grp_size, (b + c) % grp_size) for a, b in PAIRS] for c in range(2)]

    def by_core(pairs):
        return [
            (e * grp_size + (a + e % 2) % grp_size, e * grp_size + (b + e % 2) % grp_size)
            for e in range(ep_size)
            for a, b in pairs
        ]

    def part(value, which, axis):
        return lax.dynamic_slice_in_dim(value, which * half, half, axis)

    rows, id_list = [], [expert_ids]
    for c in range(2):
        id_list.append(lax.ppermute(expert_ids, "grp", partner[c]))
        rows.append(part(hidden, side[c], 1))
        rows.append(lax.ppermute(part(hidden, 1 - side[c], 1), "grp", partner[c]))
    rows = jnp.concatenate(rows, axis=0)

    def spread(weight):
        ahead = jnp.where((here == 0) | (here == 3), 0, 1)
        prev = hop(part(weight, ahead, 0), "grp", 1)
        nxt = hop(part(weight, 1 - ahead, 0), "grp", -1)
        return part(weight, here // 2, 0), prev, nxt

    def pass_on(prev, nxt, flops):
        picked = choose((here % 2)[None], prev, nxt, flops)
        far = lax.ppermute(picked, ("ep", "grp"), by_core([(0, 1), (1, 0), (2, 3), (3, 2)]))
        return far

    up_own, up_prev, up_next = spread(w_up[0])
    up_prev, up_next, down = lax.optimization_barrier((up_prev, up_next, w_down[0]))
    up_far = pass_on(up_prev, up_next, 10_000_000_000)
    down_own, down_prev, down_next = spread(down)
    down_far = pass_on(down_prev, down_next, 0)
    up_all = [up_own, up_next, up_far, up_prev]
    down_all = [down_own, down_next, down_far, down_prev]

    rank = 2 * capacity
    lanes_all = ep_size * rank
    flat_ids = jnp.concatenate(id_list, axis=0).reshape(-1)
    entries = flat_ids.shape[0]
    hits = flat_ids[:, None] == jnp.arange(ep_size, dtype=jnp.int32)[None, :]
    order = jnp.arange(entries, dtype=jnp.int32)
    per = samples * picks
    lower = (order[None, :] < order[:, None]) & (order[None, :] // per == order[:, None] // per)
    ahead = jnp.dot(
        lower.astype(jnp.bfloat16), hits.astype(jnp.bfloat16), preferred_element_type=jnp.float32
    )
    earlier = jnp.sum(jnp.where(hits, ahead, 0.0), axis=1).astype(jnp.int32)
    place = (flat_ids * rank + earlier).reshape(3, samples, picks)
    own_at, first_at, second_at = place[0], place[1], place[2]
    even = (expert_ids % 2) == 0
    place = jnp.concatenate(
        [
            jnp.where(even, own_at + side[0] * capacity, -1),
            jnp.where((id_list[1] % 2) == 0, first_at + (1 - side[0]) * capacity, -1),
            jnp.where(even, -1, own_at + side[1] * capacity),
            jnp.where((id_list[2] % 2) == 0, -1, second_at + (1 - side[1]) * capacity),
        ],
        axis=0,
    )
    match = place[:, :, None] == jnp.arange(lanes_all, dtype=jnp.int32)[None, None, :]
    placing = jnp.sum(match.astype(jnp.float32), axis=1).astype(jnp.bfloat16)
    outgoing = lax.dot_general(
        placing, rows, (((0,), (0,)), ((), ())), preferred_element_type=jnp.float32
    ).astype(jnp.bfloat16)
    arrived = lax.all_to_all(
        outgoing.reshape(ep_size, rank, half), "ep", split_axis=0, concat_axis=0, tiled=True
    ).reshape(lanes_all, half)

    moved_slot = mig_slot[0, 0]
    moved_target = mig_dest[0, 0]
    query_second, kv_second = after(outgoing, query_second, kv_second)
    q_here = lax.dynamic_index_in_dim(query_second, moved_slot, 0, keepdims=False)
    kv_here = lax.dynamic_index_in_dim(kv_second, moved_slot, 0, keepdims=True)
    packet = jnp.concatenate(
        [q_here, kv_here, jnp.zeros((15, q_here.shape[1]), jnp.bfloat16)], axis=0
    )
    offset = (moved_target - me) % grp_size
    got = packet
    for r in steps[1:]:
        got = jnp.where(offset == r, hop(packet, "grp", -r), got)
    heads = q_here.shape[0]
    q_in, kv_in = got[:heads], got[heads : heads + 1]

    lens = cache_len[0]
    pages = page_table(lens, page_perm[0], cache_pool.shape[1], cache_pool.shape[0])
    attn_first, attn_second, out_moved = attention(
        lens,
        pages,
        moved_slot[None],
        query_first,
        query_second,
        q_in,
        kv_first[:, None, :],
        kv_second[:, None, :],
        kv_in,
        cache_pool,
    )
    zero = jnp.zeros((), jnp.bfloat16)
    arrived_out = jnp.where(offset == 0, out_moved, zero)
    for r in steps[1:]:
        arrived_out = arrived_out + hop(jnp.where(offset == r, out_moved, zero), "grp", r)
    attn_second = lax.dynamic_update_index_in_dim(attn_second, arrived_out, moved_slot, 0)

    (arrived,) = after(down_far, arrived)
    mine, rounded = up_project(arrived, up_all, 2)
    theirs = lax.ppermute(rounded, ("ep", "grp"), by_core(PAIRS))
    shift = jnp.where(here % 2 == 1, grp_size - 1, 1).astype(jnp.int32)
    produced = down_project(shift[None], mine, theirs, down_all, 2)
    returned = lax.all_to_all(
        produced.reshape(ep_size, rank, half),
        "ep",
        split_axis=0,
        concat_axis=0,
        tiled=True,
    ).reshape(lanes_all, half)
    (late_gates,) = after(outgoing, gate_weights)
    gates = jnp.concatenate(
        [
            gate_weights,
            lax.ppermute(late_gates, "grp", partner[0]),
            gate_weights,
            lax.ppermute(late_gates, "grp", partner[1]),
        ],
        axis=0,
    )
    mixing = jnp.sum(jnp.where(match, gates[:, :, None], 0.0), axis=1)
    high = lax.reduce_precision(mixing, 8, 7)
    mixing = jnp.concatenate([high, mixing - high], axis=0).astype(jnp.bfloat16)
    mixed = jnp.dot(mixing, returned, preferred_element_type=jnp.float32)
    summed = (mixed[: 4 * samples] + mixed[4 * samples :]).reshape(4, samples, half)
    first, second = 0.0, 0.0
    for c in range(2):
        own = summed[2 * c]
        other = lax.ppermute(summed[2 * c + 1], "grp", partner[c])
        first = first + jnp.where(side[c] == 0, own, other)
        second = second + jnp.where(side[c] == 0, other, own)
    moe_out = jnp.concatenate([first, second], axis=1).astype(jnp.bfloat16)
    return (attn_first, attn_second, moe_out)


def solution(mesh):
    return jax.shard_map(
        shards,
        mesh=mesh,
        in_specs=(
            P(("ep", "grp"), None),
            P(("ep", "grp"), None),
            P(("ep", "grp"), None),
            P("ep", None, "grp"),
            P("ep", None, "grp"),
            P(("ep", "grp"), None, None),
            P(("ep", "grp"), None),
            P(("ep", "grp"), None, None),
            P(("ep", "grp"), None),
            P(("ep", "grp"), None, None),
            P(("ep", "grp"), None),
            P(("ep", "grp"), None),
            P("ep", "grp"),
            P("ep", "grp"),
        ),
        out_specs=(
            P(("ep", "grp"), None, None),
            P(("ep", "grp"), None, None),
            P(("ep", "grp"), None),
        ),
        check_vma=False,
    )
```

```python
import math

import jax
import jax.numpy as jnp
from jax import lax
from jax.experimental import pallas as pl
from jax.experimental.pallas import tpu as pltpu
from jax.sharding import PartitionSpec as P

LAT = 512
MAXP = 8
NEG = -1e30
PAIRS = ((1, 2), (2, 1), (3, 0), (0, 3))


def hop(value, axis, step):
    size = lax.axis_size(axis)
    return lax.ppermute(value, axis, [(i, (i + step) % size) for i in range(size)])


def after(first, *values):
    return lax.optimization_barrier((first,) + values)[1:]


def attention_kernel(
    lens, pages, moved, q_one, q_two, q_in, kv_one, kv_two, kv_in, pool, out_one, out_two, out_moved, acc
):
    slot = pl.program_id(0)
    heads = q_one.shape[1]
    rows = 2 * heads
    key_width = q_one.shape[2]
    page_rows = pool.shape[1]
    block = 2 * page_rows
    scale = 1.0 / math.sqrt(key_width / 3.0)
    is_moved = slot == moved[0]
    second = jnp.where(is_moved, q_in[...], q_two[0])
    queries = jnp.concatenate([q_one[0], second], axis=0)
    fresh_one = kv_one[0]
    fresh_two = jnp.where(is_moved, kv_in[...], kv_two[0])
    fresh = jnp.concatenate(
        [fresh_one, fresh_two, jnp.zeros((14, key_width), jnp.bfloat16)], axis=0
    )
    contract = (((1,), (1,)), ((), ()))
    scores = lax.dot_general(queries, fresh, contract, preferred_element_type=jnp.float32) * scale
    row = lax.broadcasted_iota(jnp.int32, scores.shape, 0)
    col = lax.broadcasted_iota(jnp.int32, scores.shape, 1)
    scores = jnp.where((col == 0) | ((col == 1) & (row >= heads)), scores, NEG)
    top = jnp.max(scores, axis=1, keepdims=True)
    weights = jnp.exp(scores - top)
    total = jnp.sum(weights, axis=1, keepdims=True)
    acc[...] = jnp.dot(
        weights.astype(jnp.bfloat16), fresh[:, :LAT], preferred_element_type=jnp.float32
    )
    live = lens[slot]

    def step(b, carry):
        top, total = carry
        keys = jnp.concatenate(
            [pool[pages[slot * MAXP + 2 * b]], pool[pages[slot * MAXP + 2 * b + 1]]], axis=0
        )
        scores = (
            lax.dot_general(queries, keys, contract, preferred_element_type=jnp.float32) * scale
        )
        col = lax.broadcasted_iota(jnp.int32, scores.shape, 1) + b * block
        scores = jnp.where(col < live, scores, NEG)
        new_top = jnp.maximum(top, jnp.max(scores, axis=1, keepdims=True))
        shrink = jnp.exp(top - new_top)
        weights = jnp.exp(scores - new_top)
        total = total * shrink + jnp.sum(weights, axis=1, keepdims=True)
        acc[...] = acc[...] * shrink + jnp.dot(
            weights.astype(jnp.bfloat16), keys[:, :LAT], preferred_element_type=jnp.float32
        )
        return new_top, total

    top, total = lax.fori_loop(0, (live + block - 1) // block, step, (top, total))
    result = (acc[...] / total).astype(jnp.bfloat16)
    out_one[0] = result[:heads]
    out_two[0] = result[heads:]

    @pl.when(is_moved)
    def _():
        out_moved[...] = result[heads:]


def attention(lens, pages, moved, q_one, q_two, q_in, kv_one, kv_two, kv_in, pool):
    samples, heads, key_width = q_one.shape
    one = lambda *shape: pl.BlockSpec((1,) + shape, lambda i, *_: (i,) + (0,) * len(shape))
    whole = lambda *shape: pl.BlockSpec(shape, lambda i, *_: (0,) * len(shape))
    return pl.pallas_call(
        attention_kernel,
        grid_spec=pltpu.PrefetchScalarGridSpec(
            num_scalar_prefetch=3,
            grid=(samples,),
            in_specs=[
                one(heads, key_width),
                one(heads, key_width),
                whole(heads, key_width),
                one(1, key_width),
                one(1, key_width),
                whole(1, key_width),
                whole(*pool.shape),
            ],
            out_specs=[one(heads, LAT), one(heads, LAT), whole(heads, LAT)],
            scratch_shapes=[pltpu.VMEM((2 * heads, LAT), jnp.float32)],
        ),
        out_shape=[
            jax.ShapeDtypeStruct((samples, heads, LAT), jnp.bfloat16),
            jax.ShapeDtypeStruct((samples, heads, LAT), jnp.bfloat16),
            jax.ShapeDtypeStruct((heads, LAT), jnp.bfloat16),
        ],
        compiler_params=pltpu.CompilerParams(vmem_limit_bytes=24 * 1024 * 1024),
        cost_estimate=pl.CostEstimate(
            flops=12_000_000_000, bytes_accessed=8_000_000, transcendentals=1_000_000
        ),
        name="attention",
    )(lens, pages, moved, q_one, q_two, q_in, kv_one, kv_two, kv_in, pool)


def choose_kernel(which, first, second, out):
    @pl.when(which[0] == 0)
    def _():
        out[...] = first[...]

    @pl.when(which[0] != 0)
    def _():
        out[...] = second[...]


def choose(which, first, second, flops):
    steps = 4
    block = pl.BlockSpec((first.shape[0] // steps, first.shape[1]), lambda k, *_: (k, 0))
    return pl.pallas_call(
        choose_kernel,
        grid_spec=pltpu.PrefetchScalarGridSpec(
            num_scalar_prefetch=1, grid=(steps,), in_specs=[block, block], out_specs=block
        ),
        out_shape=jax.ShapeDtypeStruct(first.shape, first.dtype),
        cost_estimate=pl.CostEstimate(
            flops=flops, bytes_accessed=3 * first.size * 2, transcendentals=0
        ),
        name="choose",
    )(which, first, second)


def up_kernel(rows, *refs):
    weights, (whole, sent) = refs[:4], refs[4:]
    for i, weight in enumerate(weights):
        part = jnp.dot(rows[...], weight[...], preferred_element_type=jnp.float32)
        whole[i] = part
        sent[i] = part.astype(jnp.bfloat16)


def up_project(rows, weights, steps):
    count, depth = rows.shape
    units = weights[0].shape[1]
    shape = (len(weights), count, units)
    out = pl.BlockSpec((len(weights), count // steps, units), lambda k: (0, k, 0))
    return pl.pallas_call(
        up_kernel,
        grid=(steps,),
        in_specs=[pl.BlockSpec((count // steps, depth), lambda k: (k, 0))]
        + [pl.BlockSpec((depth, units), lambda k: (0, 0))] * len(weights),
        out_specs=[out, out],
        out_shape=[
            jax.ShapeDtypeStruct(shape, jnp.float32),
            jax.ShapeDtypeStruct(shape, jnp.bfloat16),
        ],
        compiler_params=pltpu.CompilerParams(vmem_limit_bytes=58 * 1024 * 1024),
        cost_estimate=pl.CostEstimate(
            flops=2 * len(weights) * count * depth * units,
            bytes_accessed=9_000_000,
            transcendentals=0,
        ),
        name="up_project",
    )(rows, *weights)


def down_kernel(shift, mine, theirs, *refs):
    weights, out, held = refs[:4], refs[4], refs[5]

    @pl.when(pl.program_id(0) == 0)
    def _():
        for i in range(len(weights)):
            other = theirs[lax.rem(i + shift[0], len(weights))].astype(jnp.float32)
            value = mine[i] + other
            held[i] = (value / (1.0 + jnp.exp(-value))).astype(jnp.bfloat16)

    total = None
    for i, weight in enumerate(weights):
        part = lax.dot_general(
            held[i], weight[...], (((1,), (1,)), ((), ())), preferred_element_type=jnp.float32
        )
        total = part if total is None else total + part
    out[...] = total.astype(jnp.bfloat16)


def down_project(shift, mine, theirs, weights, steps):
    count, units = mine.shape[1:]
    depth = weights[0].shape[0]
    whole = pl.BlockSpec(mine.shape, lambda k, *_: (0, 0, 0))
    return pl.pallas_call(
        down_kernel,
        grid_spec=pltpu.PrefetchScalarGridSpec(
            num_scalar_prefetch=1,
            grid=(steps,),
            in_specs=[whole, whole]
            + [pl.BlockSpec((depth // steps, units), lambda k, *_: (k, 0))] * len(weights),
            out_specs=pl.BlockSpec((count, depth // steps), lambda k, *_: (0, k)),
            scratch_shapes=[pltpu.VMEM(mine.shape, jnp.bfloat16)],
        ),
        out_shape=jax.ShapeDtypeStruct((count, depth), jnp.bfloat16),
        compiler_params=pltpu.CompilerParams(vmem_limit_bytes=24 * 1024 * 1024),
        cost_estimate=pl.CostEstimate(
            flops=2 * len(weights) * count * depth * units,
            bytes_accessed=9_000_000,
            transcendentals=mine.size,
        ),
        name="down_project",
    )(shift, mine, theirs, *weights)


def page_table(cache_len, page_perm, page_rows, pool_pages):
    used = (cache_len + page_rows - 1) // page_rows
    slots = used.shape[0]
    before = jnp.arange(slots)[None, :] < jnp.arange(slots)[:, None]
    offset = jnp.sum(jnp.where(before, used[None, :], 0), axis=1)
    place = jnp.minimum(
        offset[:, None] + jnp.arange(MAXP, dtype=jnp.int32)[None, :], pool_pages - 1
    ).reshape(-1)
    hit = place[:, None] == jnp.arange(pool_pages, dtype=jnp.int32)[None, :]
    return jnp.sum(jnp.where(hit, page_perm[None, :], 0), axis=1)


def shards(
    hidden,
    expert_ids,
    gate_weights,
    w_up,
    w_down,
    query_first,
    kv_first,
    query_second,
    kv_second,
    cache_pool,
    cache_len,
    page_perm,
    mig_slot,
    mig_dest,
):
    samples, picks = expert_ids.shape
    width = hidden.shape[1]
    ep_size = lax.axis_size("ep")
    grp_size = lax.axis_size("grp")
    capacity = min(samples, max(2, 2 * samples * picks // ep_size))
    me = lax.axis_index("grp")
    steps = range(grp_size)

    half = width // 2
    core = lax.axis_index("ep") % 2
    turned = [(me - c) % grp_size for c in range(2)]
    side = [turned[c] // 2 for c in range(2)]
    here = jnp.where(core == 0, turned[0], turned[1])
    partner = [[((a + c) % grp_size, (b + c) % grp_size) for a, b in PAIRS] for c in range(2)]

    def by_core(pairs):
        return [
            (e * grp_size + (a + e % 2) % grp_size, e * grp_size + (b + e % 2) % grp_size)
            for e in range(ep_size)
            for a, b in pairs
        ]

    def part(value, which, axis):
        return lax.dynamic_slice_in_dim(value, which * half, half, axis)

    rows, id_list = [], [expert_ids]
    for c in range(2):
        id_list.append(lax.ppermute(expert_ids, "grp", partner[c]))
        rows.append(part(hidden, side[c], 1))
        rows.append(lax.ppermute(part(hidden, 1 - side[c], 1), "grp", partner[c]))
    rows = jnp.concatenate(rows, axis=0)

    ahead = jnp.where((here == 0) | (here == 3), 0, 1)

    def spread(weight, *first):
        to_next, to_prev = after(first, part(weight, ahead, 0), part(weight, 1 - ahead, 0))
        return part(weight, here // 2, 0), hop(to_next, "grp", 1), hop(to_prev, "grp", -1)

    def pass_on(prev, nxt, flops):
        picked = choose((here % 2)[None], prev, nxt, flops)
        far = lax.ppermute(picked, ("ep", "grp"), by_core([(0, 1), (1, 0), (2, 3), (3, 2)]))
        return far

    up_own, up_prev, up_next = spread(w_up[0], rows)
    up_far = pass_on(up_prev, up_next, 200_000_000_000)
    down_own, down_prev, down_next = spread(w_down[0], up_prev, up_next)
    down_far = pass_on(down_prev, down_next, 0)
    up_all = [up_own, up_next, up_far, up_prev]
    down_all = [down_own, down_next, down_far, down_prev]

    rank = 2 * capacity
    lanes_all = ep_size * rank
    flat_ids = jnp.concatenate(id_list, axis=0).reshape(-1)
    entries = flat_ids.shape[0]
    hits = flat_ids[:, None] == jnp.arange(ep_size, dtype=jnp.int32)[None, :]
    order = jnp.arange(entries, dtype=jnp.int32)
    per = samples * picks
    lower = (order[None, :] < order[:, None]) & (order[None, :] // per == order[:, None] // per)
    ahead = jnp.dot(
        lower.astype(jnp.bfloat16), hits.astype(jnp.bfloat16), preferred_element_type=jnp.float32
    )
    earlier = jnp.sum(jnp.where(hits, ahead, 0.0), axis=1).astype(jnp.int32)
    place = (flat_ids * rank + earlier).reshape(3, samples, picks)
    own_at, first_at, second_at = place[0], place[1], place[2]
    even = (expert_ids % 2) == 0
    place = jnp.concatenate(
        [
            jnp.where(even, own_at + side[0] * capacity, -1),
            jnp.where((id_list[1] % 2) == 0, first_at + (1 - side[0]) * capacity, -1),
            jnp.where(even, -1, own_at + side[1] * capacity),
            jnp.where((id_list[2] % 2) == 0, -1, second_at + (1 - side[1]) * capacity),
        ],
        axis=0,
    )
    match = place[:, :, None] == jnp.arange(lanes_all, dtype=jnp.int32)[None, None, :]
    placing = jnp.sum(match.astype(jnp.float32), axis=1).astype(jnp.bfloat16)
    outgoing = lax.dot_general(
        placing, rows, (((0,), (0,)), ((), ())), preferred_element_type=jnp.float32
    ).astype(jnp.bfloat16)
    arrived = lax.all_to_all(
        outgoing.reshape(ep_size, rank, half), "ep", split_axis=0, concat_axis=0, tiled=True
    ).reshape(lanes_all, half)

    moved_slot = mig_slot[0, 0]
    moved_target = mig_dest[0, 0]
    query_second, kv_second = after(outgoing, query_second, kv_second)
    q_here = lax.dynamic_index_in_dim(query_second, moved_slot, 0, keepdims=False)
    kv_here = lax.dynamic_index_in_dim(kv_second, moved_slot, 0, keepdims=True)
    packet = jnp.concatenate(
        [q_here, kv_here, jnp.zeros((15, q_here.shape[1]), jnp.bfloat16)], axis=0
    )
    offset = (moved_target - me) % grp_size
    got = packet
    for r in steps[1:]:
        got = jnp.where(offset == r, hop(packet, "grp", -r), got)
    heads = q_here.shape[0]
    q_in, kv_in = got[:heads], got[heads : heads + 1]

    lens = cache_len[0]
    pages = page_table(lens, page_perm[0], cache_pool.shape[1], cache_pool.shape[0])
    attn_first, attn_second, out_moved = attention(
        lens,
        pages,
        moved_slot[None],
        query_first,
        query_second,
        q_in,
        kv_first[:, None, :],
        kv_second[:, None, :],
        kv_in,
        cache_pool,
    )
    zero = jnp.zeros((), jnp.bfloat16)
    arrived_out = jnp.where(offset == 0, out_moved, zero)
    for r in steps[1:]:
        arrived_out = arrived_out + hop(jnp.where(offset == r, out_moved, zero), "grp", r)
    attn_second = lax.dynamic_update_index_in_dim(attn_second, arrived_out, moved_slot, 0)

    mine, rounded = up_project(arrived, up_all, 2)
    (rounded,) = after(down_far, rounded)
    theirs = lax.ppermute(rounded, ("ep", "grp"), by_core(PAIRS))
    shift = jnp.where(here % 2 == 1, grp_size - 1, 1).astype(jnp.int32)
    produced = down_project(shift[None], mine, theirs, down_all, 2)
    returned = lax.all_to_all(
        produced.reshape(ep_size, rank, half),
        "ep",
        split_axis=0,
        concat_axis=0,
        tiled=True,
    ).reshape(lanes_all, half)
    (late_gates,) = after(outgoing, gate_weights)
    gates = jnp.concatenate(
        [
            gate_weights,
            lax.ppermute(late_gates, "grp", partner[0]),
            gate_weights,
            lax.ppermute(late_gates, "grp", partner[1]),
        ],
        axis=0,
    )
    mixing = jnp.sum(jnp.where(match, gates[:, :, None], 0.0), axis=1)
    high = lax.reduce_precision(mixing, 8, 7)
    mixing = jnp.concatenate([high, mixing - high], axis=0).astype(jnp.bfloat16)
    mixed = jnp.dot(mixing, returned, preferred_element_type=jnp.float32)
    summed = (mixed[: 4 * samples] + mixed[4 * samples :]).reshape(4, samples, half)
    first, second = 0.0, 0.0
    for c in range(2):
        own = summed[2 * c]
        other = lax.ppermute(summed[2 * c + 1], "grp", partner[c])
        first = first + jnp.where(side[c] == 0, own, other)
        second = second + jnp.where(side[c] == 0, other, own)
    moe_out = jnp.concatenate([first, second], axis=1).astype(jnp.bfloat16)
    return (attn_first, attn_second, moe_out)


def solution(mesh):
    return jax.shard_map(
        shards,
        mesh=mesh,
        in_specs=(
            P(("ep", "grp"), None),
            P(("ep", "grp"), None),
            P(("ep", "grp"), None),
            P("ep", None, "grp"),
            P("ep", None, "grp"),
            P(("ep", "grp"), None, None),
            P(("ep", "grp"), None),
            P(("ep", "grp"), None, None),
            P(("ep", "grp"), None),
            P(("ep", "grp"), None, None),
            P(("ep", "grp"), None),
            P(("ep", "grp"), None),
            P("ep", "grp"),
            P("ep", "grp"),
        ),
        out_specs=(
            P(("ep", "grp"), None, None),
            P(("ep", "grp"), None, None),
            P(("ep", "grp"), None),
        ),
        check_vma=False,
    )
```

```python
import math

import jax
import jax.numpy as jnp
from jax import lax
from jax.experimental import pallas as pl
from jax.experimental.pallas import tpu as pltpu
from jax.sharding import PartitionSpec as P

LAT = 512
MAXP = 8
NEG = -1e30
PAIRS = ((1, 2), (2, 1), (3, 0), (0, 3))


def hop(value, axis, step):
    size = lax.axis_size(axis)
    return lax.ppermute(value, axis, [(i, (i + step) % size) for i in range(size)])


def after(first, *values):
    return lax.optimization_barrier((first,) + values)[1:]


def attention_kernel(
    lens, pages, moved, q_one, q_two, q_in, kv_one, kv_two, kv_in, pool, out_one, out_two, out_moved, acc
):
    slot = pl.program_id(0)
    heads = q_one.shape[1]
    rows = 2 * heads
    key_width = q_one.shape[2]
    page_rows = pool.shape[1]
    block = 2 * page_rows
    scale = 1.0 / math.sqrt(key_width / 3.0)
    is_moved = slot == moved[0]
    second = jnp.where(is_moved, q_in[...], q_two[0])
    queries = jnp.concatenate([q_one[0], second], axis=0)
    fresh_one = kv_one[0]
    fresh_two = jnp.where(is_moved, kv_in[...], kv_two[0])
    fresh = jnp.concatenate(
        [fresh_one, fresh_two, jnp.zeros((14, key_width), jnp.bfloat16)], axis=0
    )
    contract = (((1,), (1,)), ((), ()))
    scores = lax.dot_general(queries, fresh, contract, preferred_element_type=jnp.float32) * scale
    row = lax.broadcasted_iota(jnp.int32, scores.shape, 0)
    col = lax.broadcasted_iota(jnp.int32, scores.shape, 1)
    scores = jnp.where((col == 0) | ((col == 1) & (row >= heads)), scores, NEG)
    top = jnp.max(scores, axis=1, keepdims=True)
    weights = jnp.exp(scores - top)
    total = jnp.sum(weights, axis=1, keepdims=True)
    acc[...] = jnp.dot(
        weights.astype(jnp.bfloat16), fresh[:, :LAT], preferred_element_type=jnp.float32
    )
    live = lens[slot]

    def step(b, carry):
        top, total = carry
        keys = jnp.concatenate(
            [pool[pages[slot * MAXP + 2 * b]], pool[pages[slot * MAXP + 2 * b + 1]]], axis=0
        )
        scores = (
            lax.dot_general(queries, keys, contract, preferred_element_type=jnp.float32) * scale
        )
        col = lax.broadcasted_iota(jnp.int32, scores.shape, 1) + b * block
        scores = jnp.where(col < live, scores, NEG)
        new_top = jnp.maximum(top, jnp.max(scores, axis=1, keepdims=True))
        shrink = jnp.exp(top - new_top)
        weights = jnp.exp(scores - new_top)
        total = total * shrink + jnp.sum(weights, axis=1, keepdims=True)
        acc[...] = acc[...] * shrink + jnp.dot(
            weights.astype(jnp.bfloat16), keys[:, :LAT], preferred_element_type=jnp.float32
        )
        return new_top, total

    top, total = lax.fori_loop(0, (live + block - 1) // block, step, (top, total))
    result = (acc[...] / total).astype(jnp.bfloat16)
    out_one[0] = result[:heads]
    out_two[0] = result[heads:]

    @pl.when(is_moved)
    def _():
        out_moved[...] = result[heads:]


def attention(lens, pages, moved, q_one, q_two, q_in, kv_one, kv_two, kv_in, pool):
    samples, heads, key_width = q_one.shape
    one = lambda *shape: pl.BlockSpec((1,) + shape, lambda i, *_: (i,) + (0,) * len(shape))
    whole = lambda *shape: pl.BlockSpec(shape, lambda i, *_: (0,) * len(shape))
    return pl.pallas_call(
        attention_kernel,
        grid_spec=pltpu.PrefetchScalarGridSpec(
            num_scalar_prefetch=3,
            grid=(samples,),
            in_specs=[
                one(heads, key_width),
                one(heads, key_width),
                whole(heads, key_width),
                one(1, key_width),
                one(1, key_width),
                whole(1, key_width),
                whole(*pool.shape),
            ],
            out_specs=[one(heads, LAT), one(heads, LAT), whole(heads, LAT)],
            scratch_shapes=[pltpu.VMEM((2 * heads, LAT), jnp.float32)],
        ),
        out_shape=[
            jax.ShapeDtypeStruct((samples, heads, LAT), jnp.bfloat16),
            jax.ShapeDtypeStruct((samples, heads, LAT), jnp.bfloat16),
            jax.ShapeDtypeStruct((heads, LAT), jnp.bfloat16),
        ],
        compiler_params=pltpu.CompilerParams(vmem_limit_bytes=24 * 1024 * 1024),
        cost_estimate=pl.CostEstimate(
            flops=12_000_000_000, bytes_accessed=8_000_000, transcendentals=1_000_000
        ),
        name="attention",
    )(lens, pages, moved, q_one, q_two, q_in, kv_one, kv_two, kv_in, pool)


def choose_kernel(which, first, second, out):
    @pl.when(which[0] == 0)
    def _():
        out[...] = first[...]

    @pl.when(which[0] != 0)
    def _():
        out[...] = second[...]


def choose(which, first, second, flops):
    steps = 4
    block = pl.BlockSpec((first.shape[0] // steps, first.shape[1]), lambda k, *_: (k, 0))
    return pl.pallas_call(
        choose_kernel,
        grid_spec=pltpu.PrefetchScalarGridSpec(
            num_scalar_prefetch=1, grid=(steps,), in_specs=[block, block], out_specs=block
        ),
        out_shape=jax.ShapeDtypeStruct(first.shape, first.dtype),
        cost_estimate=pl.CostEstimate(
            flops=flops, bytes_accessed=3 * first.size * 2, transcendentals=0
        ),
        name="choose",
    )(which, first, second)


def up_kernel(rows, *refs):
    weights, (whole, sent) = refs[:4], refs[4:]
    for i, weight in enumerate(weights):
        part = jnp.dot(rows[...], weight[...], preferred_element_type=jnp.float32)
        whole[i] = part
        sent[i] = part.astype(jnp.bfloat16)


def up_project(rows, weights, steps):
    count, depth = rows.shape
    units = weights[0].shape[1]
    shape = (len(weights), count, units)
    out = pl.BlockSpec((len(weights), count // steps, units), lambda k: (0, k, 0))
    return pl.pallas_call(
        up_kernel,
        grid=(steps,),
        in_specs=[pl.BlockSpec((count // steps, depth), lambda k: (k, 0))]
        + [pl.BlockSpec((depth, units), lambda k: (0, 0))] * len(weights),
        out_specs=[out, out],
        out_shape=[
            jax.ShapeDtypeStruct(shape, jnp.float32),
            jax.ShapeDtypeStruct(shape, jnp.bfloat16),
        ],
        compiler_params=pltpu.CompilerParams(vmem_limit_bytes=58 * 1024 * 1024),
        cost_estimate=pl.CostEstimate(
            flops=2 * len(weights) * count * depth * units,
            bytes_accessed=9_000_000,
            transcendentals=0,
        ),
        name="up_project",
    )(rows, *weights)


def down_kernel(shift, mine, theirs, *refs):
    weights, out, held = refs[:4], refs[4], refs[5]

    @pl.when(pl.program_id(0) == 0)
    def _():
        for i in range(len(weights)):
            other = theirs[lax.rem(i + shift[0], len(weights))].astype(jnp.float32)
            value = mine[i] + other
            held[i] = (value / (1.0 + jnp.exp(-value))).astype(jnp.bfloat16)

    total = None
    for i, weight in enumerate(weights):
        part = lax.dot_general(
            held[i], weight[...], (((1,), (1,)), ((), ())), preferred_element_type=jnp.float32
        )
        total = part if total is None else total + part
    out[...] = total.astype(jnp.bfloat16)


def down_project(shift, mine, theirs, weights, steps):
    count, units = mine.shape[1:]
    depth = weights[0].shape[0]
    whole = pl.BlockSpec(mine.shape, lambda k, *_: (0, 0, 0))
    return pl.pallas_call(
        down_kernel,
        grid_spec=pltpu.PrefetchScalarGridSpec(
            num_scalar_prefetch=1,
            grid=(steps,),
            in_specs=[whole, whole]
            + [pl.BlockSpec((depth // steps, units), lambda k, *_: (k, 0))] * len(weights),
            out_specs=pl.BlockSpec((count, depth // steps), lambda k, *_: (0, k)),
            scratch_shapes=[pltpu.VMEM(mine.shape, jnp.bfloat16)],
        ),
        out_shape=jax.ShapeDtypeStruct((count, depth), jnp.bfloat16),
        compiler_params=pltpu.CompilerParams(vmem_limit_bytes=24 * 1024 * 1024),
        cost_estimate=pl.CostEstimate(
            flops=2 * len(weights) * count * depth * units,
            bytes_accessed=9_000_000,
            transcendentals=mine.size,
        ),
        name="down_project",
    )(shift, mine, theirs, *weights)


def page_table(cache_len, page_perm, page_rows, pool_pages):
    used = (cache_len + page_rows - 1) // page_rows
    slots = used.shape[0]
    before = jnp.arange(slots)[None, :] < jnp.arange(slots)[:, None]
    offset = jnp.sum(jnp.where(before, used[None, :], 0), axis=1)
    place = jnp.minimum(
        offset[:, None] + jnp.arange(MAXP, dtype=jnp.int32)[None, :], pool_pages - 1
    ).reshape(-1)
    hit = place[:, None] == jnp.arange(pool_pages, dtype=jnp.int32)[None, :]
    return jnp.sum(jnp.where(hit, page_perm[None, :], 0), axis=1)


def shards(
    hidden,
    expert_ids,
    gate_weights,
    w_up,
    w_down,
    query_first,
    kv_first,
    query_second,
    kv_second,
    cache_pool,
    cache_len,
    page_perm,
    mig_slot,
    mig_dest,
):
    samples, picks = expert_ids.shape
    width = hidden.shape[1]
    ep_size = lax.axis_size("ep")
    grp_size = lax.axis_size("grp")
    capacity = min(samples, max(2, 2 * samples * picks // ep_size))
    me = lax.axis_index("grp")
    steps = range(grp_size)

    half = width // 2
    core = lax.axis_index("ep") % 2
    cores = (core, 1 - core)
    turned = [(me - c) % grp_size for c in cores]
    side = [t // 2 for t in turned]
    here = turned[0]

    def by_core(pairs, flip=0):
        return [
            (e * grp_size + (a + (e + flip) % 2) % grp_size, e * grp_size + (b + (e + flip) % 2) % grp_size)
            for e in range(ep_size)
            for a, b in pairs
        ]

    def swap_planes(value, k):
        return lax.ppermute(value, ("ep", "grp"), by_core(PAIRS, k))

    def swap_cores(value):
        return lax.ppermute(value, "ep", [(e, e + 1 - 2 * (e % 2)) for e in range(ep_size)])

    def part(value, which, axis):
        return lax.dynamic_slice_in_dim(value, which * half, half, axis)

    rows, id_list = [], [expert_ids]
    for k in range(2):
        id_list.append(swap_planes(expert_ids, k))
        theirs = swap_planes(part(hidden, 1 - side[k], 1), k)
        rows.append(jnp.concatenate([part(hidden, side[k], 1), theirs], axis=0))

    ahead = jnp.where((here == 0) | (here == 3), 0, 1)

    def spread(weight, *first):
        to_next, to_prev = after(first, part(weight, ahead, 0), part(weight, 1 - ahead, 0))
        return part(weight, here // 2, 0), hop(to_next, "grp", 1), hop(to_prev, "grp", -1)

    def pass_on(prev, nxt, flops):
        picked = choose((here % 2)[None], prev, nxt, flops)
        return lax.ppermute(picked, ("ep", "grp"), by_core([(0, 1), (1, 0), (2, 3), (3, 2)]))

    up_own, up_prev, up_next = spread(w_up[0], *rows)
    up_far = pass_on(up_prev, up_next, 200_000_000_000)
    down_own, down_prev, down_next = spread(w_down[0], up_prev, up_next)
    down_far = pass_on(down_prev, down_next, 200_000_000_000)
    up_all = [up_own, up_next, up_far, up_prev]
    down_all = [down_own, down_next, down_far, down_prev]

    rank = 2 * capacity
    peers = ep_size // 2
    lanes = peers * rank
    flat_ids = jnp.concatenate(id_list, axis=0).reshape(-1)
    entries = flat_ids.shape[0]
    hits = flat_ids[:, None] == jnp.arange(ep_size, dtype=jnp.int32)[None, :]
    order = jnp.arange(entries, dtype=jnp.int32)
    per = samples * picks
    lower = (order[None, :] < order[:, None]) & (order[None, :] // per == order[:, None] // per)
    ahead = jnp.dot(
        lower.astype(jnp.bfloat16), hits.astype(jnp.bfloat16), preferred_element_type=jnp.float32
    )
    earlier = jnp.sum(jnp.where(hits, ahead, 0.0), axis=1).astype(jnp.int32)
    place = ((flat_ids // 2) * rank + earlier).reshape(3, samples, picks)
    groups = [[2 * j + c for j in range(peers)] for c in range(2)]

    def exchange(value):
        return lax.all_to_all(
            value.reshape(peers, rank, half),
            "ep",
            split_axis=0,
            concat_axis=0,
            axis_index_groups=groups,
            tiled=True,
        ).reshape(lanes, half)

    match, arrived = [], []
    for k in range(2):
        at = jnp.concatenate(
            [
                jnp.where(expert_ids % 2 == cores[k], place[0] + side[k] * capacity, -1),
                jnp.where(
                    id_list[k + 1] % 2 == cores[k], place[k + 1] + (1 - side[k]) * capacity, -1
                ),
            ],
            axis=0,
        )
        match.append(at[:, :, None] == jnp.arange(lanes, dtype=jnp.int32)[None, None, :])
        placing = jnp.sum(match[k].astype(jnp.float32), axis=1).astype(jnp.bfloat16)
        outgoing = lax.dot_general(
            placing, rows[k], (((0,), (0,)), ((), ())), preferred_element_type=jnp.float32
        ).astype(jnp.bfloat16)
        arrived.append(exchange(outgoing if k == 0 else swap_cores(outgoing)))

    moved_slot = mig_slot[0, 0]
    moved_target = mig_dest[0, 0]
    query_second, kv_second = after(outgoing, query_second, kv_second)
    q_here = lax.dynamic_index_in_dim(query_second, moved_slot, 0, keepdims=False)
    kv_here = lax.dynamic_index_in_dim(kv_second, moved_slot, 0, keepdims=True)
    packet = jnp.concatenate(
        [q_here, kv_here, jnp.zeros((15, q_here.shape[1]), jnp.bfloat16)], axis=0
    )
    offset = (moved_target - me) % grp_size
    got = packet
    for r in steps[1:]:
        got = jnp.where(offset == r, hop(packet, "grp", -r), got)
    heads = q_here.shape[0]
    q_in, kv_in = got[:heads], got[heads : heads + 1]

    lens = cache_len[0]
    pages = page_table(lens, page_perm[0], cache_pool.shape[1], cache_pool.shape[0])
    attn_first, attn_second, out_moved = attention(
        lens,
        pages,
        moved_slot[None],
        query_first,
        query_second,
        q_in,
        kv_first[:, None, :],
        kv_second[:, None, :],
        kv_in,
        cache_pool,
    )
    zero = jnp.zeros((), jnp.bfloat16)
    arrived_out = jnp.where(offset == 0, out_moved, zero)
    for r in steps[1:]:
        arrived_out = arrived_out + hop(jnp.where(offset == r, out_moved, zero), "grp", r)
    attn_second = lax.dynamic_update_index_in_dim(attn_second, arrived_out, moved_slot, 0)

    shift = jnp.where(here % 2 == 1, grp_size - 1, 1).astype(jnp.int32)
    (late_gates,) = after(outgoing, gate_weights)
    first, second = 0.0, 0.0
    for k in range(2):
        mine, rounded = up_project(arrived[k], up_all, 1)
        produced = down_project(shift[None], mine, swap_planes(rounded, 0), down_all, 2)
        returned = exchange(produced if k == 0 else swap_cores(produced))
        gates = jnp.concatenate([gate_weights, swap_planes(late_gates, k)], axis=0)
        mixing = jnp.sum(jnp.where(match[k], gates[:, :, None], 0.0), axis=1)
        high = lax.reduce_precision(mixing, 8, 7)
        mixing = jnp.concatenate([high, mixing - high], axis=0).astype(jnp.bfloat16)
        mixed = jnp.dot(mixing, returned, preferred_element_type=jnp.float32)
        summed = (mixed[: 2 * samples] + mixed[2 * samples :]).reshape(2, samples, half)
        own, other = summed[0], swap_planes(summed[1], k)
        first = first + jnp.where(side[k] == 0, own, other)
        second = second + jnp.where(side[k] == 0, other, own)
    moe_out = jnp.concatenate([first, second], axis=1).astype(jnp.bfloat16)
    return (attn_first, attn_second, moe_out)


def solution(mesh):
    return jax.shard_map(
        shards,
        mesh=mesh,
        in_specs=(
            P(("ep", "grp"), None),
            P(("ep", "grp"), None),
            P(("ep", "grp"), None),
            P("ep", None, "grp"),
            P("ep", None, "grp"),
            P(("ep", "grp"), None, None),
            P(("ep", "grp"), None),
            P(("ep", "grp"), None, None),
            P(("ep", "grp"), None),
            P(("ep", "grp"), None, None),
            P(("ep", "grp"), None),
            P(("ep", "grp"), None),
            P("ep", "grp"),
            P("ep", "grp"),
        ),
        out_specs=(
            P(("ep", "grp"), None, None),
            P(("ep", "grp"), None, None),
            P(("ep", "grp"), None),
        ),
        check_vma=False,
    )
```

```python
import math

import jax
import jax.numpy as jnp
from jax import lax
from jax.experimental import pallas as pl
from jax.experimental.pallas import tpu as pltpu
from jax.sharding import PartitionSpec as P

LAT = 512
MAXP = 8
NEG = -1e30
PAIRS = ((1, 2), (2, 1), (3, 0), (0, 3))


def hop(value, axis, step):
    size = lax.axis_size(axis)
    return lax.ppermute(value, axis, [(i, (i + step) % size) for i in range(size)])


def after(first, *values):
    return lax.optimization_barrier((first,) + values)[1:]


def attention_kernel(
    lens, pages, moved, q_one, q_two, q_in, kv_one, kv_two, kv_in, pool, out_one, out_two, out_moved, acc
):
    slot = pl.program_id(0)
    heads = q_one.shape[1]
    rows = 2 * heads
    key_width = q_one.shape[2]
    page_rows = pool.shape[1]
    block = 2 * page_rows
    scale = 1.0 / math.sqrt(key_width / 3.0)
    is_moved = slot == moved[0]
    second = jnp.where(is_moved, q_in[...], q_two[0])
    queries = jnp.concatenate([q_one[0], second], axis=0)
    fresh_one = kv_one[0]
    fresh_two = jnp.where(is_moved, kv_in[...], kv_two[0])
    fresh = jnp.concatenate(
        [fresh_one, fresh_two, jnp.zeros((14, key_width), jnp.bfloat16)], axis=0
    )
    contract = (((1,), (1,)), ((), ()))
    scores = lax.dot_general(queries, fresh, contract, preferred_element_type=jnp.float32) * scale
    row = lax.broadcasted_iota(jnp.int32, scores.shape, 0)
    col = lax.broadcasted_iota(jnp.int32, scores.shape, 1)
    scores = jnp.where((col == 0) | ((col == 1) & (row >= heads)), scores, NEG)
    top = jnp.max(scores, axis=1, keepdims=True)
    weights = jnp.exp(scores - top)
    total = jnp.sum(weights, axis=1, keepdims=True)
    acc[...] = jnp.dot(
        weights.astype(jnp.bfloat16), fresh[:, :LAT], preferred_element_type=jnp.float32
    )
    live = lens[slot]

    def step(b, carry):
        top, total = carry
        keys = jnp.concatenate(
            [pool[pages[slot * MAXP + 2 * b]], pool[pages[slot * MAXP + 2 * b + 1]]], axis=0
        )
        scores = (
            lax.dot_general(queries, keys, contract, preferred_element_type=jnp.float32) * scale
        )
        col = lax.broadcasted_iota(jnp.int32, scores.shape, 1) + b * block
        scores = jnp.where(col < live, scores, NEG)
        new_top = jnp.maximum(top, jnp.max(scores, axis=1, keepdims=True))
        shrink = jnp.exp(top - new_top)
        weights = jnp.exp(scores - new_top)
        total = total * shrink + jnp.sum(weights, axis=1, keepdims=True)
        acc[...] = acc[...] * shrink + jnp.dot(
            weights.astype(jnp.bfloat16), keys[:, :LAT], preferred_element_type=jnp.float32
        )
        return new_top, total

    top, total = lax.fori_loop(0, (live + block - 1) // block, step, (top, total))
    result = (acc[...] / total).astype(jnp.bfloat16)
    out_one[0] = result[:heads]
    out_two[0] = result[heads:]

    @pl.when(is_moved)
    def _():
        out_moved[...] = result[heads:]


def attention(lens, pages, moved, q_one, q_two, q_in, kv_one, kv_two, kv_in, pool):
    samples, heads, key_width = q_one.shape
    one = lambda *shape: pl.BlockSpec((1,) + shape, lambda i, *_: (i,) + (0,) * len(shape))
    whole = lambda *shape: pl.BlockSpec(shape, lambda i, *_: (0,) * len(shape))
    return pl.pallas_call(
        attention_kernel,
        grid_spec=pltpu.PrefetchScalarGridSpec(
            num_scalar_prefetch=3,
            grid=(samples,),
            in_specs=[
                one(heads, key_width),
                one(heads, key_width),
                whole(heads, key_width),
                one(1, key_width),
                one(1, key_width),
                whole(1, key_width),
                whole(*pool.shape),
            ],
            out_specs=[one(heads, LAT), one(heads, LAT), whole(heads, LAT)],
            scratch_shapes=[pltpu.VMEM((2 * heads, LAT), jnp.float32)],
        ),
        out_shape=[
            jax.ShapeDtypeStruct((samples, heads, LAT), jnp.bfloat16),
            jax.ShapeDtypeStruct((samples, heads, LAT), jnp.bfloat16),
            jax.ShapeDtypeStruct((heads, LAT), jnp.bfloat16),
        ],
        compiler_params=pltpu.CompilerParams(vmem_limit_bytes=24 * 1024 * 1024),
        cost_estimate=pl.CostEstimate(
            flops=12_000_000_000, bytes_accessed=8_000_000, transcendentals=1_000_000
        ),
        name="attention",
    )(lens, pages, moved, q_one, q_two, q_in, kv_one, kv_two, kv_in, pool)


def choose_kernel(which, first, second, out):
    @pl.when(which[0] == 0)
    def _():
        out[...] = first[...]

    @pl.when(which[0] != 0)
    def _():
        out[...] = second[...]


def choose(which, first, second, flops):
    steps = 4
    block = pl.BlockSpec((first.shape[0] // steps, first.shape[1]), lambda k, *_: (k, 0))
    return pl.pallas_call(
        choose_kernel,
        grid_spec=pltpu.PrefetchScalarGridSpec(
            num_scalar_prefetch=1, grid=(steps,), in_specs=[block, block], out_specs=block
        ),
        out_shape=jax.ShapeDtypeStruct(first.shape, first.dtype),
        cost_estimate=pl.CostEstimate(
            flops=flops, bytes_accessed=3 * first.size * 2, transcendentals=0
        ),
        name="choose",
    )(which, first, second)


def up_kernel(rows, *refs):
    weights, (whole, sent) = refs[:4], refs[4:]
    for i, weight in enumerate(weights):
        part = jnp.dot(rows[...], weight[...], preferred_element_type=jnp.float32)
        whole[i] = part
        sent[i] = part.astype(jnp.bfloat16)


def up_project(rows, weights, steps):
    count, depth = rows.shape
    units = weights[0].shape[1]
    shape = (len(weights), count, units)
    out = pl.BlockSpec((len(weights), count // steps, units), lambda k: (0, k, 0))
    return pl.pallas_call(
        up_kernel,
        grid=(steps,),
        in_specs=[pl.BlockSpec((count // steps, depth), lambda k: (k, 0))]
        + [pl.BlockSpec((depth, units), lambda k: (0, 0))] * len(weights),
        out_specs=[out, out],
        out_shape=[
            jax.ShapeDtypeStruct(shape, jnp.float32),
            jax.ShapeDtypeStruct(shape, jnp.bfloat16),
        ],
        compiler_params=pltpu.CompilerParams(vmem_limit_bytes=58 * 1024 * 1024),
        cost_estimate=pl.CostEstimate(
            flops=2 * len(weights) * count * depth * units,
            bytes_accessed=9_000_000,
            transcendentals=0,
        ),
        name="up_project",
    )(rows, *weights)


def down_kernel(shift, mine, theirs, *refs):
    weights, out, held = refs[:4], refs[4], refs[5]

    @pl.when(pl.program_id(0) == 0)
    def _():
        for i in range(len(weights)):
            other = theirs[lax.rem(i + shift[0], len(weights))].astype(jnp.float32)
            value = mine[i] + other
            held[i] = (value / (1.0 + jnp.exp(-value))).astype(jnp.bfloat16)

    total = None
    for i, weight in enumerate(weights):
        part = lax.dot_general(
            held[i], weight[...], (((1,), (1,)), ((), ())), preferred_element_type=jnp.float32
        )
        total = part if total is None else total + part
    out[...] = total.astype(jnp.bfloat16)


def down_project(shift, mine, theirs, weights, steps):
    count, units = mine.shape[1:]
    depth = weights[0].shape[0]
    whole = pl.BlockSpec(mine.shape, lambda k, *_: (0, 0, 0))
    return pl.pallas_call(
        down_kernel,
        grid_spec=pltpu.PrefetchScalarGridSpec(
            num_scalar_prefetch=1,
            grid=(steps,),
            in_specs=[whole, whole]
            + [pl.BlockSpec((depth // steps, units), lambda k, *_: (k, 0))] * len(weights),
            out_specs=pl.BlockSpec((count, depth // steps), lambda k, *_: (0, k)),
            scratch_shapes=[pltpu.VMEM(mine.shape, jnp.bfloat16)],
        ),
        out_shape=jax.ShapeDtypeStruct((count, depth), jnp.bfloat16),
        compiler_params=pltpu.CompilerParams(vmem_limit_bytes=24 * 1024 * 1024),
        cost_estimate=pl.CostEstimate(
            flops=2 * len(weights) * count * depth * units,
            bytes_accessed=9_000_000,
            transcendentals=mine.size,
        ),
        name="down_project",
    )(shift, mine, theirs, *weights)


def page_table(cache_len, page_perm, page_rows, pool_pages):
    used = (cache_len + page_rows - 1) // page_rows
    slots = used.shape[0]
    before = jnp.arange(slots)[None, :] < jnp.arange(slots)[:, None]
    offset = jnp.sum(jnp.where(before, used[None, :], 0), axis=1)
    place = jnp.minimum(
        offset[:, None] + jnp.arange(MAXP, dtype=jnp.int32)[None, :], pool_pages - 1
    ).reshape(-1)
    hit = place[:, None] == jnp.arange(pool_pages, dtype=jnp.int32)[None, :]
    return jnp.sum(jnp.where(hit, page_perm[None, :], 0), axis=1)


def shards(
    hidden,
    expert_ids,
    gate_weights,
    w_up,
    w_down,
    query_first,
    kv_first,
    query_second,
    kv_second,
    cache_pool,
    cache_len,
    page_perm,
    mig_slot,
    mig_dest,
):
    samples, picks = expert_ids.shape
    width = hidden.shape[1]
    ep_size = lax.axis_size("ep")
    grp_size = lax.axis_size("grp")
    capacity = min(samples, max(2, 2 * samples * picks // ep_size))
    me = lax.axis_index("grp")
    steps = range(grp_size)

    half = width // 2
    core = lax.axis_index("ep") % 2
    cores = (core, 1 - core)
    turned = [(me - c) % grp_size for c in cores]
    side = [t // 2 for t in turned]
    here = turned[0]

    def by_core(pairs, flip=0):
        return [
            (e * grp_size + (a + (e + flip) % 2) % grp_size, e * grp_size + (b + (e + flip) % 2) % grp_size)
            for e in range(ep_size)
            for a, b in pairs
        ]

    def swap_planes(value, k):
        return lax.ppermute(value, ("ep", "grp"), by_core(PAIRS, k))

    def swap_cores(value):
        return lax.ppermute(value, "ep", [(e, e + 1 - 2 * (e % 2)) for e in range(ep_size)])

    def part(value, which, axis):
        return lax.dynamic_slice_in_dim(value, which * half, half, axis)

    rows, id_list, gate_list = [], [expert_ids], [gate_weights]
    term = lax.reduce_precision(gate_weights, 8, 7)
    rest = gate_weights - term
    next_term = lax.reduce_precision(rest, 8, 7)
    small = jnp.concatenate(
        [expert_ids.astype(jnp.float32), term, next_term, rest - next_term], axis=1
    ).astype(jnp.bfloat16)
    small = jnp.pad(small, ((0, 0), (0, 128 - 4 * picks)))
    for k in range(2):
        sent = jnp.concatenate([part(hidden, 1 - side[k], 1), small], axis=1)
        theirs = swap_planes(sent, k)
        extra = theirs[:, half : half + 4 * picks].astype(jnp.float32).reshape(samples, 4, picks)
        id_list.append(extra[:, 0].astype(jnp.int32))
        gate_list.append((extra[:, 1] + extra[:, 2]) + extra[:, 3])
        rows.append(jnp.concatenate([part(hidden, side[k], 1), theirs[:, :half]], axis=0))

    ahead = jnp.where((here == 0) | (here == 3), 0, 1)

    def spread(weight, *first):
        to_next, to_prev = after(first, part(weight, ahead, 0), part(weight, 1 - ahead, 0))
        return part(weight, here // 2, 0), hop(to_next, "grp", 1), hop(to_prev, "grp", -1)

    def pass_on(prev, nxt, flops):
        picked = choose((here % 2)[None], prev, nxt, flops)
        return lax.ppermute(picked, ("ep", "grp"), by_core([(0, 1), (1, 0), (2, 3), (3, 2)]))

    up_own, up_prev, up_next = spread(w_up[0], *rows)
    up_far = pass_on(up_prev, up_next, 200_000_000_000)
    down_own, down_prev, down_next = spread(w_down[0], up_prev, up_next)
    down_far = pass_on(down_prev, down_next, 200_000_000_000)
    up_all = [up_own, up_next, up_far, up_prev]
    down_all = [down_own, down_next, down_far, down_prev]

    rank = 2 * capacity
    peers = ep_size // 2
    lanes = peers * rank
    flat_ids = jnp.concatenate(id_list, axis=0).reshape(-1)
    entries = flat_ids.shape[0]
    hits = flat_ids[:, None] == jnp.arange(ep_size, dtype=jnp.int32)[None, :]
    order = jnp.arange(entries, dtype=jnp.int32)
    per = samples * picks
    lower = (order[None, :] < order[:, None]) & (order[None, :] // per == order[:, None] // per)
    ahead = jnp.dot(
        lower.astype(jnp.bfloat16), hits.astype(jnp.bfloat16), preferred_element_type=jnp.float32
    )
    earlier = jnp.sum(jnp.where(hits, ahead, 0.0), axis=1).astype(jnp.int32)
    place = ((flat_ids // 2) * rank + earlier).reshape(3, samples, picks)
    groups = [[2 * j + c for j in range(peers)] for c in range(2)]

    def exchange(value):
        return lax.all_to_all(
            value.reshape(peers, rank, half),
            "ep",
            split_axis=0,
            concat_axis=0,
            axis_index_groups=groups,
            tiled=True,
        ).reshape(lanes, half)

    match, arrived = [], []
    for k in range(2):
        at = jnp.concatenate(
            [
                jnp.where(expert_ids % 2 == cores[k], place[0] + side[k] * capacity, -1),
                jnp.where(
                    id_list[k + 1] % 2 == cores[k], place[k + 1] + (1 - side[k]) * capacity, -1
                ),
            ],
            axis=0,
        )
        match.append(at[:, :, None] == jnp.arange(lanes, dtype=jnp.int32)[None, None, :])
        placing = jnp.sum(match[k].astype(jnp.float32), axis=1).astype(jnp.bfloat16)
        outgoing = lax.dot_general(
            placing, rows[k], (((0,), (0,)), ((), ())), preferred_element_type=jnp.float32
        ).astype(jnp.bfloat16)
        arrived.append(exchange(outgoing if k == 0 else swap_cores(outgoing)))

    shift = jnp.where(here % 2 == 1, grp_size - 1, 1).astype(jnp.int32)
    first, second = 0.0, 0.0
    for k in range(2):
        mine, rounded = up_project(arrived[k], up_all, 1)
        theirs = swap_planes(rounded, 0)
        if k == 1:
            (theirs,) = after((q_in, kv_in), theirs)
        produced = down_project(shift[None], mine, theirs, down_all, 2)
        if k == 0:
            moved_slot = mig_slot[0, 0]
            moved_target = mig_dest[0, 0]
            late_query, late_kv = after(produced, query_second, kv_second)
            q_here = lax.dynamic_index_in_dim(late_query, moved_slot, 0, keepdims=False)
            kv_here = lax.dynamic_index_in_dim(late_kv, moved_slot, 0, keepdims=True)
            packet = jnp.concatenate(
                [q_here, kv_here, jnp.zeros((15, q_here.shape[1]), jnp.bfloat16)], axis=0
            )
            offset = (moved_target - me) % grp_size
            got = packet
            for r in steps[1:]:
                got = jnp.where(offset == r, hop(packet, "grp", -r), got)
            heads = q_here.shape[0]
            q_in, kv_in = got[:heads], got[heads : heads + 1]
        returned = exchange(produced if k == 0 else swap_cores(produced))
        gates = jnp.concatenate([gate_weights, gate_list[k + 1]], axis=0)
        mixing = jnp.sum(jnp.where(match[k], gates[:, :, None], 0.0), axis=1)
        high = lax.reduce_precision(mixing, 8, 7)
        mixing = jnp.concatenate([high, mixing - high], axis=0).astype(jnp.bfloat16)
        mixed = jnp.dot(mixing, returned, preferred_element_type=jnp.float32)
        summed = (mixed[: 2 * samples] + mixed[2 * samples :]).reshape(2, samples, half)
        own, other = summed[0], swap_planes(summed[1], k)
        first = first + jnp.where(side[k] == 0, own, other)
        second = second + jnp.where(side[k] == 0, other, own)
    moe_out = jnp.concatenate([first, second], axis=1).astype(jnp.bfloat16)

    lens = cache_len[0]
    pages = page_table(lens, page_perm[0], cache_pool.shape[1], cache_pool.shape[0])
    attn_first, attn_second, out_moved = attention(
        lens,
        pages,
        moved_slot[None],
        query_first,
        query_second,
        q_in,
        kv_first[:, None, :],
        kv_second[:, None, :],
        kv_in,
        cache_pool,
    )
    zero = jnp.zeros((), jnp.bfloat16)
    arrived_out = jnp.where(offset == 0, out_moved, zero)
    for r in steps[1:]:
        arrived_out = arrived_out + hop(jnp.where(offset == r, out_moved, zero), "grp", r)
    attn_second = lax.dynamic_update_index_in_dim(attn_second, arrived_out, moved_slot, 0)

    return (attn_first, attn_second, moe_out)


def solution(mesh):
    return jax.shard_map(
        shards,
        mesh=mesh,
        in_specs=(
            P(("ep", "grp"), None),
            P(("ep", "grp"), None),
            P(("ep", "grp"), None),
            P("ep", None, "grp"),
            P("ep", None, "grp"),
            P(("ep", "grp"), None, None),
            P(("ep", "grp"), None),
            P(("ep", "grp"), None, None),
            P(("ep", "grp"), None),
            P(("ep", "grp"), None, None),
            P(("ep", "grp"), None),
            P(("ep", "grp"), None),
            P("ep", "grp"),
            P("ep", "grp"),
        ),
        out_specs=(
            P(("ep", "grp"), None, None),
            P(("ep", "grp"), None, None),
            P(("ep", "grp"), None),
        ),
        check_vma=False,
    )
```

```python
import math

import jax
import jax.numpy as jnp
from jax import lax
from jax.experimental import pallas as pl
from jax.experimental.pallas import tpu as pltpu
from jax.sharding import PartitionSpec as P

LAT = 512
MAXP = 8
NEG = -1e30
PAIRS = ((1, 2), (2, 1), (3, 0), (0, 3))


def hop(value, axis, step):
    size = lax.axis_size(axis)
    return lax.ppermute(value, axis, [(i, (i + step) % size) for i in range(size)])


def after(first, *values):
    return lax.optimization_barrier((first,) + values)[1:]


def attention_kernel(
    lens, pages, moved, q_one, q_two, q_in, kv_one, kv_two, kv_in, pool, out_one, out_two, out_moved, acc
):
    slot = pl.program_id(0)
    heads = q_one.shape[1]
    rows = 2 * heads
    key_width = q_one.shape[2]
    page_rows = pool.shape[1]
    block = 2 * page_rows
    scale = 1.0 / math.sqrt(key_width / 3.0)
    is_moved = slot == moved[0]
    second = jnp.where(is_moved, q_in[...], q_two[0])
    queries = jnp.concatenate([q_one[0], second], axis=0)
    fresh_one = kv_one[0]
    fresh_two = jnp.where(is_moved, kv_in[...], kv_two[0])
    fresh = jnp.concatenate(
        [fresh_one, fresh_two, jnp.zeros((14, key_width), jnp.bfloat16)], axis=0
    )
    contract = (((1,), (1,)), ((), ()))
    scores = lax.dot_general(queries, fresh, contract, preferred_element_type=jnp.float32) * scale
    row = lax.broadcasted_iota(jnp.int32, scores.shape, 0)
    col = lax.broadcasted_iota(jnp.int32, scores.shape, 1)
    scores = jnp.where((col == 0) | ((col == 1) & (row >= heads)), scores, NEG)
    top = jnp.max(scores, axis=1, keepdims=True)
    weights = jnp.exp(scores - top)
    total = jnp.sum(weights, axis=1, keepdims=True)
    acc[...] = jnp.dot(
        weights.astype(jnp.bfloat16), fresh[:, :LAT], preferred_element_type=jnp.float32
    )
    live = lens[slot]

    def step(b, carry):
        top, total = carry
        keys = jnp.concatenate(
            [pool[pages[slot * MAXP + 2 * b]], pool[pages[slot * MAXP + 2 * b + 1]]], axis=0
        )
        scores = (
            lax.dot_general(queries, keys, contract, preferred_element_type=jnp.float32) * scale
        )
        col = lax.broadcasted_iota(jnp.int32, scores.shape, 1) + b * block
        scores = jnp.where(col < live, scores, NEG)
        new_top = jnp.maximum(top, jnp.max(scores, axis=1, keepdims=True))
        shrink = jnp.exp(top - new_top)
        weights = jnp.exp(scores - new_top)
        total = total * shrink + jnp.sum(weights, axis=1, keepdims=True)
        acc[...] = acc[...] * shrink + jnp.dot(
            weights.astype(jnp.bfloat16), keys[:, :LAT], preferred_element_type=jnp.float32
        )
        return new_top, total

    top, total = lax.fori_loop(0, (live + block - 1) // block, step, (top, total))
    result = (acc[...] / total).astype(jnp.bfloat16)
    out_one[0] = result[:heads]
    out_two[0] = result[heads:]

    @pl.when(is_moved)
    def _():
        out_moved[...] = result[heads:]


def attention(lens, pages, moved, q_one, q_two, q_in, kv_one, kv_two, kv_in, pool):
    samples, heads, key_width = q_one.shape
    one = lambda *shape: pl.BlockSpec((1,) + shape, lambda i, *_: (i,) + (0,) * len(shape))
    whole = lambda *shape: pl.BlockSpec(shape, lambda i, *_: (0,) * len(shape))
    return pl.pallas_call(
        attention_kernel,
        grid_spec=pltpu.PrefetchScalarGridSpec(
            num_scalar_prefetch=3,
            grid=(samples,),
            in_specs=[
                one(heads, key_width),
                one(heads, key_width),
                whole(heads, key_width),
                one(1, key_width),
                one(1, key_width),
                whole(1, key_width),
                whole(*pool.shape),
            ],
            out_specs=[one(heads, LAT), one(heads, LAT), whole(heads, LAT)],
            scratch_shapes=[pltpu.VMEM((2 * heads, LAT), jnp.float32)],
        ),
        out_shape=[
            jax.ShapeDtypeStruct((samples, heads, LAT), jnp.bfloat16),
            jax.ShapeDtypeStruct((samples, heads, LAT), jnp.bfloat16),
            jax.ShapeDtypeStruct((heads, LAT), jnp.bfloat16),
        ],
        compiler_params=pltpu.CompilerParams(vmem_limit_bytes=24 * 1024 * 1024),
        cost_estimate=pl.CostEstimate(
            flops=12_000_000_000, bytes_accessed=8_000_000, transcendentals=1_000_000
        ),
        name="attention",
    )(lens, pages, moved, q_one, q_two, q_in, kv_one, kv_two, kv_in, pool)


def choose_kernel(which, first, second, out):
    @pl.when(which[0] == 0)
    def _():
        out[...] = first[...]

    @pl.when(which[0] != 0)
    def _():
        out[...] = second[...]


def choose(which, first, second, flops):
    steps = 4
    block = pl.BlockSpec((first.shape[0] // steps, first.shape[1]), lambda k, *_: (k, 0))
    return pl.pallas_call(
        choose_kernel,
        grid_spec=pltpu.PrefetchScalarGridSpec(
            num_scalar_prefetch=1, grid=(steps,), in_specs=[block, block], out_specs=block
        ),
        out_shape=jax.ShapeDtypeStruct(first.shape, first.dtype),
        cost_estimate=pl.CostEstimate(
            flops=flops, bytes_accessed=3 * first.size * 2, transcendentals=0
        ),
        name="choose",
    )(which, first, second)


def up_kernel(_, rows, *refs):
    weights, (whole, sent) = refs[:-2], refs[-2:]
    for i, weight in enumerate(weights):
        part = jnp.dot(rows[...], weight[...], preferred_element_type=jnp.float32)
        whole[i] = part
        sent[i] = part.astype(jnp.bfloat16)


def up_project(which, rows, weights, steps):
    count, depth = rows.shape
    units = weights[0].shape[1]
    shape = (len(weights), count, units)
    out = pl.BlockSpec((len(weights), count // steps, units), lambda k, *_: (0, k, 0))
    halves = pl.BlockSpec((depth, units), lambda k, half: (half[0], 0))
    whole = pl.BlockSpec((depth, units), lambda k, *_: (0, 0))
    return pl.pallas_call(
        up_kernel,
        grid_spec=pltpu.PrefetchScalarGridSpec(
            num_scalar_prefetch=1,
            grid=(steps,),
            in_specs=[pl.BlockSpec((count // steps, depth), lambda k, *_: (k, 0))]
            + [whole if w.shape[0] == depth else halves for w in weights],
            out_specs=[out, out],
        ),
        out_shape=[
            jax.ShapeDtypeStruct(shape, jnp.float32),
            jax.ShapeDtypeStruct(shape, jnp.bfloat16),
        ],
        compiler_params=pltpu.CompilerParams(vmem_limit_bytes=58 * 1024 * 1024),
        cost_estimate=pl.CostEstimate(
            flops=2 * len(weights) * count * depth * units,
            bytes_accessed=5_000_000,
            transcendentals=0,
        ),
        name="up_project",
    )(which, rows, *weights)


def down_kernel(scalars, mine_a, mine_b, theirs_a, theirs_b, *refs):
    weights, out, held = refs[:4], refs[4], refs[5]

    @pl.when(pl.program_id(0) == 0)
    def _():
        mine = [mine_a[0], mine_a[1], mine_b[0], mine_b[1]]
        theirs = [theirs_a.at[0], theirs_a.at[1], theirs_b.at[0], theirs_b.at[1]]
        for i in range(4):
            up, down = theirs[(i + 1) % 4][...], theirs[(i - 1) % 4][...]
            other = jnp.where(scalars[1] == 1, up.astype(jnp.float32), down.astype(jnp.float32))
            value = mine[i] + other
            held[i] = (value / (1.0 + jnp.exp(-value))).astype(jnp.bfloat16)

    total = None
    for i, weight in enumerate(weights):
        part = lax.dot_general(
            held[i], weight[...], (((1,), (1,)), ((), ())), preferred_element_type=jnp.float32
        )
        total = part if total is None else total + part
    out[...] = total.astype(jnp.bfloat16)


def down_project(scalars, mine, theirs, weights, steps):
    count, units = mine[0].shape[1:]
    depth = weights[1].shape[0]
    whole = pl.BlockSpec(mine[0].shape, lambda k, *_: (0, 0, 0))
    tile = (depth // steps, units)
    return pl.pallas_call(
        down_kernel,
        grid_spec=pltpu.PrefetchScalarGridSpec(
            num_scalar_prefetch=1,
            grid=(steps,),
            in_specs=[whole] * 4
            + [pl.BlockSpec(tile, lambda k, at: (at[0] * steps + k, 0))]
            + [pl.BlockSpec(tile, lambda k, *_: (k, 0))] * 3,
            out_specs=pl.BlockSpec((count, depth // steps), lambda k, *_: (0, k)),
            scratch_shapes=[pltpu.VMEM((4, count, units), jnp.bfloat16)],
        ),
        out_shape=jax.ShapeDtypeStruct((count, depth), jnp.bfloat16),
        compiler_params=pltpu.CompilerParams(vmem_limit_bytes=24 * 1024 * 1024),
        cost_estimate=pl.CostEstimate(
            flops=8 * count * depth * units,
            bytes_accessed=9_000_000,
            transcendentals=4 * count * units,
        ),
        name="down_project",
    )(scalars, *mine, *theirs, *weights)


def page_table(cache_len, page_perm, page_rows, pool_pages):
    used = (cache_len + page_rows - 1) // page_rows
    slots = used.shape[0]
    before = jnp.arange(slots)[None, :] < jnp.arange(slots)[:, None]
    offset = jnp.sum(jnp.where(before, used[None, :], 0), axis=1)
    place = jnp.minimum(
        offset[:, None] + jnp.arange(MAXP, dtype=jnp.int32)[None, :], pool_pages - 1
    ).reshape(-1)
    hit = place[:, None] == jnp.arange(pool_pages, dtype=jnp.int32)[None, :]
    return jnp.sum(jnp.where(hit, page_perm[None, :], 0), axis=1)


def shards(
    hidden,
    expert_ids,
    gate_weights,
    w_up,
    w_down,
    query_first,
    kv_first,
    query_second,
    kv_second,
    cache_pool,
    cache_len,
    page_perm,
    mig_slot,
    mig_dest,
):
    samples, picks = expert_ids.shape
    width = hidden.shape[1]
    ep_size = lax.axis_size("ep")
    grp_size = lax.axis_size("grp")
    capacity = min(samples, max(2, 2 * samples * picks // ep_size))
    me = lax.axis_index("grp")
    steps = range(grp_size)

    half = width // 2
    core = lax.axis_index("ep") % 2
    turned = [(me - c) % grp_size for c in range(2)]
    side = [turned[c] // 2 for c in range(2)]
    here = jnp.where(core == 0, turned[0], turned[1])
    partner = [[((a + c) % grp_size, (b + c) % grp_size) for a, b in PAIRS] for c in range(2)]

    def by_core(pairs):
        return [
            (e * grp_size + (a + e % 2) % grp_size, e * grp_size + (b + e % 2) % grp_size)
            for e in range(ep_size)
            for a, b in pairs
        ]

    def part(value, which, axis):
        return lax.dynamic_slice_in_dim(value, which * half, half, axis)

    rows, id_list, gate_list = [], [expert_ids], []
    term = lax.reduce_precision(gate_weights, 8, 7)
    rest = gate_weights - term
    next_term = lax.reduce_precision(rest, 8, 7)
    small = jnp.concatenate(
        [expert_ids.astype(jnp.float32), term, next_term, rest - next_term], axis=1
    ).astype(jnp.bfloat16)
    small = jnp.pad(small, ((0, 0), (0, 128 - 4 * picks)))
    for c in range(2):
        sent = jnp.concatenate([part(hidden, 1 - side[c], 1), small], axis=1)
        theirs = lax.ppermute(sent, "grp", partner[c])
        extra = theirs[:, half : half + 4 * picks].astype(jnp.float32).reshape(samples, 4, picks)
        id_list.append(extra[:, 0].astype(jnp.int32))
        gate_list += [gate_weights, (extra[:, 1] + extra[:, 2]) + extra[:, 3]]
        rows += [part(hidden, side[c], 1), theirs[:, :half]]
    rows = jnp.concatenate(rows, axis=0)

    ahead = jnp.where((here == 0) | (here == 3), 0, 1)

    def spread(weight, *first):
        to_next, to_prev = after(first, part(weight, ahead, 0), part(weight, 1 - ahead, 0))
        return hop(to_next, "grp", 1), hop(to_prev, "grp", -1)

    def pass_on(prev, nxt, flops):
        picked = choose((here % 2)[None], prev, nxt, flops)
        far = lax.ppermute(picked, ("ep", "grp"), by_core([(0, 1), (1, 0), (2, 3), (3, 2)]))
        return far

    up_prev, up_next = spread(w_up[0], rows)
    up_far = pass_on(up_prev, up_next, 200_000_000_000)
    down_prev, down_next = spread(w_down[0], up_prev, up_next)
    down_far = pass_on(down_prev, down_next, 0)

    rank = 2 * capacity
    lanes_all = ep_size * rank
    flat_ids = jnp.concatenate(id_list, axis=0).reshape(-1)
    entries = flat_ids.shape[0]
    hits = flat_ids[:, None] == jnp.arange(ep_size, dtype=jnp.int32)[None, :]
    order = jnp.arange(entries, dtype=jnp.int32)
    per = samples * picks
    lower = (order[None, :] < order[:, None]) & (order[None, :] // per == order[:, None] // per)
    ahead = jnp.dot(
        lower.astype(jnp.bfloat16), hits.astype(jnp.bfloat16), preferred_element_type=jnp.float32
    )
    earlier = jnp.sum(jnp.where(hits, ahead, 0.0), axis=1).astype(jnp.int32)
    place = (flat_ids * rank + earlier).reshape(3, samples, picks)
    own_at, first_at, second_at = place[0], place[1], place[2]
    even = (expert_ids % 2) == 0
    place = jnp.concatenate(
        [
            jnp.where(even, own_at + side[0] * capacity, -1),
            jnp.where((id_list[1] % 2) == 0, first_at + (1 - side[0]) * capacity, -1),
            jnp.where(even, -1, own_at + side[1] * capacity),
            jnp.where((id_list[2] % 2) == 0, -1, second_at + (1 - side[1]) * capacity),
        ],
        axis=0,
    )
    match = place[:, :, None] == jnp.arange(lanes_all, dtype=jnp.int32)[None, None, :]
    placing = jnp.sum(match.astype(jnp.float32), axis=1).astype(jnp.bfloat16)
    outgoing = lax.dot_general(
        placing, rows, (((0,), (0,)), ((), ())), preferred_element_type=jnp.float32
    ).astype(jnp.bfloat16)
    arrived = lax.all_to_all(
        outgoing.reshape(ep_size, rank, half), "ep", split_axis=0, concat_axis=0, tiled=True
    ).reshape(lanes_all, half)

    moved_slot = mig_slot[0, 0]
    moved_target = mig_dest[0, 0]
    query_second, kv_second = after(outgoing, query_second, kv_second)
    q_here = lax.dynamic_index_in_dim(query_second, moved_slot, 0, keepdims=False)
    kv_here = lax.dynamic_index_in_dim(kv_second, moved_slot, 0, keepdims=True)
    packet = jnp.concatenate(
        [q_here, kv_here, jnp.zeros((15, q_here.shape[1]), jnp.bfloat16)], axis=0
    )
    offset = (moved_target - me) % grp_size
    got = packet
    for r in steps[1:]:
        got = jnp.where(offset == r, hop(packet, "grp", -r), got)
    heads = q_here.shape[0]
    q_in, kv_in = got[:heads], got[heads : heads + 1]

    lens = cache_len[0]
    pages = page_table(lens, page_perm[0], cache_pool.shape[1], cache_pool.shape[0])
    attn_first, attn_second, out_moved = attention(
        lens,
        pages,
        moved_slot[None],
        query_first,
        query_second,
        q_in,
        kv_first[:, None, :],
        kv_second[:, None, :],
        kv_in,
        cache_pool,
    )
    zero = jnp.zeros((), jnp.bfloat16)
    arrived_out = jnp.where(offset == 0, out_moved, zero)
    for r in steps[1:]:
        arrived_out = arrived_out + hop(jnp.where(offset == r, out_moved, zero), "grp", r)
    attn_second = lax.dynamic_update_index_in_dim(attn_second, arrived_out, moved_slot, 0)

    scalars = jnp.stack([here // 2, 1 - here % 2]).astype(jnp.int32)
    mine_a, sent_a = up_project(scalars, arrived, [w_up[0], up_next], 2)
    theirs_a = lax.ppermute(sent_a, ("ep", "grp"), by_core(PAIRS))
    mine_b, sent_b = up_project(scalars, arrived, [up_far, up_prev], 2)
    (sent_b,) = after(down_far, sent_b)
    theirs_b = lax.ppermute(sent_b, ("ep", "grp"), by_core(PAIRS))
    produced = down_project(
        scalars,
        [mine_a, mine_b],
        [theirs_a, theirs_b],
        [w_down[0], down_next, down_far, down_prev],
        2,
    )
    returned = lax.all_to_all(
        produced.reshape(ep_size, rank, half),
        "ep",
        split_axis=0,
        concat_axis=0,
        tiled=True,
    ).reshape(lanes_all, half)
    gates = jnp.concatenate(gate_list, axis=0)
    mixing = jnp.sum(jnp.where(match, gates[:, :, None], 0.0), axis=1)
    high = lax.reduce_precision(mixing, 8, 7)
    mixing = jnp.concatenate([high, mixing - high], axis=0).astype(jnp.bfloat16)
    mixed = jnp.dot(mixing, returned, preferred_element_type=jnp.float32)
    summed = (mixed[: 4 * samples] + mixed[4 * samples :]).reshape(4, samples, half)
    first, second = 0.0, 0.0
    for c in range(2):
        own = summed[2 * c]
        other = lax.ppermute(summed[2 * c + 1], "grp", partner[c])
        first = first + jnp.where(side[c] == 0, own, other)
        second = second + jnp.where(side[c] == 0, other, own)
    moe_out = jnp.concatenate([first, second], axis=1).astype(jnp.bfloat16)
    return (attn_first, attn_second, moe_out)


def solution(mesh):
    return jax.shard_map(
        shards,
        mesh=mesh,
        in_specs=(
            P(("ep", "grp"), None),
            P(("ep", "grp"), None),
            P(("ep", "grp"), None),
            P("ep", None, "grp"),
            P("ep", None, "grp"),
            P(("ep", "grp"), None, None),
            P(("ep", "grp"), None),
            P(("ep", "grp"), None, None),
            P(("ep", "grp"), None),
            P(("ep", "grp"), None, None),
            P(("ep", "grp"), None),
            P(("ep", "grp"), None),
            P("ep", "grp"),
            P("ep", "grp"),
        ),
        out_specs=(
            P(("ep", "grp"), None, None),
            P(("ep", "grp"), None, None),
            P(("ep", "grp"), None),
        ),
        check_vma=False,
    )
```

```python
import math

import jax
import jax.numpy as jnp
from jax import lax
from jax.experimental import pallas as pl
from jax.experimental.pallas import tpu as pltpu
from jax.sharding import PartitionSpec as P

LAT = 512
MAXP = 8
NEG = -1e30
PAIRS = ((1, 2), (2, 1), (3, 0), (0, 3))


def hop(value, axis, step):
    size = lax.axis_size(axis)
    return lax.ppermute(value, axis, [(i, (i + step) % size) for i in range(size)])


def after(first, *values):
    return lax.optimization_barrier((first,) + values)[1:]


def attention_kernel(
    lens, pages, moved, q_one, q_two, q_in, kv_one, kv_two, kv_in, pool, out_one, out_two, out_moved, acc
):
    slot = pl.program_id(0)
    heads = q_one.shape[1]
    rows = 2 * heads
    key_width = q_one.shape[2]
    page_rows = pool.shape[1]
    block = 2 * page_rows
    scale = 1.0 / math.sqrt(key_width / 3.0)
    is_moved = slot == moved[0]
    second = jnp.where(is_moved, q_in[...], q_two[0])
    queries = jnp.concatenate([q_one[0], second], axis=0)
    fresh_one = kv_one[0]
    fresh_two = jnp.where(is_moved, kv_in[...], kv_two[0])
    fresh = jnp.concatenate(
        [fresh_one, fresh_two, jnp.zeros((14, key_width), jnp.bfloat16)], axis=0
    )
    contract = (((1,), (1,)), ((), ()))
    scores = lax.dot_general(queries, fresh, contract, preferred_element_type=jnp.float32) * scale
    row = lax.broadcasted_iota(jnp.int32, scores.shape, 0)
    col = lax.broadcasted_iota(jnp.int32, scores.shape, 1)
    scores = jnp.where((col == 0) | ((col == 1) & (row >= heads)), scores, NEG)
    top = jnp.max(scores, axis=1, keepdims=True)
    weights = jnp.exp(scores - top)
    total = jnp.sum(weights, axis=1, keepdims=True)
    acc[...] = jnp.dot(
        weights.astype(jnp.bfloat16), fresh[:, :LAT], preferred_element_type=jnp.float32
    )
    live = lens[slot]

    def step(b, carry):
        top, total = carry
        keys = jnp.concatenate(
            [pool[pages[slot * MAXP + 2 * b]], pool[pages[slot * MAXP + 2 * b + 1]]], axis=0
        )
        scores = (
            lax.dot_general(queries, keys, contract, preferred_element_type=jnp.float32) * scale
        )
        col = lax.broadcasted_iota(jnp.int32, scores.shape, 1) + b * block
        scores = jnp.where(col < live, scores, NEG)
        new_top = jnp.maximum(top, jnp.max(scores, axis=1, keepdims=True))
        shrink = jnp.exp(top - new_top)
        weights = jnp.exp(scores - new_top)
        total = total * shrink + jnp.sum(weights, axis=1, keepdims=True)
        acc[...] = acc[...] * shrink + jnp.dot(
            weights.astype(jnp.bfloat16), keys[:, :LAT], preferred_element_type=jnp.float32
        )
        return new_top, total

    top, total = lax.fori_loop(0, (live + block - 1) // block, step, (top, total))
    result = (acc[...] / total).astype(jnp.bfloat16)
    out_one[0] = result[:heads]
    out_two[0] = result[heads:]

    @pl.when(is_moved)
    def _():
        out_moved[...] = result[heads:]


def attention(lens, pages, moved, q_one, q_two, q_in, kv_one, kv_two, kv_in, pool):
    samples, heads, key_width = q_one.shape
    one = lambda *shape: pl.BlockSpec((1,) + shape, lambda i, *_: (i,) + (0,) * len(shape))
    whole = lambda *shape: pl.BlockSpec(shape, lambda i, *_: (0,) * len(shape))
    return pl.pallas_call(
        attention_kernel,
        grid_spec=pltpu.PrefetchScalarGridSpec(
            num_scalar_prefetch=3,
            grid=(samples,),
            in_specs=[
                one(heads, key_width),
                one(heads, key_width),
                whole(heads, key_width),
                one(1, key_width),
                one(1, key_width),
                whole(1, key_width),
                whole(*pool.shape),
            ],
            out_specs=[one(heads, LAT), one(heads, LAT), whole(heads, LAT)],
            scratch_shapes=[pltpu.VMEM((2 * heads, LAT), jnp.float32)],
        ),
        out_shape=[
            jax.ShapeDtypeStruct((samples, heads, LAT), jnp.bfloat16),
            jax.ShapeDtypeStruct((samples, heads, LAT), jnp.bfloat16),
            jax.ShapeDtypeStruct((heads, LAT), jnp.bfloat16),
        ],
        compiler_params=pltpu.CompilerParams(vmem_limit_bytes=24 * 1024 * 1024),
        cost_estimate=pl.CostEstimate(
            flops=12_000_000_000, bytes_accessed=8_000_000, transcendentals=1_000_000
        ),
        name="attention",
    )(lens, pages, moved, q_one, q_two, q_in, kv_one, kv_two, kv_in, pool)


def choose_kernel(which, first, second, out):
    @pl.when(which[0] == 0)
    def _():
        out[...] = first[...]

    @pl.when(which[0] != 0)
    def _():
        out[...] = second[...]


def choose(which, first, second, flops):
    steps = 4
    block = pl.BlockSpec((first.shape[0] // steps, first.shape[1]), lambda k, *_: (k, 0))
    return pl.pallas_call(
        choose_kernel,
        grid_spec=pltpu.PrefetchScalarGridSpec(
            num_scalar_prefetch=1, grid=(steps,), in_specs=[block, block], out_specs=block
        ),
        out_shape=jax.ShapeDtypeStruct(first.shape, first.dtype),
        cost_estimate=pl.CostEstimate(
            flops=flops, bytes_accessed=3 * first.size * 2, transcendentals=0
        ),
        name="choose",
    )(which, first, second)


def up_kernel(_, rows, *refs):
    weights, (whole, sent) = refs[:-2], refs[-2:]
    for i, weight in enumerate(weights):
        part = jnp.dot(rows[...], weight[...], preferred_element_type=jnp.float32)
        whole[i] = part
        sent[i] = part.astype(jnp.bfloat16)


def up_project(which, rows, weights, steps):
    count, depth = rows.shape
    units = weights[0].shape[1]
    shape = (len(weights), count, units)
    out = pl.BlockSpec((len(weights), count // steps, units), lambda k, *_: (0, k, 0))
    halves = pl.BlockSpec((depth, units), lambda k, half: (half[0], 0))
    whole = pl.BlockSpec((depth, units), lambda k, *_: (0, 0))
    return pl.pallas_call(
        up_kernel,
        grid_spec=pltpu.PrefetchScalarGridSpec(
            num_scalar_prefetch=1,
            grid=(steps,),
            in_specs=[pl.BlockSpec((count // steps, depth), lambda k, *_: (k, 0))]
            + [whole if w.shape[0] == depth else halves for w in weights],
            out_specs=[out, out],
        ),
        out_shape=[
            jax.ShapeDtypeStruct(shape, jnp.float32),
            jax.ShapeDtypeStruct(shape, jnp.bfloat16),
        ],
        compiler_params=pltpu.CompilerParams(vmem_limit_bytes=24 * 1024 * 1024),
        cost_estimate=pl.CostEstimate(
            flops=2 * len(weights) * count * depth * units,
            bytes_accessed=5_000_000,
            transcendentals=0,
        ),
        name="up_project",
    )(which, rows, *weights)


def down_kernel(scalars, mine_a, mine_b, theirs_a, theirs_b, *refs):
    weights, out, held = refs[:4], refs[4], refs[5]

    @pl.when(pl.program_id(0) == 0)
    def _():
        mine = [mine_a[0], mine_a[1], mine_b[0], mine_b[1]]
        theirs = [theirs_a.at[0], theirs_a.at[1], theirs_b.at[0], theirs_b.at[1]]
        for i in range(4):
            up, down = theirs[(i + 1) % 4][...], theirs[(i - 1) % 4][...]
            other = jnp.where(scalars[1] == 1, up.astype(jnp.float32), down.astype(jnp.float32))
            value = mine[i] + other
            held[i] = (value / (1.0 + jnp.exp(-value))).astype(jnp.bfloat16)

    total = None
    for i, weight in enumerate(weights):
        part = lax.dot_general(
            held[i], weight[...], (((1,), (1,)), ((), ())), preferred_element_type=jnp.float32
        )
        total = part if total is None else total + part
    out[...] = total.astype(jnp.bfloat16)


def down_project(scalars, mine, theirs, weights, steps):
    count, units = mine[0].shape[1:]
    depth = weights[1].shape[0]
    whole = pl.BlockSpec(mine[0].shape, lambda k, *_: (0, 0, 0))
    tile = (depth // steps, units)
    return pl.pallas_call(
        down_kernel,
        grid_spec=pltpu.PrefetchScalarGridSpec(
            num_scalar_prefetch=1,
            grid=(steps,),
            in_specs=[whole] * 4
            + [pl.BlockSpec(tile, lambda k, at: (at[0] * steps + k, 0))]
            + [pl.BlockSpec(tile, lambda k, *_: (k, 0))] * 3,
            out_specs=pl.BlockSpec((count, depth // steps), lambda k, *_: (0, k)),
            scratch_shapes=[pltpu.VMEM((4, count, units), jnp.bfloat16)],
        ),
        out_shape=jax.ShapeDtypeStruct((count, depth), jnp.bfloat16),
        compiler_params=pltpu.CompilerParams(vmem_limit_bytes=24 * 1024 * 1024),
        cost_estimate=pl.CostEstimate(
            flops=8 * count * depth * units,
            bytes_accessed=9_000_000,
            transcendentals=4 * count * units,
        ),
        name="down_project",
    )(scalars, *mine, *theirs, *weights)


def page_table(cache_len, page_perm, page_rows, pool_pages):
    used = (cache_len + page_rows - 1) // page_rows
    slots = used.shape[0]
    before = jnp.arange(slots)[None, :] < jnp.arange(slots)[:, None]
    offset = jnp.sum(jnp.where(before, used[None, :], 0), axis=1)
    place = jnp.minimum(
        offset[:, None] + jnp.arange(MAXP, dtype=jnp.int32)[None, :], pool_pages - 1
    ).reshape(-1)
    hit = place[:, None] == jnp.arange(pool_pages, dtype=jnp.int32)[None, :]
    return jnp.sum(jnp.where(hit, page_perm[None, :], 0), axis=1)


def shards(
    hidden,
    expert_ids,
    gate_weights,
    w_up,
    w_down,
    query_first,
    kv_first,
    query_second,
    kv_second,
    cache_pool,
    cache_len,
    page_perm,
    mig_slot,
    mig_dest,
):
    samples, picks = expert_ids.shape
    width = hidden.shape[1]
    ep_size = lax.axis_size("ep")
    grp_size = lax.axis_size("grp")
    capacity = min(samples, max(2, 2 * samples * picks // ep_size))
    me = lax.axis_index("grp")
    steps = range(grp_size)

    half = width // 2
    core = lax.axis_index("ep") % 2
    turned = [(me - c) % grp_size for c in range(2)]
    side = [turned[c] // 2 for c in range(2)]
    here = jnp.where(core == 0, turned[0], turned[1])
    partner = [[((a + c) % grp_size, (b + c) % grp_size) for a, b in PAIRS] for c in range(2)]

    def by_core(pairs):
        return [
            (e * grp_size + (a + e % 2) % grp_size, e * grp_size + (b + e % 2) % grp_size)
            for e in range(ep_size)
            for a, b in pairs
        ]

    def part(value, which, axis):
        return lax.dynamic_slice_in_dim(value, which * half, half, axis)

    rows, id_list, gate_list = [], [expert_ids], []
    term = lax.reduce_precision(gate_weights, 8, 7)
    rest = gate_weights - term
    next_term = lax.reduce_precision(rest, 8, 7)
    small = jnp.concatenate(
        [expert_ids.astype(jnp.float32), term, next_term, rest - next_term], axis=1
    ).astype(jnp.bfloat16)
    small = jnp.pad(small, ((0, 0), (0, 128 - 4 * picks)))
    for c in range(2):
        sent = jnp.concatenate([part(hidden, 1 - side[c], 1), small], axis=1)
        theirs = lax.ppermute(sent, "grp", partner[c])
        extra = theirs[:, half : half + 4 * picks].astype(jnp.float32).reshape(samples, 4, picks)
        id_list.append(extra[:, 0].astype(jnp.int32))
        gate_list += [gate_weights, (extra[:, 1] + extra[:, 2]) + extra[:, 3]]
        rows += [part(hidden, side[c], 1), theirs[:, :half]]
    rows = jnp.concatenate(rows, axis=0)

    ahead = jnp.where((here == 0) | (here == 3), 0, 1)

    def spread(weight, *first):
        to_next, to_prev = after(first, part(weight, ahead, 0), part(weight, 1 - ahead, 0))
        return hop(to_next, "grp", 1), hop(to_prev, "grp", -1)

    def pass_on(prev, nxt, flops):
        picked = choose((here % 2)[None], prev, nxt, flops)
        far = lax.ppermute(picked, ("ep", "grp"), by_core([(0, 1), (1, 0), (2, 3), (3, 2)]))
        return far

    up_prev, up_next = spread(w_up[0], rows)
    up_far = pass_on(up_prev, up_next, 200_000_000_000)
    down_prev, down_next = spread(w_down[0], up_prev, up_next)
    down_far = pass_on(down_prev, down_next, 0)

    rank = 2 * capacity
    lanes_all = ep_size * rank
    flat_ids = jnp.concatenate(id_list, axis=0).reshape(-1)
    entries = flat_ids.shape[0]
    hits = flat_ids[:, None] == jnp.arange(ep_size, dtype=jnp.int32)[None, :]
    order = jnp.arange(entries, dtype=jnp.int32)
    per = samples * picks
    lower = (order[None, :] < order[:, None]) & (order[None, :] // per == order[:, None] // per)
    ahead = jnp.dot(
        lower.astype(jnp.bfloat16), hits.astype(jnp.bfloat16), preferred_element_type=jnp.float32
    )
    earlier = jnp.sum(jnp.where(hits, ahead, 0.0), axis=1).astype(jnp.int32)
    place = (flat_ids * rank + earlier).reshape(3, samples, picks)
    own_at, first_at, second_at = place[0], place[1], place[2]
    even = (expert_ids % 2) == 0
    place = jnp.concatenate(
        [
            jnp.where(even, own_at + side[0] * capacity, -1),
            jnp.where((id_list[1] % 2) == 0, first_at + (1 - side[0]) * capacity, -1),
            jnp.where(even, -1, own_at + side[1] * capacity),
            jnp.where((id_list[2] % 2) == 0, -1, second_at + (1 - side[1]) * capacity),
        ],
        axis=0,
    )
    match = place[:, :, None] == jnp.arange(lanes_all, dtype=jnp.int32)[None, None, :]
    placing = jnp.sum(match.astype(jnp.float32), axis=1).astype(jnp.bfloat16)
    outgoing = lax.dot_general(
        placing, rows, (((0,), (0,)), ((), ())), preferred_element_type=jnp.float32
    ).astype(jnp.bfloat16)
    arrived = lax.all_to_all(
        outgoing.reshape(ep_size, rank, half), "ep", split_axis=0, concat_axis=0, tiled=True
    ).reshape(lanes_all, half)

    moved_slot = mig_slot[0, 0]
    moved_target = mig_dest[0, 0]
    query_second, kv_second = after(outgoing, query_second, kv_second)
    q_here = lax.dynamic_index_in_dim(query_second, moved_slot, 0, keepdims=False)
    kv_here = lax.dynamic_index_in_dim(kv_second, moved_slot, 0, keepdims=True)
    packet = jnp.concatenate(
        [q_here, kv_here, jnp.zeros((15, q_here.shape[1]), jnp.bfloat16)], axis=0
    )
    offset = (moved_target - me) % grp_size
    got = packet
    for r in steps[1:]:
        got = jnp.where(offset == r, hop(packet, "grp", -r), got)
    heads = q_here.shape[0]
    q_in, kv_in = got[:heads], got[heads : heads + 1]

    lens = cache_len[0]
    pages = page_table(lens, page_perm[0], cache_pool.shape[1], cache_pool.shape[0])
    attn_first, attn_second, out_moved = attention(
        lens,
        pages,
        moved_slot[None],
        query_first,
        query_second,
        q_in,
        kv_first[:, None, :],
        kv_second[:, None, :],
        kv_in,
        cache_pool,
    )
    zero = jnp.zeros((), jnp.bfloat16)
    arrived_out = jnp.where(offset == 0, out_moved, zero)
    for r in steps[1:]:
        arrived_out = arrived_out + hop(jnp.where(offset == r, out_moved, zero), "grp", r)
    attn_second = lax.dynamic_update_index_in_dim(attn_second, arrived_out, moved_slot, 0)

    scalars = jnp.stack([here // 2, 1 - here % 2]).astype(jnp.int32)
    mine_a, sent_a = up_project(scalars, arrived, [w_up[0], up_next], 2)
    theirs_a = lax.ppermute(sent_a, ("ep", "grp"), by_core(PAIRS))
    mine_b, sent_b = up_project(scalars, arrived, [up_far, up_prev], 2)
    (sent_b,) = after(down_far, sent_b)
    theirs_b = lax.ppermute(sent_b, ("ep", "grp"), by_core(PAIRS))
    produced = down_project(
        scalars,
        [mine_a, mine_b],
        [theirs_a, theirs_b],
        [w_down[0], down_next, down_far, down_prev],
        2,
    )
    returned = lax.all_to_all(
        produced.reshape(ep_size, rank, half),
        "ep",
        split_axis=0,
        concat_axis=0,
        tiled=True,
    ).reshape(lanes_all, half)
    gates = jnp.concatenate(gate_list, axis=0)
    mixing = jnp.sum(jnp.where(match, gates[:, :, None], 0.0), axis=1)
    high = lax.reduce_precision(mixing, 8, 7)
    mixing = jnp.concatenate([high, mixing - high], axis=0).astype(jnp.bfloat16)
    mixed = jnp.dot(mixing, returned, preferred_element_type=jnp.float32)
    summed = (mixed[: 4 * samples] + mixed[4 * samples :]).reshape(4, samples, half)
    first, second = 0.0, 0.0
    for c in range(2):
        own = summed[2 * c]
        other = lax.ppermute(summed[2 * c + 1], "grp", partner[c])
        first = first + jnp.where(side[c] == 0, own, other)
        second = second + jnp.where(side[c] == 0, other, own)
    moe_out = jnp.concatenate([first, second], axis=1).astype(jnp.bfloat16)
    return (attn_first, attn_second, moe_out)


def solution(mesh):
    return jax.shard_map(
        shards,
        mesh=mesh,
        in_specs=(
            P(("ep", "grp"), None),
            P(("ep", "grp"), None),
            P(("ep", "grp"), None),
            P("ep", None, "grp"),
            P("ep", None, "grp"),
            P(("ep", "grp"), None, None),
            P(("ep", "grp"), None),
            P(("ep", "grp"), None, None),
            P(("ep", "grp"), None),
            P(("ep", "grp"), None, None),
            P(("ep", "grp"), None),
            P(("ep", "grp"), None),
            P("ep", "grp"),
            P("ep", "grp"),
        ),
        out_specs=(
            P(("ep", "grp"), None, None),
            P(("ep", "grp"), None, None),
            P(("ep", "grp"), None),
        ),
        check_vma=False,
    )
```

```python
import math

import jax
import jax.numpy as jnp
from jax import lax
from jax.experimental import pallas as pl
from jax.experimental.pallas import tpu as pltpu
from jax.sharding import PartitionSpec as P

LAT = 512
MAXP = 8
NEG = -1e30
PAIRS = ((1, 2), (2, 1), (3, 0), (0, 3))


def hop(value, axis, step):
    size = lax.axis_size(axis)
    return lax.ppermute(value, axis, [(i, (i + step) % size) for i in range(size)])


def after(first, *values):
    return lax.optimization_barrier((first,) + values)[1:]


def attention_kernel(
    lens, pages, moved, q_one, q_two, q_in, kv_one, kv_two, kv_in, pool, out_one, out_two, out_moved, acc
):
    slot = pl.program_id(0)
    heads = q_one.shape[1]
    rows = 2 * heads
    key_width = q_one.shape[2]
    page_rows = pool.shape[1]
    block = 2 * page_rows
    scale = 1.0 / math.sqrt(key_width / 3.0)
    is_moved = slot == moved[0]
    second = jnp.where(is_moved, q_in[...], q_two[0])
    queries = jnp.concatenate([q_one[0], second], axis=0)
    fresh_one = kv_one[0]
    fresh_two = jnp.where(is_moved, kv_in[...], kv_two[0])
    fresh = jnp.concatenate(
        [fresh_one, fresh_two, jnp.zeros((14, key_width), jnp.bfloat16)], axis=0
    )
    contract = (((1,), (1,)), ((), ()))
    scores = lax.dot_general(queries, fresh, contract, preferred_element_type=jnp.float32) * scale
    row = lax.broadcasted_iota(jnp.int32, scores.shape, 0)
    col = lax.broadcasted_iota(jnp.int32, scores.shape, 1)
    scores = jnp.where((col == 0) | ((col == 1) & (row >= heads)), scores, NEG)
    top = jnp.max(scores, axis=1, keepdims=True)
    weights = jnp.exp(scores - top)
    total = jnp.sum(weights, axis=1, keepdims=True)
    acc[...] = jnp.dot(
        weights.astype(jnp.bfloat16), fresh[:, :LAT], preferred_element_type=jnp.float32
    )
    live = lens[slot]

    def step(b, carry):
        top, total = carry
        keys = jnp.concatenate(
            [pool[pages[slot * MAXP + 2 * b]], pool[pages[slot * MAXP + 2 * b + 1]]], axis=0
        )
        scores = (
            lax.dot_general(queries, keys, contract, preferred_element_type=jnp.float32) * scale
        )
        col = lax.broadcasted_iota(jnp.int32, scores.shape, 1) + b * block
        scores = jnp.where(col < live, scores, NEG)
        new_top = jnp.maximum(top, jnp.max(scores, axis=1, keepdims=True))
        shrink = jnp.exp(top - new_top)
        weights = jnp.exp(scores - new_top)
        total = total * shrink + jnp.sum(weights, axis=1, keepdims=True)
        acc[...] = acc[...] * shrink + jnp.dot(
            weights.astype(jnp.bfloat16), keys[:, :LAT], preferred_element_type=jnp.float32
        )
        return new_top, total

    top, total = lax.fori_loop(0, (live + block - 1) // block, step, (top, total))
    result = (acc[...] / total).astype(jnp.bfloat16)
    out_one[0] = result[:heads]
    out_two[0] = result[heads:]

    @pl.when(is_moved)
    def _():
        out_moved[...] = result[heads:]


def attention(lens, pages, moved, q_one, q_two, q_in, kv_one, kv_two, kv_in, pool):
    samples, heads, key_width = q_one.shape
    one = lambda *shape: pl.BlockSpec((1,) + shape, lambda i, *_: (i,) + (0,) * len(shape))
    whole = lambda *shape: pl.BlockSpec(shape, lambda i, *_: (0,) * len(shape))
    return pl.pallas_call(
        attention_kernel,
        grid_spec=pltpu.PrefetchScalarGridSpec(
            num_scalar_prefetch=3,
            grid=(samples,),
            in_specs=[
                one(heads, key_width),
                one(heads, key_width),
                whole(heads, key_width),
                one(1, key_width),
                one(1, key_width),
                whole(1, key_width),
                whole(*pool.shape),
            ],
            out_specs=[one(heads, LAT), one(heads, LAT), whole(heads, LAT)],
            scratch_shapes=[pltpu.VMEM((2 * heads, LAT), jnp.float32)],
        ),
        out_shape=[
            jax.ShapeDtypeStruct((samples, heads, LAT), jnp.bfloat16),
            jax.ShapeDtypeStruct((samples, heads, LAT), jnp.bfloat16),
            jax.ShapeDtypeStruct((heads, LAT), jnp.bfloat16),
        ],
        compiler_params=pltpu.CompilerParams(vmem_limit_bytes=24 * 1024 * 1024),
        cost_estimate=pl.CostEstimate(
            flops=12_000_000_000, bytes_accessed=8_000_000, transcendentals=1_000_000
        ),
        name="attention",
    )(lens, pages, moved, q_one, q_two, q_in, kv_one, kv_two, kv_in, pool)


def choose_kernel(which, first, second, out):
    @pl.when(which[0] == 0)
    def _():
        out[...] = first[...]

    @pl.when(which[0] != 0)
    def _():
        out[...] = second[...]


def choose(which, first, second, flops):
    steps = 4
    block = pl.BlockSpec((first.shape[0] // steps, first.shape[1]), lambda k, *_: (k, 0))
    return pl.pallas_call(
        choose_kernel,
        grid_spec=pltpu.PrefetchScalarGridSpec(
            num_scalar_prefetch=1, grid=(steps,), in_specs=[block, block], out_specs=block
        ),
        out_shape=jax.ShapeDtypeStruct(first.shape, first.dtype),
        cost_estimate=pl.CostEstimate(
            flops=flops, bytes_accessed=3 * first.size * 2, transcendentals=0
        ),
        name="choose",
    )(which, first, second)


def up_kernel(_, rows, *refs):
    weights, (whole, sent) = refs[:-2], refs[-2:]
    for i, weight in enumerate(weights):
        part = jnp.dot(rows[...], weight[...], preferred_element_type=jnp.float32)
        whole[i] = part
        sent[i] = part.astype(jnp.bfloat16)


def up_project(which, rows, weights, steps):
    count, depth = rows.shape
    units = weights[0].shape[1]
    shape = (len(weights), count, units)
    out = pl.BlockSpec((len(weights), count // steps, units), lambda k, *_: (0, k, 0))
    halves = pl.BlockSpec((depth, units), lambda k, half: (half[0], 0))
    whole = pl.BlockSpec((depth, units), lambda k, *_: (0, 0))
    return pl.pallas_call(
        up_kernel,
        grid_spec=pltpu.PrefetchScalarGridSpec(
            num_scalar_prefetch=1,
            grid=(steps,),
            in_specs=[pl.BlockSpec((count // steps, depth), lambda k, *_: (k, 0))]
            + [whole if w.shape[0] == depth else halves for w in weights],
            out_specs=[out, out],
        ),
        out_shape=[
            jax.ShapeDtypeStruct(shape, jnp.float32),
            jax.ShapeDtypeStruct(shape, jnp.bfloat16),
        ],
        compiler_params=pltpu.CompilerParams(vmem_limit_bytes=24 * 1024 * 1024),
        cost_estimate=pl.CostEstimate(
            flops=2 * len(weights) * count * depth * units,
            bytes_accessed=5_000_000,
            transcendentals=0,
        ),
        name="up_project",
    )(which, rows, *weights)


def down_kernel(scalars, mine_a, mine_b, theirs_a, theirs_b, *refs):
    weights, out, held = refs[:4], refs[4], refs[5]

    @pl.when(pl.program_id(0) == 0)
    def _():
        mine = [mine_a.at[0], mine_a.at[1], mine_b.at[0], mine_b.at[1]]
        theirs = [theirs_a.at[0], theirs_a.at[1], theirs_b.at[0], theirs_b.at[1]]

        def fill(turn):
            for i in range(4):
                value = mine[i][...] + theirs[(i + turn) % 4][...].astype(jnp.float32)
                held[i] = (value / (1.0 + jnp.exp(-value))).astype(jnp.bfloat16)

        pl.when(scalars[1] == 1)(lambda: fill(1))
        pl.when(scalars[1] != 1)(lambda: fill(3))

    total = None
    for i, weight in enumerate(weights):
        part = lax.dot_general(
            held[i], weight[...], (((1,), (1,)), ((), ())), preferred_element_type=jnp.float32
        )
        total = part if total is None else total + part
    out[...] = total.astype(jnp.bfloat16)


def down_project(scalars, mine, theirs, weights, steps):
    count, units = mine[0].shape[1:]
    depth = weights[1].shape[0]
    whole = pl.BlockSpec(mine[0].shape, lambda k, *_: (0, 0, 0))
    tile = (depth // steps, units)
    return pl.pallas_call(
        down_kernel,
        grid_spec=pltpu.PrefetchScalarGridSpec(
            num_scalar_prefetch=1,
            grid=(steps,),
            in_specs=[whole] * 4
            + [pl.BlockSpec(tile, lambda k, at: (at[0] * steps + k, 0))]
            + [pl.BlockSpec(tile, lambda k, *_: (k, 0))] * 3,
            out_specs=pl.BlockSpec((count, depth // steps), lambda k, *_: (0, k)),
            scratch_shapes=[pltpu.VMEM((4, count, units), jnp.bfloat16)],
        ),
        out_shape=jax.ShapeDtypeStruct((count, depth), jnp.bfloat16),
        compiler_params=pltpu.CompilerParams(vmem_limit_bytes=24 * 1024 * 1024),
        cost_estimate=pl.CostEstimate(
            flops=8 * count * depth * units,
            bytes_accessed=9_000_000,
            transcendentals=4 * count * units,
        ),
        name="down_project",
    )(scalars, *mine, *theirs, *weights)


def page_table(cache_len, page_perm, page_rows, pool_pages):
    used = (cache_len + page_rows - 1) // page_rows
    slots = used.shape[0]
    before = jnp.arange(slots)[None, :] < jnp.arange(slots)[:, None]
    offset = jnp.sum(jnp.where(before, used[None, :], 0), axis=1)
    place = jnp.minimum(
        offset[:, None] + jnp.arange(MAXP, dtype=jnp.int32)[None, :], pool_pages - 1
    ).reshape(-1)
    hit = place[:, None] == jnp.arange(pool_pages, dtype=jnp.int32)[None, :]
    return jnp.sum(jnp.where(hit, page_perm[None, :], 0), axis=1)


def shards(
    hidden,
    expert_ids,
    gate_weights,
    w_up,
    w_down,
    query_first,
    kv_first,
    query_second,
    kv_second,
    cache_pool,
    cache_len,
    page_perm,
    mig_slot,
    mig_dest,
):
    samples, picks = expert_ids.shape
    width = hidden.shape[1]
    ep_size = lax.axis_size("ep")
    grp_size = lax.axis_size("grp")
    capacity = min(samples, max(2, 2 * samples * picks // ep_size))
    me = lax.axis_index("grp")
    steps = range(grp_size)

    half = width // 2
    core = lax.axis_index("ep") % 2
    turned = [(me - c) % grp_size for c in range(2)]
    side = [turned[c] // 2 for c in range(2)]
    here = jnp.where(core == 0, turned[0], turned[1])
    partner = [[((a + c) % grp_size, (b + c) % grp_size) for a, b in PAIRS] for c in range(2)]

    def by_core(pairs):
        return [
            (e * grp_size + (a + e % 2) % grp_size, e * grp_size + (b + e % 2) % grp_size)
            for e in range(ep_size)
            for a, b in pairs
        ]

    def part(value, which, axis):
        return lax.dynamic_slice_in_dim(value, which * half, half, axis)

    rows, id_list, gate_list = [], [expert_ids], []
    term = lax.reduce_precision(gate_weights, 8, 7)
    rest = gate_weights - term
    next_term = lax.reduce_precision(rest, 8, 7)
    small = jnp.concatenate(
        [expert_ids.astype(jnp.float32), term, next_term, rest - next_term], axis=1
    ).astype(jnp.bfloat16)
    small = jnp.pad(small, ((0, 0), (0, 128 - 4 * picks)))
    for c in range(2):
        sent = jnp.concatenate([part(hidden, 1 - side[c], 1), small], axis=1)
        theirs = lax.ppermute(sent, "grp", partner[c])
        extra = theirs[:, half : half + 4 * picks].astype(jnp.float32).reshape(samples, 4, picks)
        id_list.append(extra[:, 0].astype(jnp.int32))
        gate_list += [gate_weights, (extra[:, 1] + extra[:, 2]) + extra[:, 3]]
        rows += [part(hidden, side[c], 1), theirs[:, :half]]
    rows = jnp.concatenate(rows, axis=0)

    lead = jnp.where((here == 0) | (here == 3), 0, 1)

    def spread(weight, ahead, *first):
        to_next, to_prev = after(first, part(weight, ahead, 0), part(weight, 1 - ahead, 0))
        return hop(to_next, "grp", 1), hop(to_prev, "grp", -1)

    def pass_on(prev, nxt, flops):
        picked = choose((here % 2)[None], prev, nxt, flops)
        far = lax.ppermute(picked, ("ep", "grp"), by_core([(0, 1), (1, 0), (2, 3), (3, 2)]))
        return far

    up_prev, up_next = spread(w_up[0], lead, rows)
    up_far = pass_on(up_prev, up_next, 200_000_000_000)

    rank = 2 * capacity
    lanes_all = ep_size * rank
    flat_ids = jnp.concatenate(id_list, axis=0).reshape(-1)
    entries = flat_ids.shape[0]
    hits = flat_ids[:, None] == jnp.arange(ep_size, dtype=jnp.int32)[None, :]
    order = jnp.arange(entries, dtype=jnp.int32)
    per = samples * picks
    lower = (order[None, :] < order[:, None]) & (order[None, :] // per == order[:, None] // per)
    ahead = jnp.dot(
        lower.astype(jnp.bfloat16), hits.astype(jnp.bfloat16), preferred_element_type=jnp.float32
    )
    earlier = jnp.sum(jnp.where(hits, ahead, 0.0), axis=1).astype(jnp.int32)
    place = (flat_ids * rank + earlier).reshape(3, samples, picks)
    own_at, first_at, second_at = place[0], place[1], place[2]
    even = (expert_ids % 2) == 0
    place = jnp.concatenate(
        [
            jnp.where(even, own_at + side[0] * capacity, -1),
            jnp.where((id_list[1] % 2) == 0, first_at + (1 - side[0]) * capacity, -1),
            jnp.where(even, -1, own_at + side[1] * capacity),
            jnp.where((id_list[2] % 2) == 0, -1, second_at + (1 - side[1]) * capacity),
        ],
        axis=0,
    )
    match = place[:, :, None] == jnp.arange(lanes_all, dtype=jnp.int32)[None, None, :]
    placing = jnp.sum(match.astype(jnp.float32), axis=1).astype(jnp.bfloat16)
    outgoing = lax.dot_general(
        placing, rows, (((0,), (0,)), ((), ())), preferred_element_type=jnp.float32
    ).astype(jnp.bfloat16)
    late = jnp.minimum(placing[0, 0].astype(jnp.float32), 0.0).astype(jnp.int32)
    down_prev, down_next = spread(w_down[0], lead + late, up_prev, up_next)
    down_far = pass_on(down_prev, down_next, 0)
    arrived = lax.all_to_all(
        outgoing.reshape(ep_size, rank, half), "ep", split_axis=0, concat_axis=0, tiled=True
    ).reshape(lanes_all, half)

    moved_slot = mig_slot[0, 0]
    moved_target = mig_dest[0, 0]
    query_second, kv_second = after(outgoing, query_second, kv_second)
    q_here = lax.dynamic_index_in_dim(query_second, moved_slot, 0, keepdims=False)
    kv_here = lax.dynamic_index_in_dim(kv_second, moved_slot, 0, keepdims=True)
    packet = jnp.concatenate(
        [q_here, kv_here, jnp.zeros((15, q_here.shape[1]), jnp.bfloat16)], axis=0
    )
    offset = (moved_target - me) % grp_size
    got = packet
    for r in steps[1:]:
        got = jnp.where(offset == r, hop(packet, "grp", -r), got)
    heads = q_here.shape[0]
    q_in, kv_in = got[:heads], got[heads : heads + 1]

    lens = cache_len[0]
    pages = page_table(lens, page_perm[0], cache_pool.shape[1], cache_pool.shape[0])
    attn_first, attn_second, out_moved = attention(
        lens,
        pages,
        moved_slot[None],
        query_first,
        query_second,
        q_in,
        kv_first[:, None, :],
        kv_second[:, None, :],
        kv_in,
        cache_pool,
    )
    zero = jnp.zeros((), jnp.bfloat16)
    arrived_out = jnp.where(offset == 0, out_moved, zero)
    for r in steps[1:]:
        arrived_out = arrived_out + hop(jnp.where(offset == r, out_moved, zero), "grp", r)
    attn_second = lax.dynamic_update_index_in_dim(attn_second, arrived_out, moved_slot, 0)

    scalars = jnp.stack([here // 2, 1 - here % 2]).astype(jnp.int32)
    mine_a, sent_a = up_project(scalars, arrived, [w_up[0], up_next], 2)
    theirs_a = lax.ppermute(sent_a, ("ep", "grp"), by_core(PAIRS))
    mine_b, sent_b = up_project(scalars, arrived, [up_far, up_prev], 2)
    (sent_b,) = after(down_far, sent_b)
    theirs_b = lax.ppermute(sent_b, ("ep", "grp"), by_core(PAIRS))
    produced = down_project(
        scalars,
        [mine_a, mine_b],
        [theirs_a, theirs_b],
        [w_down[0], down_next, down_far, down_prev],
        2,
    )
    returned = lax.all_to_all(
        produced.reshape(ep_size, rank, half),
        "ep",
        split_axis=0,
        concat_axis=0,
        tiled=True,
    ).reshape(lanes_all, half)
    gates = jnp.concatenate(gate_list, axis=0)
    mixing = jnp.sum(jnp.where(match, gates[:, :, None], 0.0), axis=1)
    high = lax.reduce_precision(mixing, 8, 7)
    mixing = jnp.concatenate([high, mixing - high], axis=0).astype(jnp.bfloat16)
    mixed = jnp.dot(mixing, returned, preferred_element_type=jnp.float32)
    summed = (mixed[: 4 * samples] + mixed[4 * samples :]).reshape(4, samples, half)
    first, second = 0.0, 0.0
    for c in range(2):
        own = summed[2 * c]
        other = lax.ppermute(summed[2 * c + 1], "grp", partner[c])
        first = first + jnp.where(side[c] == 0, own, other)
        second = second + jnp.where(side[c] == 0, other, own)
    moe_out = jnp.concatenate([first, second], axis=1).astype(jnp.bfloat16)
    return (attn_first, attn_second, moe_out)


def solution(mesh):
    return jax.shard_map(
        shards,
        mesh=mesh,
        in_specs=(
            P(("ep", "grp"), None),
            P(("ep", "grp"), None),
            P(("ep", "grp"), None),
            P("ep", None, "grp"),
            P("ep", None, "grp"),
            P(("ep", "grp"), None, None),
            P(("ep", "grp"), None),
            P(("ep", "grp"), None, None),
            P(("ep", "grp"), None),
            P(("ep", "grp"), None, None),
            P(("ep", "grp"), None),
            P(("ep", "grp"), None),
            P("ep", "grp"),
            P("ep", "grp"),
        ),
        out_specs=(
            P(("ep", "grp"), None, None),
            P(("ep", "grp"), None, None),
            P(("ep", "grp"), None),
        ),
        check_vma=False,
    )
```

```python
import math

import jax
import jax.numpy as jnp
from jax import lax
from jax.experimental import pallas as pl
from jax.experimental.pallas import tpu as pltpu
from jax.sharding import PartitionSpec as P

LAT = 512
MAXP = 8
NEG = -1e30
PAIRS = ((1, 2), (2, 1), (3, 0), (0, 3))


def hop(value, axis, step):
    size = lax.axis_size(axis)
    return lax.ppermute(value, axis, [(i, (i + step) % size) for i in range(size)])


def after(first, *values):
    return lax.optimization_barrier((first,) + values)[1:]


def attention_kernel(
    lens, pages, moved, q_one, q_two, q_in, kv_one, kv_two, kv_in, pool, out_one, out_two, out_moved, acc
):
    slot = pl.program_id(0)
    heads = q_one.shape[1]
    rows = 2 * heads
    key_width = q_one.shape[2]
    page_rows = pool.shape[1]
    block = 2 * page_rows
    scale = 1.0 / math.sqrt(key_width / 3.0)
    is_moved = slot == moved[0]
    second = jnp.where(is_moved, q_in[...], q_two[0])
    queries = jnp.concatenate([q_one[0], second], axis=0)
    fresh_one = kv_one[0]
    fresh_two = jnp.where(is_moved, kv_in[...], kv_two[0])
    fresh = jnp.concatenate(
        [fresh_one, fresh_two, jnp.zeros((14, key_width), jnp.bfloat16)], axis=0
    )
    contract = (((1,), (1,)), ((), ()))
    scores = lax.dot_general(queries, fresh, contract, preferred_element_type=jnp.float32) * scale
    row = lax.broadcasted_iota(jnp.int32, scores.shape, 0)
    col = lax.broadcasted_iota(jnp.int32, scores.shape, 1)
    scores = jnp.where((col == 0) | ((col == 1) & (row >= heads)), scores, NEG)
    top = jnp.max(scores, axis=1, keepdims=True)
    weights = jnp.exp(scores - top)
    total = jnp.sum(weights, axis=1, keepdims=True)
    acc[...] = jnp.dot(
        weights.astype(jnp.bfloat16), fresh[:, :LAT], preferred_element_type=jnp.float32
    )
    live = lens[slot]

    def step(b, carry):
        top, total = carry
        keys = jnp.concatenate(
            [pool[pages[slot * MAXP + 2 * b]], pool[pages[slot * MAXP + 2 * b + 1]]], axis=0
        )
        scores = (
            lax.dot_general(queries, keys, contract, preferred_element_type=jnp.float32) * scale
        )
        col = lax.broadcasted_iota(jnp.int32, scores.shape, 1) + b * block
        scores = jnp.where(col < live, scores, NEG)
        new_top = jnp.maximum(top, jnp.max(scores, axis=1, keepdims=True))
        shrink = jnp.exp(top - new_top)
        weights = jnp.exp(scores - new_top)
        total = total * shrink + jnp.sum(weights, axis=1, keepdims=True)
        acc[...] = acc[...] * shrink + jnp.dot(
            weights.astype(jnp.bfloat16), keys[:, :LAT], preferred_element_type=jnp.float32
        )
        return new_top, total

    top, total = lax.fori_loop(0, (live + block - 1) // block, step, (top, total))
    result = (acc[...] / total).astype(jnp.bfloat16)
    out_one[0] = result[:heads]
    out_two[0] = result[heads:]

    @pl.when(is_moved)
    def _():
        out_moved[...] = result[heads:]


def attention(lens, pages, moved, q_one, q_two, q_in, kv_one, kv_two, kv_in, pool):
    samples, heads, key_width = q_one.shape
    one = lambda *shape: pl.BlockSpec((1,) + shape, lambda i, *_: (i,) + (0,) * len(shape))
    whole = lambda *shape: pl.BlockSpec(shape, lambda i, *_: (0,) * len(shape))
    return pl.pallas_call(
        attention_kernel,
        grid_spec=pltpu.PrefetchScalarGridSpec(
            num_scalar_prefetch=3,
            grid=(samples,),
            in_specs=[
                one(heads, key_width),
                one(heads, key_width),
                whole(heads, key_width),
                one(1, key_width),
                one(1, key_width),
                whole(1, key_width),
                whole(*pool.shape),
            ],
            out_specs=[one(heads, LAT), one(heads, LAT), whole(heads, LAT)],
            scratch_shapes=[pltpu.VMEM((2 * heads, LAT), jnp.float32)],
        ),
        out_shape=[
            jax.ShapeDtypeStruct((samples, heads, LAT), jnp.bfloat16),
            jax.ShapeDtypeStruct((samples, heads, LAT), jnp.bfloat16),
            jax.ShapeDtypeStruct((heads, LAT), jnp.bfloat16),
        ],
        compiler_params=pltpu.CompilerParams(vmem_limit_bytes=24 * 1024 * 1024),
        cost_estimate=pl.CostEstimate(
            flops=12_000_000_000, bytes_accessed=8_000_000, transcendentals=1_000_000
        ),
        name="attention",
    )(lens, pages, moved, q_one, q_two, q_in, kv_one, kv_two, kv_in, pool)


def choose_kernel(which, first, second, out):
    @pl.when(which[0] == 0)
    def _():
        out[...] = first[...]

    @pl.when(which[0] != 0)
    def _():
        out[...] = second[...]


def choose(which, first, second, flops):
    steps = 4
    block = pl.BlockSpec((first.shape[0] // steps, first.shape[1]), lambda k, *_: (k, 0))
    return pl.pallas_call(
        choose_kernel,
        grid_spec=pltpu.PrefetchScalarGridSpec(
            num_scalar_prefetch=1, grid=(steps,), in_specs=[block, block], out_specs=block
        ),
        out_shape=jax.ShapeDtypeStruct(first.shape, first.dtype),
        cost_estimate=pl.CostEstimate(
            flops=flops, bytes_accessed=3 * first.size * 2, transcendentals=0
        ),
        name="choose",
    )(which, first, second)


def up_kernel(_, rows, *refs):
    weights, (whole, sent) = refs[:-2], refs[-2:]
    for i, weight in enumerate(weights):
        part = jnp.dot(rows[...], weight[...], preferred_element_type=jnp.float32)
        whole[i] = part
        sent[i] = part.astype(jnp.bfloat16)


def up_project(which, rows, weights, steps, room):
    count, depth = rows.shape
    units = weights[0].shape[1]
    shape = (len(weights), count, units)
    out = pl.BlockSpec((len(weights), count // steps, units), lambda k, *_: (0, k, 0))
    halves = pl.BlockSpec((depth, units), lambda k, half: (half[0], 0))
    whole = pl.BlockSpec((depth, units), lambda k, *_: (0, 0))
    return pl.pallas_call(
        up_kernel,
        grid_spec=pltpu.PrefetchScalarGridSpec(
            num_scalar_prefetch=1,
            grid=(steps,),
            in_specs=[pl.BlockSpec((count // steps, depth), lambda k, *_: (k, 0))]
            + [whole if w.shape[0] == depth else halves for w in weights],
            out_specs=[out, out],
        ),
        out_shape=[
            jax.ShapeDtypeStruct(shape, jnp.float32),
            jax.ShapeDtypeStruct(shape, jnp.bfloat16),
        ],
        compiler_params=pltpu.CompilerParams(vmem_limit_bytes=room * 1024 * 1024),
        cost_estimate=pl.CostEstimate(
            flops=2 * len(weights) * count * depth * units,
            bytes_accessed=5_000_000,
            transcendentals=0,
        ),
        name="up_project",
    )(which, rows, *weights)


def down_kernel(scalars, mine_a, mine_b, theirs_a, theirs_b, *refs):
    weights, out, held = refs[:4], refs[4], refs[5]

    @pl.when(pl.program_id(0) == 0)
    def _():
        mine = [mine_a.at[0], mine_a.at[1], mine_b.at[0], mine_b.at[1]]
        theirs = [theirs_a.at[0], theirs_a.at[1], theirs_b.at[0], theirs_b.at[1]]

        def fill(turn):
            for i in range(4):
                value = mine[i][...] + theirs[(i + turn) % 4][...].astype(jnp.float32)
                held[i] = (value / (1.0 + jnp.exp(-value))).astype(jnp.bfloat16)

        pl.when(scalars[1] == 1)(lambda: fill(1))
        pl.when(scalars[1] != 1)(lambda: fill(3))

    total = None
    for i, weight in enumerate(weights):
        part = lax.dot_general(
            held[i], weight[...], (((1,), (1,)), ((), ())), preferred_element_type=jnp.float32
        )
        total = part if total is None else total + part
    out[...] = total.astype(jnp.bfloat16)


def down_project(scalars, mine, theirs, weights, steps):
    count, units = mine[0].shape[1:]
    depth = weights[1].shape[0]
    whole = pl.BlockSpec(mine[0].shape, lambda k, *_: (0, 0, 0))
    tile = (depth // steps, units)
    return pl.pallas_call(
        down_kernel,
        grid_spec=pltpu.PrefetchScalarGridSpec(
            num_scalar_prefetch=1,
            grid=(steps,),
            in_specs=[whole] * 4
            + [pl.BlockSpec(tile, lambda k, at: (at[0] * steps + k, 0))]
            + [pl.BlockSpec(tile, lambda k, *_: (k, 0))] * 3,
            out_specs=pl.BlockSpec((count, depth // steps), lambda k, *_: (0, k)),
            scratch_shapes=[pltpu.VMEM((4, count, units), jnp.bfloat16)],
        ),
        out_shape=jax.ShapeDtypeStruct((count, depth), jnp.bfloat16),
        compiler_params=pltpu.CompilerParams(vmem_limit_bytes=24 * 1024 * 1024),
        cost_estimate=pl.CostEstimate(
            flops=8 * count * depth * units,
            bytes_accessed=9_000_000,
            transcendentals=4 * count * units,
        ),
        name="down_project",
    )(scalars, *mine, *theirs, *weights)


def page_table(cache_len, page_perm, page_rows, pool_pages):
    used = (cache_len + page_rows - 1) // page_rows
    slots = used.shape[0]
    before = jnp.arange(slots)[None, :] < jnp.arange(slots)[:, None]
    offset = jnp.sum(jnp.where(before, used[None, :], 0), axis=1)
    place = jnp.minimum(
        offset[:, None] + jnp.arange(MAXP, dtype=jnp.int32)[None, :], pool_pages - 1
    ).reshape(-1)
    hit = place[:, None] == jnp.arange(pool_pages, dtype=jnp.int32)[None, :]
    return jnp.sum(jnp.where(hit, page_perm[None, :], 0), axis=1)


def shards(
    hidden,
    expert_ids,
    gate_weights,
    w_up,
    w_down,
    query_first,
    kv_first,
    query_second,
    kv_second,
    cache_pool,
    cache_len,
    page_perm,
    mig_slot,
    mig_dest,
):
    samples, picks = expert_ids.shape
    width = hidden.shape[1]
    ep_size = lax.axis_size("ep")
    grp_size = lax.axis_size("grp")
    capacity = min(samples, max(2, 2 * samples * picks // ep_size))
    me = lax.axis_index("grp")
    steps = range(grp_size)

    half = width // 2
    core = lax.axis_index("ep") % 2
    turned = [(me - c) % grp_size for c in range(2)]
    side = [turned[c] // 2 for c in range(2)]
    here = jnp.where(core == 0, turned[0], turned[1])
    partner = [[((a + c) % grp_size, (b + c) % grp_size) for a, b in PAIRS] for c in range(2)]

    def by_core(pairs):
        return [
            (e * grp_size + (a + e % 2) % grp_size, e * grp_size + (b + e % 2) % grp_size)
            for e in range(ep_size)
            for a, b in pairs
        ]

    def part(value, which, axis):
        return lax.dynamic_slice_in_dim(value, which * half, half, axis)

    rows, id_list, gate_list = [], [expert_ids], []
    term = lax.reduce_precision(gate_weights, 8, 7)
    rest = gate_weights - term
    next_term = lax.reduce_precision(rest, 8, 7)
    small = jnp.concatenate(
        [expert_ids.astype(jnp.float32), term, next_term, rest - next_term], axis=1
    ).astype(jnp.bfloat16)
    small = jnp.pad(small, ((0, 0), (0, 128 - 4 * picks)))
    for c in range(2):
        sent = jnp.concatenate([part(hidden, 1 - side[c], 1), small], axis=1)
        theirs = lax.ppermute(sent, "grp", partner[c])
        extra = theirs[:, half : half + 4 * picks].astype(jnp.float32).reshape(samples, 4, picks)
        id_list.append(extra[:, 0].astype(jnp.int32))
        gate_list += [gate_weights, (extra[:, 1] + extra[:, 2]) + extra[:, 3]]
        rows += [part(hidden, side[c], 1), theirs[:, :half]]
    rows = jnp.concatenate(rows, axis=0)

    lead = jnp.where((here == 0) | (here == 3), 0, 1)

    def spread(weight, ahead, *first):
        to_next, to_prev = after(first, part(weight, ahead, 0), part(weight, 1 - ahead, 0))
        return hop(to_next, "grp", 1), hop(to_prev, "grp", -1)

    def pass_on(prev, nxt, flops):
        picked = choose((here % 2)[None], prev, nxt, flops)
        far = lax.ppermute(picked, ("ep", "grp"), by_core([(0, 1), (1, 0), (2, 3), (3, 2)]))
        return far

    up_prev, up_next = spread(w_up[0], lead, rows)
    up_far = pass_on(up_prev, up_next, 200_000_000_000)

    rank = 2 * capacity
    lanes_all = ep_size * rank
    flat_ids = jnp.concatenate(id_list, axis=0).reshape(-1)
    entries = flat_ids.shape[0]
    hits = flat_ids[:, None] == jnp.arange(ep_size, dtype=jnp.int32)[None, :]
    order = jnp.arange(entries, dtype=jnp.int32)
    per = samples * picks
    lower = (order[None, :] < order[:, None]) & (order[None, :] // per == order[:, None] // per)
    ahead = jnp.dot(
        lower.astype(jnp.bfloat16), hits.astype(jnp.bfloat16), preferred_element_type=jnp.float32
    )
    earlier = jnp.sum(jnp.where(hits, ahead, 0.0), axis=1).astype(jnp.int32)
    place = (flat_ids * rank + earlier).reshape(3, samples, picks)
    own_at, first_at, second_at = place[0], place[1], place[2]
    even = (expert_ids % 2) == 0
    place = jnp.concatenate(
        [
            jnp.where(even, own_at + side[0] * capacity, -1),
            jnp.where((id_list[1] % 2) == 0, first_at + (1 - side[0]) * capacity, -1),
            jnp.where(even, -1, own_at + side[1] * capacity),
            jnp.where((id_list[2] % 2) == 0, -1, second_at + (1 - side[1]) * capacity),
        ],
        axis=0,
    )
    match = place[:, :, None] == jnp.arange(lanes_all, dtype=jnp.int32)[None, None, :]
    placing = jnp.sum(match.astype(jnp.float32), axis=1).astype(jnp.bfloat16)
    outgoing = lax.dot_general(
        placing, rows, (((0,), (0,)), ((), ())), preferred_element_type=jnp.float32
    ).astype(jnp.bfloat16)
    late = jnp.minimum(placing[0, 0].astype(jnp.float32), 0.0).astype(jnp.int32)
    down_prev, down_next = spread(w_down[0], lead + late, up_prev, up_next)
    down_far = pass_on(down_prev, down_next, 0)
    arrived = lax.all_to_all(
        outgoing.reshape(ep_size, rank, half), "ep", split_axis=0, concat_axis=0, tiled=True
    ).reshape(lanes_all, half)

    moved_slot = mig_slot[0, 0]
    moved_target = mig_dest[0, 0]
    query_second, kv_second = after(outgoing, query_second, kv_second)
    q_here = lax.dynamic_index_in_dim(query_second, moved_slot, 0, keepdims=False)
    kv_here = lax.dynamic_index_in_dim(kv_second, moved_slot, 0, keepdims=True)
    packet = jnp.concatenate(
        [q_here, kv_here, jnp.zeros((15, q_here.shape[1]), jnp.bfloat16)], axis=0
    )
    offset = (moved_target - me) % grp_size
    got = packet
    for r in steps[1:]:
        got = jnp.where(offset == r, hop(packet, "grp", -r), got)
    heads = q_here.shape[0]
    q_in, kv_in = got[:heads], got[heads : heads + 1]

    lens = cache_len[0]
    pages = page_table(lens, page_perm[0], cache_pool.shape[1], cache_pool.shape[0])
    attn_first, attn_second, out_moved = attention(
        lens,
        pages,
        moved_slot[None],
        query_first,
        query_second,
        q_in,
        kv_first[:, None, :],
        kv_second[:, None, :],
        kv_in,
        cache_pool,
    )
    zero = jnp.zeros((), jnp.bfloat16)
    arrived_out = jnp.where(offset == 0, out_moved, zero)
    for r in steps[1:]:
        arrived_out = arrived_out + hop(jnp.where(offset == r, out_moved, zero), "grp", r)
    attn_second = lax.dynamic_update_index_in_dim(attn_second, arrived_out, moved_slot, 0)

    scalars = jnp.stack([here // 2, 1 - here % 2]).astype(jnp.int32)
    mine_a, sent_a = up_project(scalars, arrived, [w_up[0], up_next], 2, 58)
    theirs_a = lax.ppermute(sent_a, ("ep", "grp"), by_core(PAIRS))
    mine_b, sent_b = up_project(scalars, arrived, [up_far, up_prev], 2, 24)
    (sent_b,) = after(down_far, sent_b)
    theirs_b = lax.ppermute(sent_b, ("ep", "grp"), by_core(PAIRS))
    produced = down_project(
        scalars,
        [mine_a, mine_b],
        [theirs_a, theirs_b],
        [w_down[0], down_next, down_far, down_prev],
        2,
    )
    returned = lax.all_to_all(
        produced.reshape(ep_size, rank, half),
        "ep",
        split_axis=0,
        concat_axis=0,
        tiled=True,
    ).reshape(lanes_all, half)
    gates = jnp.concatenate(gate_list, axis=0)
    mixing = jnp.sum(jnp.where(match, gates[:, :, None], 0.0), axis=1)
    high = lax.reduce_precision(mixing, 8, 7)
    mixing = jnp.concatenate([high, mixing - high], axis=0).astype(jnp.bfloat16)
    mixed = jnp.dot(mixing, returned, preferred_element_type=jnp.float32)
    summed = (mixed[: 4 * samples] + mixed[4 * samples :]).reshape(4, samples, half)
    first, second = 0.0, 0.0
    for c in range(2):
        own = summed[2 * c]
        other = lax.ppermute(summed[2 * c + 1], "grp", partner[c])
        first = first + jnp.where(side[c] == 0, own, other)
        second = second + jnp.where(side[c] == 0, other, own)
    moe_out = jnp.concatenate([first, second], axis=1).astype(jnp.bfloat16)
    return (attn_first, attn_second, moe_out)


def solution(mesh):
    return jax.shard_map(
        shards,
        mesh=mesh,
        in_specs=(
            P(("ep", "grp"), None),
            P(("ep", "grp"), None),
            P(("ep", "grp"), None),
            P("ep", None, "grp"),
            P("ep", None, "grp"),
            P(("ep", "grp"), None, None),
            P(("ep", "grp"), None),
            P(("ep", "grp"), None, None),
            P(("ep", "grp"), None),
            P(("ep", "grp"), None, None),
            P(("ep", "grp"), None),
            P(("ep", "grp"), None),
            P("ep", "grp"),
            P("ep", "grp"),
        ),
        out_specs=(
            P(("ep", "grp"), None, None),
            P(("ep", "grp"), None, None),
            P(("ep", "grp"), None),
        ),
        check_vma=False,
    )
```
